32 devices in a mesh: node: 4 (over x, core), local: 8 (over z, y).
Axes of the slice: x: 2, y: 2, z: 4, core: 2. Of those that a mesh axis runs over, the one named last changes fastest.
Arguments:
- partials: bfloat16 [4, 8, 1048576], P('node', 'local'), may hold values from -8 to 8
- signs: int32 [1048576], replicated, may hold values 0 or 1
Outputs:
- reduced: float32 [1048576], P(('node', 'local'))
- rotated_max: float32 [8192], P(('node', 'local'))
The draws below stay inside these ranges and needn't reach their ends.
Inputs may be any that keep to these rules, and one draw needn't show every extreme that they name: `signs`: 0 selects the sign +1 and 1 the sign -1 of a position.
All inputs are finite; a program needn't handle non-finite values.
Results may differ from the reference program's by a relative error of at most 0.0003.
Values may be sent and summed in bfloat16 or wider, within the bound.
No kernel may reach another device: no remote copies, remote signals or barrier semaphores. Data moves between devices by JAX's collectives and lax.ppermute only.
A program may use at most 64 MiB of HBM per device.

```python
import math
import jax
import jax.numpy as jnp
from jax import lax

BUCKET = 1048576
ROT = 256
QGROUP = 128
GROUPS = 4
MEMBERS = 8


def draw_partials(key, part):
    streams = jax.random.split(jax.random.fold_in(key, 7001), 2)
    shape = (GROUPS, MEMBERS, BUCKET)
    noise = jax.random.normal(streams[0], shape, jnp.float32)
    replica_scale = jnp.exp(jax.random.uniform(streams[1], (GROUPS, MEMBERS, 1), jnp.float32, math.log(0.8), math.log(1.2)))
    magnitude = jnp.clip(jnp.abs(noise), 1.0 / 16.0, 4.0)
    direction = jnp.where(noise >= 0.0, 1.0, -1.0)
    values = direction * magnitude * replica_scale / 16.0
    return values.astype(jnp.bfloat16)


def touch_ends(values, rng, least, high):
    place = [jax.random.randint(jax.random.fold_in(rng, axis), (), 0, length) for axis, length in enumerate(values.shape)]
    widest = values.shape.index(max(values.shape))
    next_to = place[:widest] + [(place[widest] + 1) % values.shape[widest]] + place[widest + 1:]
    return values.at[tuple(place)].set(least).at[tuple(next_to)].set(high)


def setup_inputs(seed: int = 0) -> dict:
    key_of = jax.random.split(jax.random.key(seed), 3)
    partials = draw_partials(jax.random.fold_in(key_of[2], 71), 0)
    signs = touch_ends((jax.random.randint(key_of[1], (BUCKET,), 0, 2) < 1).astype(jnp.int32), jax.random.fold_in(key_of[1], 1), 0, 1)
    return {"partials": partials, "signs": signs}


def sylvester():
    positions = jnp.arange(ROT, dtype=jnp.int32)
    parity = jnp.zeros((ROT, ROT), dtype=jnp.int32)
    for level in range(ROT.bit_length() - 1):
        column = positions >> level & 1
        parity = parity + column[:, None] * column[None, :]
    return (1 - 2 * (parity % 2)).astype(jnp.float32)

def power_scale(largest):
    scaling = jnp.full(largest.shape, 2.0 ** (-37), dtype=jnp.float32)
    for power in range(-30, 31):
        scaling = jnp.where(largest >= 2.0 ** power, jnp.float32(2.0 ** (power - 7)), scaling)
    return scaling

def quantize(scaled):
    magnitude = jnp.abs(scaled)
    spacing = jnp.full(scaled.shape, 2.0 ** (-9), dtype=jnp.float32)
    for power in range(-5, 8):
        spacing = jnp.where(magnitude >= 2.0 ** power, jnp.float32(2.0 ** (power - 3)), spacing)
    return jnp.sign(scaled) * jnp.floor(magnitude / spacing + 0.5) * spacing

def encode(values):
    grouped = values.reshape(values.shape[:-1] + (values.shape[-1] // QGROUP, QGROUP))
    largest = lax.optimization_barrier(jnp.max(jnp.abs(grouped), axis=-1))
    scaling = power_scale(largest)
    coded = quantize(grouped / scaling[..., None]).astype(jnp.bfloat16)
    return (coded.reshape(values.shape), scaling.astype(jnp.bfloat16))

def decode(coded, scales):
    grouped = coded.reshape(coded.shape[:-1] + (coded.shape[-1] // QGROUP, QGROUP))
    values = grouped.astype(jnp.float32) * scales.astype(jnp.float32)[..., None]
    return values.reshape(coded.shape)

def reference(partials, signs):
    flips = (1 - 2 * signs).astype(jnp.float32)
    matrix = sylvester()

    def group_sum(replicas):
        signed = replicas.astype(jnp.float32) * flips
        rotated = jnp.dot(signed.reshape(-1, ROT), matrix, precision=lax.Precision.HIGHEST, preferred_element_type=jnp.float32).reshape(signed.shape)
        coded, scales = encode(rotated)
        first = lax.optimization_barrier(jnp.sum(decode(coded, scales), axis=0))
        coded_two, scales_two = encode(first)
        return decode(coded_two, scales_two)
    group_parts = lax.map(group_sum, partials)
    second = lax.optimization_barrier(jnp.sum(group_parts, axis=0))
    rotated_max = lax.optimization_barrier(jnp.max(jnp.abs(second.reshape(-1, QGROUP)), axis=-1)) / jnp.sqrt(jnp.float32(ROT))
    turned_back = jnp.dot(second.reshape(-1, ROT), matrix, precision=lax.Precision.HIGHEST, preferred_element_type=jnp.float32).reshape(second.shape)
    reduced = turned_back / ROT * flips
    return (reduced, rotated_max)
```

```python
import functools
import jax
import jax.numpy as jnp
from jax import lax
from jax.experimental import pallas as pl
from jax.experimental.pallas import tpu as pltpu
from jax.sharding import PartitionSpec as P

ROT = 256
QGROUP = 128
HALVES = ROT // QGROUP
LANES = 128
VMEM_LIMIT = 40 * 1024 * 1024


def sylvester():
    positions = jnp.arange(ROT, dtype=jnp.int32)
    parity = jnp.zeros((ROT, ROT), dtype=jnp.int32)
    for level in range(ROT.bit_length() - 1):
        column = positions >> level & 1
        parity = parity + column[:, None] * column[None, :]
    return (1 - 2 * (parity % 2)).astype(jnp.float32)


def leading_power(x):
    q = x * jnp.float32(2.0**23 + 1.0)
    return q - q * jnp.float32(1.0 - 2.0**-24)


def recode(values):
    columns = values.shape[1]
    magnitude = jnp.abs(values)
    grouped = magnitude.reshape(values.shape[0] // QGROUP, QGROUP, columns)
    largest = jnp.max(grouped, axis=1, keepdims=True)
    top = leading_power(jnp.clip(largest, 2.0**-30, 2.0**30))
    scale = top * jnp.float32(2.0**-7)
    least = scale * jnp.float32(2.0**-6)
    power = jnp.maximum(leading_power(grouped), least)
    shift = power * jnp.float32(2.0**20)
    nudged = grouped + power * jnp.float32(2.0**-4)
    nearest = (nudged + shift) - shift
    spacing = power * jnp.float32(2.0**-3)
    floored = jnp.where(nearest > nudged, nearest - spacing, nearest).reshape(values.shape)
    return jnp.where(values < 0.0, -floored, floored)


def rotate_kernel(sections, matrix_ref, *refs):
    value_refs = refs[:sections]
    sign_refs = refs[sections : 2 * sections]
    out_ref, turned = refs[2 * sections :]
    rows = sign_refs[0].shape[0]
    blocks = rows // HALVES
    for section in range(sections):
        values = value_refs[section][...].astype(jnp.float32).reshape(rows, LANES)
        turned[...] = jnp.where(sign_refs[section][...] == 0, values, -values)
        halves = [turned[pl.ds(half, blocks, stride=HALVES), :] for half in range(HALVES)]
        signed = jnp.concatenate(halves, axis=1).astype(jnp.bfloat16)
        rotated = lax.dot_general(
            matrix_ref[...], signed, (((1,), (1,)), ((), ())), preferred_element_type=jnp.float32
        )
        out_ref[0, :, section * blocks : (section + 1) * blocks] = recode(rotated).astype(jnp.bfloat16)


def rotate(values, signs, matrix, members, groups, first_section, sections):
    length = values.shape[1]
    portion = length // (members * groups)
    blocks = portion // ROT
    rows = portion // LANES

    def place(section, member):
        return (first_section + section) * members + member

    value_specs = [
        pl.BlockSpec((1, portion), functools.partial(lambda s, l: (0, place(s, l)), s)) for s in range(sections)
    ]
    sign_specs = [
        pl.BlockSpec((rows, LANES), functools.partial(lambda s, l: (place(s, l), 0), s)) for s in range(sections)
    ]
    count = sections * members * portion
    return pl.pallas_call(
        functools.partial(rotate_kernel, sections),
        grid=(members,),
        in_specs=[pl.BlockSpec((ROT, ROT), lambda l: (0, 0))] + value_specs + sign_specs,
        out_specs=pl.BlockSpec((1, ROT, sections * blocks), lambda l: (l, 0, 0)),
        out_shape=jax.ShapeDtypeStruct((members, ROT, sections * blocks), jnp.bfloat16),
        scratch_shapes=[pltpu.VMEM((rows, LANES), jnp.float32)],
        compiler_params=pltpu.CompilerParams(vmem_limit_bytes=VMEM_LIMIT),
        cost_estimate=pl.CostEstimate(flops=2 * count * ROT, bytes_accessed=10 * count, transcendentals=0),
        name="rotate_code",
    )(matrix, *([values] * sections), *([signs] * sections))


def group_sum_kernel(parts_ref, out_ref):
    total = parts_ref[0].astype(jnp.float32)
    for member in range(1, parts_ref.shape[0]):
        total = total + parts_ref[member].astype(jnp.float32)
    first = recode(total).astype(jnp.bfloat16)
    sections, _, blocks = out_ref.shape
    for section in range(sections):
        out_ref[section] = first[:, section * blocks : (section + 1) * blocks]


def group_sum(parts, sections):
    members, _, columns = parts.shape
    blocks = columns // sections
    together = sections if blocks % LANES else 1
    return pl.pallas_call(
        group_sum_kernel,
        grid=(sections // together,),
        in_specs=[pl.BlockSpec((members, ROT, together * blocks), lambda n: (0, 0, n))],
        out_specs=pl.BlockSpec((together, ROT, blocks), lambda n: (n, 0, 0)),
        out_shape=jax.ShapeDtypeStruct((sections, ROT, blocks), jnp.bfloat16),
        compiler_params=pltpu.CompilerParams(vmem_limit_bytes=VMEM_LIMIT),
        cost_estimate=pl.CostEstimate(
            flops=20 * sections * ROT * blocks, bytes_accessed=2 * parts.size, transcendentals=0
        ),
        name="group_sum_code",
    )(parts)


def finish_kernel(place_ref, matrix_ref, parts_ref, sign_ref, out_ref, max_ref):
    del place_ref
    second = parts_ref[0].astype(jnp.float32)
    for group in range(1, parts_ref.shape[0]):
        second = second + parts_ref[group].astype(jnp.float32)
    blocks = second.shape[1]
    natural = second.T
    block = lax.broadcasted_iota(jnp.int32, (blocks, HALVES * blocks), 0)
    lane = lax.broadcasted_iota(jnp.int32, (blocks, HALVES * blocks), 1)
    largest = jnp.zeros((1, HALVES * blocks), jnp.float32)
    for half in range(HALVES):
        peak = jnp.max(jnp.abs(natural[:, half * QGROUP : (half + 1) * QGROUP]), axis=1, keepdims=True)
        chosen = jnp.where(lane == HALVES * block + half, peak, 0.0)
        largest = jnp.maximum(largest, jnp.max(chosen, axis=0, keepdims=True))
    max_ref[...] = largest * jnp.float32(ROT**-0.5)
    turned = jnp.dot(
        natural, matrix_ref[...], precision=lax.Precision.HIGHEST, preferred_element_type=jnp.float32
    ) * jnp.float32(1.0 / ROT)
    for half in range(HALVES):
        at = pl.ds(half, blocks, stride=HALVES)
        part = turned[:, half * QGROUP : (half + 1) * QGROUP]
        out_ref[at, :] = jnp.where(sign_ref[at, :] == 0, part, -part)


def finish(parts, signs, matrix, place):
    groups, _, blocks = parts.shape
    rows = blocks * HALVES
    return pl.pallas_call(
        finish_kernel,
        grid_spec=pltpu.PrefetchScalarGridSpec(
            num_scalar_prefetch=1,
            grid=(1,),
            in_specs=[
                pl.BlockSpec((ROT, ROT), lambda i, p: (0, 0)),
                pl.BlockSpec((groups, ROT, blocks), lambda i, p: (0, 0, 0)),
                pl.BlockSpec((rows, LANES), lambda i, p: (p[0], 0)),
            ],
            out_specs=[
                pl.BlockSpec((rows, LANES), lambda i, p: (0, 0)),
                pl.BlockSpec((1, rows), lambda i, p: (0, 0)),
            ],
        ),
        out_shape=[
            jax.ShapeDtypeStruct((rows, LANES), jnp.float32),
            jax.ShapeDtypeStruct((1, rows), jnp.float32),
        ],
        compiler_params=pltpu.CompilerParams(vmem_limit_bytes=VMEM_LIMIT),
        name="sum_unrotate",
    )(place, matrix, parts, signs)


def shards(partials, signs):
    length = partials.shape[-1]
    members = lax.axis_size("local")
    groups = lax.axis_size("node")
    matrix = sylvester()
    values = partials.reshape(1, length)
    sign_rows = signs.reshape(length // LANES, LANES)
    coded = rotate(values, sign_rows, matrix.astype(jnp.bfloat16), members, groups, 0, groups)
    coded = lax.all_to_all(coded, "local", split_axis=0, concat_axis=0, tiled=True)
    first = group_sum(coded, groups)
    first = lax.all_to_all(first, "node", split_axis=0, concat_axis=0, tiled=True)
    place = (lax.axis_index("node") * members + lax.axis_index("local")).astype(jnp.int32).reshape(1)
    reduced, rotated_max = finish(first, sign_rows, matrix, place)
    return (reduced.reshape(-1), rotated_max.reshape(-1))


def solution(mesh):
    in_specs = (P("node", "local", None), P())
    out_specs = (P(("node", "local")), P(("node", "local")))
    return jax.shard_map(shards, mesh=mesh, in_specs=in_specs, out_specs=out_specs, check_vma=False)
```

```python
import functools
import jax
import jax.numpy as jnp
import numpy as np
from jax import lax
from jax.experimental import pallas as pl
from jax.experimental.pallas import tpu as pltpu
from jax.sharding import PartitionSpec as P

ROT = 256
QGROUP = 128
HALVES = ROT // QGROUP
LANES = 128
VMEM_LIMIT = 60 * 1024 * 1024
SUM_VMEM_LIMIT = 24 * 1024 * 1024


def sylvester():
    matrix = np.ones((1, 1), np.float32)
    while matrix.shape[0] < ROT:
        matrix = np.kron(np.array([[1, 1], [1, -1]], np.float32), matrix)
    return matrix


def leading_power(x):
    q = x * jnp.float32(2.0**23 + 1.0)
    return q - q * jnp.float32(1.0 - 2.0**-24)


def recode(values):
    columns = values.shape[1]
    magnitude = jnp.abs(values)
    grouped = magnitude.reshape(values.shape[0] // QGROUP, QGROUP, columns)
    largest = jnp.max(grouped, axis=1, keepdims=True)
    top = leading_power(jnp.clip(largest, 2.0**-30, 2.0**30))
    scale = top * jnp.float32(2.0**-7)
    least = scale * jnp.float32(2.0**-6)
    power = jnp.maximum(leading_power(grouped), least)
    shift = power * jnp.float32(2.0**20)
    nudged = grouped + power * jnp.float32(2.0**-4)
    nearest = (nudged + shift) - shift
    spacing = power * jnp.float32(2.0**-3)
    floored = jnp.where(nearest > nudged, nearest - spacing, nearest).reshape(values.shape)
    return jnp.where(values < 0.0, -floored, floored)


def rotate_kernel(sections, place_ref, matrix_ref, *refs):
    del place_ref
    value_refs = refs[:sections]
    sign_refs = refs[sections : 2 * sections]
    out_ref, turned = refs[2 * sections :]
    rows = sign_refs[0].shape[0]
    blocks = rows // HALVES
    for section in range(sections):
        values = value_refs[section][...].astype(jnp.float32).reshape(rows, LANES)
        turned[...] = jnp.where(sign_refs[section][...] == 0, values, -values)
        halves = [turned[pl.ds(half, blocks, stride=HALVES), :] for half in range(HALVES)]
        signed = jnp.concatenate(halves, axis=1).astype(jnp.bfloat16)
        rotated = lax.dot_general(
            matrix_ref[...], signed, (((1,), (1,)), ((), ())), preferred_element_type=jnp.float32
        )
        out_ref[0, :, section * blocks : (section + 1) * blocks] = recode(rotated).astype(jnp.bfloat16)


def rotate(values, signs, matrix, first_member, count, members, groups):
    length = values.shape[1]
    portion = length // (members * groups)
    blocks = portion // ROT
    rows = portion // LANES

    def place(section, member, first):
        return section * members + first[0] + member

    value_specs = [
        pl.BlockSpec((1, portion), functools.partial(lambda s, l, f: (0, place(s, l, f)), s)) for s in range(groups)
    ]
    sign_specs = [
        pl.BlockSpec((rows, LANES), functools.partial(lambda s, l, f: (place(s, l, f), 0), s)) for s in range(groups)
    ]
    entries = groups * count * portion
    return pl.pallas_call(
        functools.partial(rotate_kernel, groups),
        grid_spec=pltpu.PrefetchScalarGridSpec(
            num_scalar_prefetch=1,
            grid=(count,),
            in_specs=[pl.BlockSpec((ROT, ROT), lambda l, f: (0, 0))] + value_specs + sign_specs,
            out_specs=pl.BlockSpec((1, ROT, groups * blocks), lambda l, f: (l, 0, 0)),
            scratch_shapes=[pltpu.VMEM((rows, LANES), jnp.float32)],
        ),
        out_shape=jax.ShapeDtypeStruct((count, ROT, groups * blocks), jnp.bfloat16),
        compiler_params=pltpu.CompilerParams(vmem_limit_bytes=VMEM_LIMIT),
        cost_estimate=pl.CostEstimate(flops=2 * entries * ROT, bytes_accessed=10 * entries, transcendentals=0),
        name="rotate_code",
    )(first_member, matrix, *([values] * groups), *([signs] * groups))


def add_parts(parts_ref):
    total = parts_ref[0].astype(jnp.float32)
    for part in range(1, parts_ref.shape[0]):
        total = total + parts_ref[part].astype(jnp.float32)
    return total


def far_sum_kernel(parts_ref, out_ref):
    out_ref[...] = add_parts(parts_ref)


def far_sum(parts):
    members, _, columns = parts.shape
    tile = LANES if columns % LANES == 0 else columns
    return pl.pallas_call(
        far_sum_kernel,
        grid=(columns // tile,),
        in_specs=[pl.BlockSpec((members, ROT, tile), lambda n: (0, 0, n))],
        out_specs=pl.BlockSpec((ROT, tile), lambda n: (0, n)),
        out_shape=jax.ShapeDtypeStruct((ROT, columns), jnp.float32),
        compiler_params=pltpu.CompilerParams(vmem_limit_bytes=SUM_VMEM_LIMIT),
        cost_estimate=pl.CostEstimate(flops=2 * parts.size, bytes_accessed=3 * parts.size, transcendentals=0),
        name="far_sum",
    )(parts)


def group_sum_kernel(parts_ref, far_ref, out_ref):
    first = recode(add_parts(parts_ref) + far_ref[...]).astype(jnp.bfloat16)
    sections, _, blocks = out_ref.shape
    for section in range(sections):
        out_ref[section] = first[:, section * blocks : (section + 1) * blocks]


def group_sum(parts, far, sections):
    members, _, columns = parts.shape
    blocks = columns // sections
    together = sections if blocks % LANES else 1
    return pl.pallas_call(
        group_sum_kernel,
        grid=(sections // together,),
        in_specs=[
            pl.BlockSpec((members, ROT, together * blocks), lambda n: (0, 0, n)),
            pl.BlockSpec((ROT, together * blocks), lambda n: (0, n)),
        ],
        out_specs=pl.BlockSpec((together, ROT, blocks), lambda n: (n, 0, 0)),
        out_shape=jax.ShapeDtypeStruct((sections, ROT, blocks), jnp.bfloat16),
        compiler_params=pltpu.CompilerParams(vmem_limit_bytes=SUM_VMEM_LIMIT),
        cost_estimate=pl.CostEstimate(
            flops=20 * sections * ROT * blocks, bytes_accessed=3 * parts.size, transcendentals=0
        ),
        name="group_sum_code",
    )(parts, far)


def finish_kernel(place_ref, matrix_ref, parts_ref, sign_ref, out_ref, max_ref):
    del place_ref
    second = parts_ref[0].astype(jnp.float32)
    for group in range(1, parts_ref.shape[0]):
        second = second + parts_ref[group].astype(jnp.float32)
    blocks = second.shape[1]
    natural = second.T
    block = lax.broadcasted_iota(jnp.int32, (blocks, HALVES * blocks), 0)
    lane = lax.broadcasted_iota(jnp.int32, (blocks, HALVES * blocks), 1)
    largest = jnp.zeros((1, HALVES * blocks), jnp.float32)
    for half in range(HALVES):
        peak = jnp.max(jnp.abs(natural[:, half * QGROUP : (half + 1) * QGROUP]), axis=1, keepdims=True)
        chosen = jnp.where(lane == HALVES * block + half, peak, 0.0)
        largest = jnp.maximum(largest, jnp.max(chosen, axis=0, keepdims=True))
    max_ref[...] = largest * jnp.float32(ROT**-0.5)
    turned = jnp.dot(
        natural, matrix_ref[...], precision=lax.Precision.HIGHEST, preferred_element_type=jnp.float32
    ) * jnp.float32(1.0 / ROT)
    for half in range(HALVES):
        at = pl.ds(half, blocks, stride=HALVES)
        part = turned[:, half * QGROUP : (half + 1) * QGROUP]
        out_ref[at, :] = jnp.where(sign_ref[at, :] == 0, part, -part)


def finish(parts, signs, matrix, place):
    groups, _, blocks = parts.shape
    rows = blocks * HALVES
    return pl.pallas_call(
        finish_kernel,
        grid_spec=pltpu.PrefetchScalarGridSpec(
            num_scalar_prefetch=1,
            grid=(1,),
            in_specs=[
                pl.BlockSpec((ROT, ROT), lambda i, p: (0, 0)),
                pl.BlockSpec((groups, ROT, blocks), lambda i, p: (0, 0, 0)),
                pl.BlockSpec((rows, LANES), lambda i, p: (p[0], 0)),
            ],
            out_specs=[
                pl.BlockSpec((rows, LANES), lambda i, p: (0, 0)),
                pl.BlockSpec((1, rows), lambda i, p: (0, 0)),
            ],
        ),
        out_shape=[
            jax.ShapeDtypeStruct((rows, LANES), jnp.float32),
            jax.ShapeDtypeStruct((1, rows), jnp.float32),
        ],
        compiler_params=pltpu.CompilerParams(vmem_limit_bytes=VMEM_LIMIT),
        name="sum_unrotate",
    )(place, matrix, parts, signs)


def shards(partials, signs):
    length = partials.shape[-1]
    members = lax.axis_size("local")
    groups = lax.axis_size("node")
    half = members // 2
    matrix = sylvester()
    binary = jnp.asarray(matrix, jnp.bfloat16)
    values = partials.reshape(1, length)
    sign_rows = signs.reshape(length // LANES, LANES)
    node = lax.axis_index("node").astype(jnp.int32)
    member = lax.axis_index("local").astype(jnp.int32)
    near_first = (member - lax.rem(member, half)).reshape(1)
    far_first = half - near_first
    sides = [list(range(half)), list(range(half, members))]

    def exchange(parts):
        return lax.all_to_all(parts, "local", split_axis=0, concat_axis=0, axis_index_groups=sides, tiled=True)

    far = exchange(rotate(values, sign_rows, binary, far_first, half, members, groups))
    near = exchange(rotate(values, sign_rows, binary, near_first, half, members, groups))
    across = [(m, (m + half) % members) for m in range(members)]
    far = lax.ppermute(far_sum(far), "local", across)
    first = group_sum(near, far, groups)
    first = lax.all_to_all(first, "node", split_axis=0, concat_axis=0, tiled=True)
    place = (node * members + member).reshape(1)
    reduced, rotated_max = finish(first, sign_rows, jnp.asarray(matrix), place)
    return (reduced.reshape(-1), rotated_max.reshape(-1))


def solution(mesh):
    in_specs = (P("node", "local", None), P())
    out_specs = (P(("node", "local")), P(("node", "local")))
    return jax.shard_map(shards, mesh=mesh, in_specs=in_specs, out_specs=out_specs, check_vma=False)
```

```python
import functools
import jax
import jax.numpy as jnp
import numpy as np
from jax import lax
from jax.experimental import pallas as pl
from jax.experimental.pallas import tpu as pltpu
from jax.sharding import PartitionSpec as P

ROT = 256
QGROUP = 128
HALVES = ROT // QGROUP
LANES = 128
VMEM_LIMIT = 60 * 1024 * 1024
SUM_VMEM_LIMIT = 24 * 1024 * 1024


def sylvester():
    matrix = np.ones((1, 1), np.float32)
    while matrix.shape[0] < ROT:
        matrix = np.kron(np.array([[1, 1], [1, -1]], np.float32), matrix)
    return matrix


def partner(index, step, count):
    if count & (count - 1) == 0:
        return index ^ step
    return (index + step) % count


def leading_power(x):
    q = x * jnp.float32(2.0**23 + 1.0)
    return q - q * jnp.float32(1.0 - 2.0**-24)


def recode(values):
    magnitude = jnp.abs(values)
    largest = jnp.max(magnitude, axis=0, keepdims=True)
    scale = leading_power(jnp.clip(largest, 2.0**-30, 2.0**30)) * jnp.float32(2.0**-7)
    least = scale * jnp.float32(2.0**-6)
    power = jnp.maximum(leading_power(magnitude), least)
    shift = power * jnp.float32(2.0**20)
    nudged = magnitude + power * jnp.float32(2.0**-4)
    nearest = (nudged + shift) - shift
    spacing = power * jnp.float32(2.0**-3)
    floored = jnp.where(nearest > nudged, nearest - spacing, nearest)
    return jnp.where(values < 0.0, -floored, floored)


def rotate_kernel(sections, place_ref, matrix_ref, *refs):
    del place_ref
    value_refs = refs[:sections]
    sign_refs = refs[sections : 2 * sections]
    out_refs = refs[2 * sections : -1]
    turned = refs[-1]
    rows = sign_refs[0].shape[0]
    blocks = rows // HALVES
    for section in range(sections):
        values = value_refs[section][...].astype(jnp.float32).reshape(rows, LANES)
        turned[...] = jnp.where(sign_refs[section][...] == 0, values, -values)
        halves = [turned[pl.ds(half, blocks, stride=HALVES), :] for half in range(HALVES)]
        signed = jnp.concatenate(halves, axis=1).astype(jnp.bfloat16)
        rotated = lax.dot_general(
            matrix_ref[...], signed, (((1,), (1,)), ((), ())), preferred_element_type=jnp.float32
        )
        columns = slice(section * blocks, (section + 1) * blocks)
        for half in range(HALVES):
            coded = recode(rotated[half * QGROUP : (half + 1) * QGROUP]).astype(jnp.bfloat16)
            if len(out_refs) == 1:
                out_refs[0][half * QGROUP : (half + 1) * QGROUP, columns] = coded
            else:
                out_refs[half][:, columns] = coded


def rotate(values, signs, matrix, place, other, step, members, groups, split):
    length = values.shape[1]
    portion = length // (members * groups)
    blocks = portion // ROT
    rows = portion // LANES
    half = members // 2

    def position(section, at):
        first = half - at[1] if other else at[1]
        return partner(at[0], section, groups) * members + first + partner(at[2], step, half)

    value_specs = [
        pl.BlockSpec((1, portion), functools.partial(lambda s, i, at: (0, position(s, at)), s)) for s in range(groups)
    ]
    sign_specs = [
        pl.BlockSpec((rows, LANES), functools.partial(lambda s, i, at: (position(s, at), 0), s)) for s in range(groups)
    ]
    entries = groups * portion
    shape = (QGROUP if split else ROT, groups * blocks)
    outs = HALVES if split else 1
    return pl.pallas_call(
        functools.partial(rotate_kernel, groups),
        grid_spec=pltpu.PrefetchScalarGridSpec(
            num_scalar_prefetch=1,
            grid=(1,),
            in_specs=[pl.BlockSpec((ROT, ROT), lambda i, at: (0, 0))] + value_specs + sign_specs,
            out_specs=[pl.BlockSpec(shape, lambda i, at: (0, 0))] * outs,
            scratch_shapes=[pltpu.VMEM((rows, LANES), jnp.float32)],
        ),
        out_shape=[jax.ShapeDtypeStruct(shape, jnp.bfloat16)] * outs,
        compiler_params=pltpu.CompilerParams(vmem_limit_bytes=VMEM_LIMIT),
        cost_estimate=pl.CostEstimate(flops=2 * entries * ROT, bytes_accessed=10 * entries, transcendentals=0),
        name="rotate_code",
    )(place, matrix, *([values] * groups), *([signs] * groups))


def add_all(refs):
    total = refs[0][...].astype(jnp.float32)
    for ref in refs[1:]:
        total = total + ref[...].astype(jnp.float32)
    return total


def far_sum_kernel(*refs):
    refs[-1][...] = add_all(refs[:-1])


def far_sum(parts):
    shape = parts[0].shape
    size = shape[0] * shape[1]
    return pl.pallas_call(
        far_sum_kernel,
        out_shape=jax.ShapeDtypeStruct(shape, jnp.float32),
        compiler_params=pltpu.CompilerParams(vmem_limit_bytes=SUM_VMEM_LIMIT),
        cost_estimate=pl.CostEstimate(
            flops=2 * len(parts) * size, bytes_accessed=(2 * len(parts) + 4) * size, transcendentals=0
        ),
        name="far_sum",
    )(*parts)


def group_sum_kernel(parts, *refs):
    first = recode(add_all(refs[:parts])).astype(jnp.bfloat16)
    blocks = refs[parts].shape[1]
    for section, out_ref in enumerate(refs[parts:]):
        out_ref[...] = first[:, section * blocks : (section + 1) * blocks]


def group_sum(near, far, half, groups):
    columns = near[0].shape[1]
    blocks = columns // groups
    size = QGROUP * columns
    count = len(near) + len(far)
    return pl.pallas_call(
        functools.partial(group_sum_kernel, count),
        grid=(1,),
        in_specs=[pl.BlockSpec((QGROUP, columns), lambda i: (half, 0))] * len(near)
        + [pl.BlockSpec((QGROUP, columns), lambda i: (0, 0))] * len(far),
        out_specs=[pl.BlockSpec((QGROUP, blocks), lambda i: (0, 0))] * groups,
        out_shape=[jax.ShapeDtypeStruct((QGROUP, blocks), jnp.bfloat16)] * groups,
        compiler_params=pltpu.CompilerParams(vmem_limit_bytes=SUM_VMEM_LIMIT),
        cost_estimate=pl.CostEstimate(flops=20 * size, bytes_accessed=2 * (count + 1) * size, transcendentals=0),
        name="group_sum_code",
    )(*near, *far)


def bfloat16_terms(values):
    terms = []
    for _ in range(3):
        terms.append(values.astype(jnp.bfloat16))
        values = values - terms[-1].astype(jnp.float32)
    return terms


def finish_kernel(groups, matrix_ref, sign_ref, *refs):
    out_ref, max_ref = refs[-2:]
    second = [add_all(refs[half * groups : (half + 1) * groups]) for half in range(HALVES)]
    blocks = second[0].shape[1]
    natural = jnp.concatenate([part.T for part in second], axis=1)
    block = lax.broadcasted_iota(jnp.int32, (blocks, HALVES * blocks), 0)
    lane = lax.broadcasted_iota(jnp.int32, (blocks, HALVES * blocks), 1)
    largest = jnp.zeros((1, HALVES * blocks), jnp.float32)
    for half in range(HALVES):
        peak = jnp.max(jnp.abs(natural[:, half * QGROUP : (half + 1) * QGROUP]), axis=1, keepdims=True)
        chosen = jnp.where(lane == HALVES * block + half, peak, 0.0)
        largest = jnp.maximum(largest, jnp.max(chosen, axis=0, keepdims=True))
    max_ref[...] = largest * jnp.float32(ROT**-0.5)
    high, middle, low = [
        jnp.dot(term, matrix_ref[...], preferred_element_type=jnp.float32) for term in bfloat16_terms(natural)
    ]
    turned = (high + (middle + low)) * jnp.float32(1.0 / ROT)
    for half in range(HALVES):
        at = pl.ds(half, blocks, stride=HALVES)
        part = turned[:, half * QGROUP : (half + 1) * QGROUP]
        out_ref[at, :] = jnp.where(sign_ref[at, :] == 0, part, -part)


def finish(parts, signs, matrix):
    groups = len(parts[0])
    rows = signs.shape[0]
    return pl.pallas_call(
        functools.partial(finish_kernel, groups),
        out_shape=[
            jax.ShapeDtypeStruct((rows, LANES), jnp.float32),
            jax.ShapeDtypeStruct((1, rows), jnp.float32),
        ],
        compiler_params=pltpu.CompilerParams(vmem_limit_bytes=SUM_VMEM_LIMIT),
        name="sum_unrotate",
    )(matrix, signs, *[part for half in parts for part in half])


def shards(partials, signs):
    length = partials.shape[-1]
    members = lax.axis_size("local")
    groups = lax.axis_size("node")
    half = members // 2
    binary = jnp.asarray(sylvester(), jnp.bfloat16)
    values = partials.reshape(1, length)
    sign_rows = signs.reshape(length // LANES, LANES)
    node = lax.axis_index("node").astype(jnp.int32)
    member = lax.axis_index("local").astype(jnp.int32)
    inner = lax.rem(member, half)
    place = jnp.stack([node, member - inner, inner])
    own_rows = sign_rows.shape[0] // (members * groups)
    own_signs = lax.dynamic_slice_in_dim(sign_rows, (node * members + member) * own_rows, own_rows)

    def turn(other, step, split):
        return rotate(values, sign_rows, binary, place, other, step, members, groups, split)

    def send(part, other, step):
        pairs = []
        for source in range(members):
            first, index = source // half * half, source % half
            pairs.append((source, (half - first if other else first) + partner(index, step, half)))
        return lax.ppermute(part, "local", pairs)

    def share(parts):
        moved = [parts[0]]
        for step in range(1, groups):
            pairs = [(source, partner(source, step, groups)) for source in range(groups)]
            moved.append(lax.ppermute(parts[step], "node", pairs))
        return moved

    summed, direct, near = [], [], []
    for step in list(range(1, half)) + [0]:
        for_sum, for_owner = turn(True, step, True)
        summed.append(send(for_sum, False, step) if step else for_sum)
        direct.append(send(for_owner, True, step))
    for step in list(range(1, half)) + [0]:
        (part,) = turn(False, step, False)
        near.append(send(part, False, step) if step else part)
    across = send(far_sum(summed), True, 0)
    second_half = share(group_sum(near, direct, 1, groups))
    first_half = share(group_sum(near, [across], 0, groups))
    reduced, rotated_max = finish([first_half, second_half], own_signs, binary)
    return (reduced.reshape(-1), rotated_max.reshape(-1))


def solution(mesh):
    in_specs = (P("node", "local", None), P())
    out_specs = (P(("node", "local")), P(("node", "local")))
    return jax.shard_map(shards, mesh=mesh, in_specs=in_specs, out_specs=out_specs, check_vma=False)
```

```python
import functools
import jax
import jax.numpy as jnp
import numpy as np
from jax import lax
from jax.experimental import pallas as pl
from jax.experimental.pallas import tpu as pltpu
from jax.sharding import PartitionSpec as P

ROT = 256
QGROUP = 128
HALVES = ROT // QGROUP
LANES = 128
VMEM_LIMIT = 60 * 1024 * 1024
SUM_VMEM_LIMIT = 24 * 1024 * 1024


def sylvester():
    matrix = np.ones((1, 1), np.float32)
    while matrix.shape[0] < ROT:
        matrix = np.kron(np.array([[1, 1], [1, -1]], np.float32), matrix)
    return matrix


def partner(index, step, count):
    if count & (count - 1) == 0:
        return index ^ step
    return (index + step) % count


def leading_power(x):
    q = x * jnp.float32(2.0**23 + 1.0)
    return q - q * jnp.float32(1.0 - 2.0**-24)


def recode(values):
    magnitude = jnp.abs(values)
    largest = jnp.max(magnitude, axis=-2, keepdims=True)
    least = leading_power(jnp.clip(largest, 2.0**-30, 2.0**30)) * jnp.float32(2.0**-13)
    shift = leading_power(jnp.maximum(magnitude, least)) * jnp.float32(2.0**20)
    nearest = (magnitude + shift) - shift
    rest = magnitude - nearest
    coded = jnp.where(rest == shift * jnp.float32(2.0**-24), magnitude + rest, nearest)
    return jnp.where(values < 0.0, -coded, coded)


class Layout:
    def __init__(self, length, members, groups):
        self.members = members
        self.groups = groups
        self.half = members // 2
        self.portion = length // (members * groups)
        self.rows = self.portion // LANES
        self.blocks = self.portion // ROT
        self.together = 1
        if self.blocks < LANES and LANES % self.blocks == 0 and groups % (LANES // self.blocks) == 0:
            self.together = LANES // self.blocks
        self.units = groups // self.together
        self.columns = self.together * self.blocks

    def shape(self):
        return (self.units, QGROUP, self.columns)


def rotate_kernel(layout, other, steps, split, values_ref, signs_ref, matrix_ref, *refs):
    count = len(steps) * layout.units
    outs = len(steps) * (HALVES if split else 1)
    out_refs = refs[:outs]
    values, flips, turned, coded, value_sems, sign_sems, out_sems = refs[outs:]
    node = lax.axis_index("node")
    member = lax.axis_index("local")
    inner = lax.rem(member, layout.half)
    first = layout.half - (member - inner) if other else member - inner
    portion, rows = layout.portion, layout.rows

    def fetches(unit, part, place):
        return (
            pltpu.make_async_copy(
                values_ref.at[:, pl.ds(pl.multiple_of(place * portion, portion), portion)],
                values.at[unit, :, pl.ds(part * portion, portion)],
                value_sems.at[unit, part],
            ),
            pltpu.make_async_copy(
                signs_ref.at[pl.ds(pl.multiple_of(place * rows, rows), rows), :],
                flips.at[unit, pl.ds(part * rows, rows), :],
                sign_sems.at[unit, part],
            ),
        )

    for index, step in enumerate(steps):
        for section in range(layout.groups):
            place = partner(node, section, layout.groups) * layout.members + first + partner(inner, step, layout.half)
            unit = index * layout.units + section // layout.together
            for copy in fetches(unit, section % layout.together, place):
                copy.start()

    def results(index):
        if split:
            return [
                pltpu.make_async_copy(
                    coded.at[pl.ds(index * layout.units, layout.units), pl.ds(half * QGROUP, QGROUP), :],
                    out_refs[index * HALVES + half],
                    out_sems.at[index, half],
                )
                for half in range(HALVES)
            ]
        return [
            pltpu.make_async_copy(
                coded.at[pl.ds(index * layout.units, layout.units)], out_refs[index], out_sems.at[index, 0]
            )
        ]

    def body(unit, carry):
        for part in range(layout.together):
            for copy in fetches(unit, part, 0):
                copy.wait()
        wide = values[unit].astype(jnp.float32).reshape(layout.together * rows, LANES)
        turned[...] = jnp.where(flips[unit] == 0, wide, -wide)
        halves = [turned[pl.ds(half, layout.columns, stride=HALVES), :] for half in range(HALVES)]
        signed = jnp.concatenate(halves, axis=1).astype(jnp.bfloat16)
        rotated = lax.dot_general(
            matrix_ref[...], signed, (((1,), (1,)), ((), ())), preferred_element_type=jnp.float32
        )
        for half in range(HALVES):
            at = slice(half * QGROUP, (half + 1) * QGROUP)
            coded[unit, at, :] = recode(rotated[at]).astype(jnp.bfloat16)
        for index in range(len(steps)):

            @pl.when(unit == (index + 1) * layout.units - 1)
            def _():
                for copy in results(index):
                    copy.start()

        return carry

    lax.fori_loop(0, count, body, 0)
    for index in range(len(steps)):
        for copy in results(index):
            copy.wait()


def rotate(values, signs, matrix, layout, other, steps, split):
    count = len(steps) * layout.units
    entries = len(steps) * layout.groups * layout.portion
    outs = [layout.shape()] * (HALVES * len(steps))
    if not split:
        outs = [(layout.units, ROT, layout.columns)] * len(steps)
    return pl.pallas_call(
        functools.partial(rotate_kernel, layout, other, steps, split),
        in_specs=[
            pl.BlockSpec(memory_space=pl.ANY),
            pl.BlockSpec(memory_space=pl.ANY),
            pl.BlockSpec(memory_space=pltpu.VMEM),
        ],
        out_specs=[pl.BlockSpec(memory_space=pl.ANY)] * len(outs),
        out_shape=[jax.ShapeDtypeStruct(shape, jnp.bfloat16) for shape in outs],
        scratch_shapes=[
            pltpu.VMEM((count, 1, layout.together * layout.portion), jnp.bfloat16),
            pltpu.VMEM((count, layout.together * layout.rows, LANES), jnp.int32),
            pltpu.VMEM((layout.together * layout.rows, LANES), jnp.float32),
            pltpu.VMEM((count, ROT, layout.columns), jnp.bfloat16),
            pltpu.SemaphoreType.DMA((count, layout.together)),
            pltpu.SemaphoreType.DMA((count, layout.together)),
            pltpu.SemaphoreType.DMA((len(steps), HALVES)),
        ],
        compiler_params=pltpu.CompilerParams(vmem_limit_bytes=VMEM_LIMIT),
        cost_estimate=pl.CostEstimate(flops=2 * entries * ROT, bytes_accessed=10 * entries, transcendentals=0),
        name="rotate_code",
    )(values, signs, matrix)


def add_all(refs):
    total = refs[0][...].astype(jnp.float32)
    for ref in refs[1:]:
        total = total + ref[...].astype(jnp.float32)
    return total


def far_sum_kernel(*refs):
    refs[-1][...] = add_all(refs[:-1])


def far_sum(parts):
    size = parts[0].size
    return pl.pallas_call(
        far_sum_kernel,
        out_shape=jax.ShapeDtypeStruct(parts[0].shape, jnp.float32),
        compiler_params=pltpu.CompilerParams(vmem_limit_bytes=SUM_VMEM_LIMIT),
        cost_estimate=pl.CostEstimate(
            flops=2 * len(parts) * size, bytes_accessed=(2 * len(parts) + 4) * size, transcendentals=0
        ),
        name="far_sum",
    )(*parts)


def group_sum_kernel(layout, parts, *refs):
    first = recode(add_all(refs[:parts])).astype(jnp.bfloat16)
    for section, out_ref in enumerate(refs[parts:]):
        at = section % layout.together * layout.blocks
        out_ref[...] = first[section // layout.together, :, at : at + layout.blocks]


def group_sum(near, far, half, layout):
    size = far[0].size
    count = len(near) + len(far)
    return pl.pallas_call(
        functools.partial(group_sum_kernel, layout, count),
        grid=(1,),
        in_specs=[pl.BlockSpec(layout.shape(), lambda i: (0, half, 0))] * len(near)
        + [pl.BlockSpec(layout.shape(), lambda i: (0, 0, 0))] * len(far),
        out_specs=[pl.BlockSpec((QGROUP, layout.blocks), lambda i: (0, 0))] * layout.groups,
        out_shape=[jax.ShapeDtypeStruct((QGROUP, layout.blocks), jnp.bfloat16)] * layout.groups,
        compiler_params=pltpu.CompilerParams(vmem_limit_bytes=SUM_VMEM_LIMIT),
        cost_estimate=pl.CostEstimate(flops=20 * size, bytes_accessed=2 * (count + 1) * size, transcendentals=0),
        name="group_sum_code",
    )(*near, *far)


def bfloat16_terms(values):
    terms = []
    for _ in range(3):
        terms.append(values.astype(jnp.bfloat16))
        values = values - terms[-1].astype(jnp.float32)
    return terms


def finish_kernel(groups, matrix_ref, sign_ref, *refs):
    out_ref, max_ref = refs[-2:]
    second = [add_all(refs[half * groups : (half + 1) * groups]) for half in range(HALVES)]
    blocks = second[0].shape[1]
    natural = jnp.concatenate([part.T for part in second], axis=1)
    block = lax.broadcasted_iota(jnp.int32, (blocks, HALVES * blocks), 0)
    lane = lax.broadcasted_iota(jnp.int32, (blocks, HALVES * blocks), 1)
    largest = jnp.zeros((1, HALVES * blocks), jnp.float32)
    for half in range(HALVES):
        peak = jnp.max(jnp.abs(natural[:, half * QGROUP : (half + 1) * QGROUP]), axis=1, keepdims=True)
        chosen = jnp.where(lane == HALVES * block + half, peak, 0.0)
        largest = jnp.maximum(largest, jnp.max(chosen, axis=0, keepdims=True))
    max_ref[...] = largest * jnp.float32(ROT**-0.5)
    high, middle, low = [
        jnp.dot(term, matrix_ref[...], preferred_element_type=jnp.float32) for term in bfloat16_terms(natural)
    ]
    turned = (high + (middle + low)) * jnp.float32(1.0 / ROT)
    for half in range(HALVES):
        at = pl.ds(half, blocks, stride=HALVES)
        part = turned[:, half * QGROUP : (half + 1) * QGROUP]
        out_ref[at, :] = jnp.where(sign_ref[at, :] == 0, part, -part)


def finish(parts, signs, matrix):
    groups = len(parts[0])
    rows = signs.shape[0]
    return pl.pallas_call(
        functools.partial(finish_kernel, groups),
        out_shape=[
            jax.ShapeDtypeStruct((rows, LANES), jnp.float32),
            jax.ShapeDtypeStruct((1, rows), jnp.float32),
        ],
        compiler_params=pltpu.CompilerParams(vmem_limit_bytes=SUM_VMEM_LIMIT),
        name="sum_unrotate",
    )(matrix, signs, *[part for half in parts for part in half])


def shards(partials, signs):
    length = partials.shape[-1]
    members = lax.axis_size("local")
    groups = lax.axis_size("node")
    layout = Layout(length, members, groups)
    half = layout.half
    matrix = jnp.asarray(sylvester(), jnp.bfloat16)
    values = partials.reshape(1, length)
    sign_rows = signs.reshape(length // LANES, LANES)
    own = (lax.axis_index("node") * members + lax.axis_index("local")) * layout.rows
    own_signs = lax.dynamic_slice_in_dim(sign_rows, own, layout.rows)

    def send(part, other, step):
        pairs = []
        for source in range(members):
            first, index = source // half * half, source % half
            pairs.append((source, (half - first if other else first) + partner(index, step, half)))
        return lax.ppermute(part, "local", pairs)

    def share(parts):
        moved = [parts[0]]
        for step in range(1, groups):
            pairs = [(source, partner(source, step, groups)) for source in range(groups)]
            moved.append(lax.ppermute(parts[step], "node", pairs))
        return moved

    steps = list(range(half))
    far = rotate(values, sign_rows, matrix, layout, True, steps, True)
    direct = [send(far[HALVES * step + 1], True, step) for step in steps]
    summed = [far[0]] + [send(far[HALVES * step], False, step) for step in steps[1:]]
    near = rotate(values, sign_rows, matrix, layout, False, steps, False)
    near = [near[0]] + [send(near[step], False, step) for step in steps[1:]]
    across = send(far_sum(summed), True, 0)
    second_half = share(group_sum(near, direct, 1, layout))
    first_half = share(group_sum(near, [across], 0, layout))
    reduced, rotated_max = finish([first_half, second_half], own_signs, matrix)
    return (reduced.reshape(-1), rotated_max.reshape(-1))


def solution(mesh):
    in_specs = (P("node", "local", None), P())
    out_specs = (P(("node", "local")), P(("node", "local")))
    return jax.shard_map(shards, mesh=mesh, in_specs=in_specs, out_specs=out_specs, check_vma=False)
```

```python
import functools
import jax
import jax.numpy as jnp
from jax import lax
from jax.experimental import pallas as pl
from jax.experimental.pallas import tpu as pltpu
from jax.sharding import PartitionSpec as P

ROT = 256
QGROUP = 128
HALVES = ROT // QGROUP
LANES = 128
VMEM_LIMIT = 60 * 1024 * 1024
SUM_VMEM_LIMIT = 24 * 1024 * 1024


def sylvester():
    row = lax.broadcasted_iota(jnp.int32, (ROT, ROT), 0)
    column = lax.broadcasted_iota(jnp.int32, (ROT, ROT), 1)
    parity = lax.population_count(row & column) & 1
    return (1 - 2 * parity).astype(jnp.float32).astype(jnp.bfloat16)


def partner(index, step, count):
    if count & (count - 1) == 0:
        return index ^ step
    return (index + step) % count


def leading_power(x):
    q = x * jnp.float32(2.0**23 + 1.0)
    return q - q * jnp.float32(1.0 - 2.0**-24)


def recode(values):
    magnitude = jnp.abs(values)
    largest = jnp.max(magnitude, axis=-2, keepdims=True)
    least = leading_power(jnp.clip(largest, 2.0**-30, 2.0**30)) * jnp.float32(2.0**-13)
    shift = leading_power(jnp.maximum(magnitude, least)) * jnp.float32(2.0**20)
    nearest = (magnitude + shift) - shift
    rest = magnitude - nearest
    coded = jnp.where(rest == shift * jnp.float32(2.0**-24), magnitude + rest, nearest)
    return jnp.where(values < 0.0, -coded, coded)


class Layout:
    def __init__(self, length, members, groups):
        self.members = members
        self.groups = groups
        self.half = members // 2
        self.portion = length // (members * groups)
        self.rows = self.portion // LANES
        self.blocks = self.portion // ROT
        self.together = 1
        if self.blocks < LANES and LANES % self.blocks == 0 and groups % (LANES // self.blocks) == 0:
            self.together = LANES // self.blocks
        self.units = groups // self.together
        self.columns = self.together * self.blocks

    def shape(self):
        return (self.units, QGROUP, self.columns)


def rotate_kernel(layout, values_ref, signs_ref, *refs):
    half, units = layout.half, layout.units
    direct_ref, flips_ref = refs[:2]
    paired_refs = refs[2 : 2 + half]
    values, flips, turned, matrix, coded, value_sems, sign_sems, out_sems, flip_sem = refs[2 + half :]
    node = lax.axis_index("node")
    member = lax.axis_index("local")
    inner = lax.rem(member, half)
    near_first = member - inner
    portion, rows = layout.portion, layout.rows

    def owner(index):
        far = index % 2 == 0
        return jnp.where(far, half - near_first, near_first) + partner(inner, index // 2, half)

    def fetches(index, unit, part):
        section = unit * layout.together + part
        place = partner(node, section, layout.groups) * layout.members + owner(index)
        return (
            pltpu.make_async_copy(
                values_ref.at[:, pl.ds(pl.multiple_of(place * portion, portion), portion)],
                values.at[index, unit, :, pl.ds(part * portion, portion)],
                value_sems.at[index, unit, part],
            ),
            pltpu.make_async_copy(
                signs_ref.at[pl.ds(pl.multiple_of(place * rows, rows), rows), :],
                flips.at[index, unit, pl.ds(part * rows, rows), :],
                sign_sems.at[index, unit, part],
            ),
        )

    def pieces():
        return [(unit, part) for unit in range(units) for part in range(layout.together)]

    def own_flips():
        own = node * layout.members + member
        return pltpu.make_async_copy(
            signs_ref.at[pl.ds(pl.multiple_of(own * rows, rows), rows), :], flips_ref, flip_sem
        )

    def fetch(index, carry):
        for unit, part in pieces():
            for copy in fetches(index, unit, part):
                copy.start()
        return carry

    lax.fori_loop(0, layout.members, fetch, 0)
    own_flips().start()
    matrix[...] = sylvester()

    def direct(index):
        return pltpu.make_async_copy(coded.at[index, 1], direct_ref.at[owner(index)], out_sems.at[index, 1])

    def paired(index, step):
        return pltpu.make_async_copy(coded.at[index, 0], paired_refs[step].at[index % 2], out_sems.at[index, 0])

    def body(index, carry):
        for unit, part in pieces():
            for copy in fetches(index, unit, part):
                copy.wait()
        for unit in range(units):
            wide = values[index, unit].astype(jnp.float32).reshape(layout.together * rows, LANES)
            turned[unit] = jnp.where(flips[index, unit] == 0, wide, -wide)
            halves = [turned[unit, pl.ds(part, layout.columns, stride=HALVES), :] for part in range(HALVES)]
            signed = jnp.concatenate(halves, axis=1).astype(jnp.bfloat16)
            rotated = lax.dot_general(
                matrix[...], signed, (((1,), (1,)), ((), ())), preferred_element_type=jnp.float32
            )
            for part in range(HALVES):
                coded[index, part, unit] = recode(rotated[part * QGROUP : (part + 1) * QGROUP]).astype(jnp.bfloat16)
        direct(index).start()
        for step in range(half):

            @pl.when(index // 2 == step)
            def _():
                paired(index, step).start()

        return carry

    lax.fori_loop(0, layout.members, body, 0)

    def finish_copies(index, carry):
        direct(index).wait()
        paired(index, 0).wait()
        return carry

    lax.fori_loop(0, layout.members, finish_copies, 0)
    own_flips().wait()


def rotate(values, signs, layout):
    members, units, columns = layout.members, layout.units, layout.columns
    entries = members * layout.groups * layout.portion
    return pl.pallas_call(
        functools.partial(rotate_kernel, layout),
        in_specs=[pl.BlockSpec(memory_space=pl.ANY)] * 2,
        out_specs=[pl.BlockSpec(memory_space=pl.ANY)] * (2 + layout.half),
        out_shape=[
            jax.ShapeDtypeStruct((members,) + layout.shape(), jnp.bfloat16),
            jax.ShapeDtypeStruct((layout.rows, LANES), jnp.int32),
        ]
        + [jax.ShapeDtypeStruct((2,) + layout.shape(), jnp.bfloat16)] * layout.half,
        scratch_shapes=[
            pltpu.VMEM((members, units, 1, layout.together * layout.portion), jnp.bfloat16),
            pltpu.VMEM((members, units, layout.together * layout.rows, LANES), jnp.int32),
            pltpu.VMEM((units, layout.together * layout.rows, LANES), jnp.float32),
            pltpu.VMEM((ROT, ROT), jnp.bfloat16),
            pltpu.VMEM((members, HALVES) + layout.shape(), jnp.bfloat16),
            pltpu.SemaphoreType.DMA((members, units, layout.together)),
            pltpu.SemaphoreType.DMA((members, units, layout.together)),
            pltpu.SemaphoreType.DMA((members, HALVES)),
            pltpu.SemaphoreType.DMA,
        ],
        compiler_params=pltpu.CompilerParams(vmem_limit_bytes=VMEM_LIMIT),
        cost_estimate=pl.CostEstimate(flops=2 * entries * ROT, bytes_accessed=10 * entries, transcendentals=0),
        name="rotate_code",
    )(values, signs)


def add_all(arrays):
    total = arrays[0].astype(jnp.float32)
    for array in arrays[1:]:
        total = total + array.astype(jnp.float32)
    return total


def far_sum_kernel(*refs):
    refs[-1][...] = add_all([ref[0] for ref in refs[:-1]])


def far_sum(paired, layout):
    size = paired[0].size // 2
    return pl.pallas_call(
        far_sum_kernel,
        out_shape=jax.ShapeDtypeStruct(layout.shape(), jnp.float32),
        compiler_params=pltpu.CompilerParams(vmem_limit_bytes=SUM_VMEM_LIMIT),
        cost_estimate=pl.CostEstimate(
            flops=2 * len(paired) * size, bytes_accessed=(2 * len(paired) + 4) * size, transcendentals=0
        ),
        name="far_sum",
    )(*paired)


def write_sections(layout, total, out_refs):
    first = recode(total).astype(jnp.bfloat16)
    for section, out_ref in enumerate(out_refs):
        at = section % layout.together * layout.blocks
        out_ref[...] = first[section // layout.together, :, at : at + layout.blocks]


def direct_sum_kernel(layout, parts_ref, *out_refs):
    write_sections(layout, add_all([parts_ref[member] for member in range(layout.members)]), out_refs)


def paired_sum_kernel(layout, across_ref, *refs):
    near = [ref[1] for ref in refs[: layout.half]]
    write_sections(layout, add_all(near + [across_ref[...]]), refs[layout.half :])


def group_sum(kernel, layout, *parts):
    size = QGROUP * layout.units * layout.columns
    return pl.pallas_call(
        functools.partial(kernel, layout),
        out_shape=[jax.ShapeDtypeStruct((QGROUP, layout.blocks), jnp.bfloat16)] * layout.groups,
        compiler_params=pltpu.CompilerParams(vmem_limit_bytes=SUM_VMEM_LIMIT),
        cost_estimate=pl.CostEstimate(
            flops=30 * size, bytes_accessed=2 * (layout.members + 1) * size, transcendentals=0
        ),
        name="group_sum_code",
    )(*parts)


def bfloat16_terms(values):
    terms = []
    for _ in range(3):
        terms.append(values.astype(jnp.bfloat16))
        values = values - terms[-1].astype(jnp.float32)
    return terms


def finish_kernel(groups, sign_ref, *refs):
    out_ref, max_ref = refs[-2:]
    second = [
        add_all([ref[...] for ref in refs[half * groups : (half + 1) * groups]]) for half in range(HALVES)
    ]
    blocks = second[0].shape[1]
    natural = jnp.concatenate([part.T for part in second], axis=1)
    block = lax.broadcasted_iota(jnp.int32, (blocks, HALVES * blocks), 0)
    lane = lax.broadcasted_iota(jnp.int32, (blocks, HALVES * blocks), 1)
    largest = jnp.zeros((1, HALVES * blocks), jnp.float32)
    for half in range(HALVES):
        peak = jnp.max(jnp.abs(natural[:, half * QGROUP : (half + 1) * QGROUP]), axis=1, keepdims=True)
        chosen = jnp.where(lane == HALVES * block + half, peak, 0.0)
        largest = jnp.maximum(largest, jnp.max(chosen, axis=0, keepdims=True))
    max_ref[...] = largest * jnp.float32(ROT**-0.5)
    matrix = sylvester()
    high, middle, low = [
        jnp.dot(term, matrix, preferred_element_type=jnp.float32) for term in bfloat16_terms(natural)
    ]
    turned = (high + (middle + low)) * jnp.float32(1.0 / ROT)
    for half in range(HALVES):
        at = pl.ds(half, blocks, stride=HALVES)
        part = turned[:, half * QGROUP : (half + 1) * QGROUP]
        out_ref[at, :] = jnp.where(sign_ref[at, :] == 0, part, -part)


def finish(parts, signs):
    groups = len(parts[0])
    rows = signs.shape[0]
    return pl.pallas_call(
        functools.partial(finish_kernel, groups),
        out_shape=[
            jax.ShapeDtypeStruct((rows, LANES), jnp.float32),
            jax.ShapeDtypeStruct((1, rows), jnp.float32),
        ],
        compiler_params=pltpu.CompilerParams(vmem_limit_bytes=SUM_VMEM_LIMIT),
        name="sum_unrotate",
    )(signs, *[part for half in parts for part in half])


def shards(partials, signs):
    length = partials.shape[-1]
    members = lax.axis_size("local")
    groups = lax.axis_size("node")
    layout = Layout(length, members, groups)
    half = layout.half

    def swap(part, step):
        pairs = []
        for source in range(members):
            first, index = source // half * half, source % half
            pairs.append((source, first + partner(index, step, half)))
        return lax.ppermute(part, "local", pairs)

    def share(parts):
        moved = [parts[0]]
        for step in range(1, groups):
            pairs = [(source, partner(source, step, groups)) for source in range(groups)]
            moved.append(lax.ppermute(parts[step], "node", pairs))
        return moved

    direct, own_signs, *paired = rotate(partials.reshape(1, length), signs.reshape(length // LANES, LANES), layout)
    direct = lax.all_to_all(direct, "local", split_axis=0, concat_axis=0, tiled=True)
    paired = paired[:1] + [swap(paired[step], step) for step in range(1, half)]
    counterparts = [(member, (member + half) % members) for member in range(members)]
    across = lax.ppermute(far_sum(paired, layout), "local", counterparts)
    second_half = share(group_sum(direct_sum_kernel, layout, direct))
    first_half = share(group_sum(paired_sum_kernel, layout, across, *paired))
    reduced, rotated_max = finish([first_half, second_half], own_signs)
    return (reduced.reshape(-1), rotated_max.reshape(-1))


def solution(mesh):
    in_specs = (P("node", "local", None), P())
    out_specs = (P(("node", "local")), P(("node", "local")))
    return jax.shard_map(shards, mesh=mesh, in_specs=in_specs, out_specs=out_specs, check_vma=False)
```

```python
import functools
import jax
import jax.numpy as jnp
from jax import lax
from jax.experimental import pallas as pl
from jax.experimental.pallas import tpu as pltpu
from jax.sharding import PartitionSpec as P

ROT = 256
QGROUP = 128
HALVES = ROT // QGROUP
LANES = 128
VMEM_LIMIT = 50 * 1024 * 1024
SUM_VMEM_LIMIT = 24 * 1024 * 1024


def sylvester():
    row = lax.broadcasted_iota(jnp.int32, (ROT, ROT), 0)
    column = lax.broadcasted_iota(jnp.int32, (ROT, ROT), 1)
    parity = lax.population_count(row & column) & 1
    return (1 - 2 * parity).astype(jnp.float32).astype(jnp.bfloat16)


def partner(index, step, count):
    if count & (count - 1) == 0:
        return index ^ step
    return (index + step) % count


def leading_power(x):
    q = x * jnp.float32(2.0**23 + 1.0)
    return q - q * jnp.float32(1.0 - 2.0**-24)


def recode(values):
    magnitude = jnp.abs(values)
    largest = jnp.max(magnitude, axis=-2, keepdims=True)
    least = leading_power(jnp.clip(largest, 2.0**-30, 2.0**30)) * jnp.float32(2.0**-13)
    shift = leading_power(jnp.maximum(magnitude, least)) * jnp.float32(2.0**20)
    nearest = (magnitude + shift) - shift
    rest = magnitude - nearest
    coded = jnp.where(rest == shift * jnp.float32(2.0**-24), magnitude + rest, nearest)
    return jnp.where(values < 0.0, -coded, coded)


class Layout:
    def __init__(self, length, members, groups):
        self.members = members
        self.groups = groups
        self.half = members // 2
        self.portion = length // (members * groups)
        self.rows = self.portion // LANES
        self.blocks = self.portion // ROT
        self.together = 1
        if self.blocks < LANES and LANES % self.blocks == 0 and groups % (LANES // self.blocks) == 0:
            self.together = LANES // self.blocks
        self.units = groups // self.together
        self.columns = self.together * self.blocks

    def shape(self):
        return (self.units, QGROUP, self.columns)


def rotate_kernel(layout, other, values_ref, signs_ref, *refs):
    values, flips, turned, matrix, value_sems, sign_sems = refs[-6:]
    out_refs = refs[:-6]
    half, portion, rows = layout.half, layout.portion, layout.rows
    node = lax.axis_index("node")
    member = lax.axis_index("local")
    inner = lax.rem(member, half)
    first = half - (member - inner) if other else member - inner

    def fetches(unit, part):
        place = partner(node, unit * layout.together + part, layout.groups) * layout.members + first
        return (
            pltpu.make_async_copy(
                values_ref.at[:, pl.ds(pl.multiple_of(place * portion, portion), half * portion)],
                values.at[unit, part],
                value_sems.at[unit, part],
            ),
            pltpu.make_async_copy(
                signs_ref.at[pl.ds(pl.multiple_of(place * rows, rows), half * rows), :],
                flips.at[unit, part],
                sign_sems.at[unit, part],
            ),
        )

    for unit in range(layout.units):
        for part in range(layout.together):
            for copy in fetches(unit, part):
                copy.start()
    matrix[...] = sylvester()

    def body(unit, carry):
        for part in range(layout.together):
            for copy in fetches(unit, part):
                copy.wait()
        for step in range(half):
            owner = partner(inner, step, half)
            at = pl.ds(pl.multiple_of(owner * portion, portion), portion)
            at_rows = pl.ds(pl.multiple_of(owner * rows, rows), rows)
            for part in range(layout.together):
                wide = values[unit, part, :, at].astype(jnp.float32).reshape(rows, LANES)
                turned[step, part * rows : (part + 1) * rows] = jnp.where(
                    flips[unit, part, at_rows, :] == 0, wide, -wide
                )
            halves = [turned[step, pl.ds(part, layout.columns, stride=HALVES), :] for part in range(HALVES)]
            signed = jnp.concatenate(halves, axis=1).astype(jnp.bfloat16)
            rotated = lax.dot_general(
                matrix[...], signed, (((1,), (1,)), ((), ())), preferred_element_type=jnp.float32
            )
            for part in range(HALVES):
                rows_of = slice(part * QGROUP, (part + 1) * QGROUP)
                coded = recode(rotated[rows_of]).astype(jnp.bfloat16)
                if other:
                    out_refs[step * HALVES + part][unit] = coded
                else:
                    out_refs[step][unit, rows_of] = coded
        return carry

    lax.fori_loop(0, layout.units, body, 0)
    if not other:
        out_refs[-1][...] = flips[0, 0, pl.ds(pl.multiple_of(inner * rows, rows), rows), :]


def rotate(values, signs, layout, other):
    half, units, columns = layout.half, layout.units, layout.columns
    entries = half * layout.groups * layout.portion
    if other:
        outs = [jax.ShapeDtypeStruct(layout.shape(), jnp.bfloat16)] * (HALVES * half)
    else:
        outs = [jax.ShapeDtypeStruct((units, ROT, columns), jnp.bfloat16)] * half
        outs.append(jax.ShapeDtypeStruct((layout.rows, LANES), jnp.int32))
    return pl.pallas_call(
        functools.partial(rotate_kernel, layout, other),
        in_specs=[pl.BlockSpec(memory_space=pltpu.HBM)] * 2,
        out_shape=outs,
        scratch_shapes=[
            pltpu.VMEM((units, layout.together, 1, half * layout.portion), jnp.bfloat16),
            pltpu.VMEM((units, layout.together, half * layout.rows, LANES), jnp.int32),
            pltpu.VMEM((half, layout.together * layout.rows, LANES), jnp.float32),
            pltpu.VMEM((ROT, ROT), jnp.bfloat16),
            pltpu.SemaphoreType.DMA((units, layout.together)),
            pltpu.SemaphoreType.DMA((units, layout.together)),
        ],
        compiler_params=pltpu.CompilerParams(vmem_limit_bytes=VMEM_LIMIT),
        cost_estimate=pl.CostEstimate(flops=2 * entries * ROT, bytes_accessed=10 * entries, transcendentals=0),
        name="rotate_code",
    )(values, signs)


def add_all(arrays):
    total = arrays[0].astype(jnp.float32)
    for array in arrays[1:]:
        total = total + array.astype(jnp.float32)
    return total


def far_sum_kernel(*refs):
    refs[-1][...] = add_all([ref[...] for ref in refs[:-1]])


def far_sum(parts, layout):
    size = parts[0].size
    return pl.pallas_call(
        far_sum_kernel,
        out_shape=jax.ShapeDtypeStruct(layout.shape(), jnp.float32),
        compiler_params=pltpu.CompilerParams(vmem_limit_bytes=SUM_VMEM_LIMIT),
        cost_estimate=pl.CostEstimate(
            flops=2 * len(parts) * size, bytes_accessed=(2 * len(parts) + 4) * size, transcendentals=0
        ),
        name="far_sum",
    )(*parts)


def group_sum_kernel(layout, half, across_ref, *refs):
    near = [ref[:, half * QGROUP : (half + 1) * QGROUP] for ref in refs[: layout.half]]
    first = recode(add_all(near + [across_ref[...]])).astype(jnp.bfloat16)
    for section, out_ref in enumerate(refs[layout.half :]):
        at = section % layout.together * layout.blocks
        out_ref[...] = first[section // layout.together, :, at : at + layout.blocks]


def group_sum(near, across, layout, half):
    size = across.size
    return pl.pallas_call(
        functools.partial(group_sum_kernel, layout, half),
        out_shape=[jax.ShapeDtypeStruct((QGROUP, layout.blocks), jnp.bfloat16)] * layout.groups,
        compiler_params=pltpu.CompilerParams(vmem_limit_bytes=SUM_VMEM_LIMIT),
        cost_estimate=pl.CostEstimate(
            flops=30 * size, bytes_accessed=2 * (layout.half + 3) * size, transcendentals=0
        ),
        name="group_sum_code",
    )(across, *near)


def bfloat16_terms(values):
    terms = []
    for _ in range(3):
        terms.append(values.astype(jnp.bfloat16))
        values = values - terms[-1].astype(jnp.float32)
    return terms


def finish_kernel(groups, sign_ref, *refs):
    out_ref, max_ref = refs[-2:]
    second = [
        add_all([ref[...] for ref in refs[half * groups : (half + 1) * groups]]) for half in range(HALVES)
    ]
    blocks = second[0].shape[1]
    natural = jnp.concatenate([part.T for part in second], axis=1)
    block = lax.broadcasted_iota(jnp.int32, (blocks, HALVES * blocks), 0)
    lane = lax.broadcasted_iota(jnp.int32, (blocks, HALVES * blocks), 1)
    largest = jnp.zeros((1, HALVES * blocks), jnp.float32)
    for half in range(HALVES):
        peak = jnp.max(jnp.abs(natural[:, half * QGROUP : (half + 1) * QGROUP]), axis=1, keepdims=True)
        chosen = jnp.where(lane == HALVES * block + half, peak, 0.0)
        largest = jnp.maximum(largest, jnp.max(chosen, axis=0, keepdims=True))
    max_ref[...] = largest * jnp.float32(ROT**-0.5)
    matrix = sylvester()
    high, middle, low = [
        jnp.dot(term, matrix, preferred_element_type=jnp.float32) for term in bfloat16_terms(natural)
    ]
    turned = (high + (middle + low)) * jnp.float32(1.0 / ROT)
    for half in range(HALVES):
        at = pl.ds(half, blocks, stride=HALVES)
        part = turned[:, half * QGROUP : (half + 1) * QGROUP]
        out_ref[at, :] = jnp.where(sign_ref[at, :] == 0, part, -part)


def finish(parts, signs):
    groups = len(parts[0])
    rows = signs.shape[0]
    return pl.pallas_call(
        functools.partial(finish_kernel, groups),
        out_shape=[
            jax.ShapeDtypeStruct((rows, LANES), jnp.float32),
            jax.ShapeDtypeStruct((1, rows), jnp.float32),
        ],
        compiler_params=pltpu.CompilerParams(vmem_limit_bytes=SUM_VMEM_LIMIT),
        name="sum_unrotate",
    )(signs, *[part for half in parts for part in half])


def shards(partials, signs):
    length = partials.shape[-1]
    members = lax.axis_size("local")
    groups = lax.axis_size("node")
    layout = Layout(length, members, groups)
    half = layout.half

    def swap(part, step):
        pairs = []
        for source in range(members):
            first, index = source // half * half, source % half
            pairs.append((source, first + partner(index, step, half)))
        return lax.ppermute(part, "local", pairs)

    def share(parts):
        moved = [parts[0]]
        for step in range(1, groups):
            pairs = [(source, partner(source, step, groups)) for source in range(groups)]
            moved.append(lax.ppermute(parts[step], "node", pairs))
        return moved

    values, sign_rows = partials.reshape(1, length), signs.reshape(length // LANES, LANES)
    counterparts = [(member, (member + half) % members) for member in range(members)]
    far = rotate(values, sign_rows, layout, True)
    across = []
    for part in range(HALVES):
        parts = [far[part]] + [swap(far[HALVES * step + part], step) for step in range(1, half)]
        across.append(lax.ppermute(far_sum(parts, layout), "local", counterparts))
    *near, own_signs = rotate(values, sign_rows, layout, False)
    near = near[:1] + [swap(near[step], step) for step in range(1, half)]
    first_half, second_half = [share(group_sum(near, across[part], layout, part)) for part in range(HALVES)]
    reduced, rotated_max = finish([first_half, second_half], own_signs)
    return (reduced.reshape(-1), rotated_max.reshape(-1))


def solution(mesh):
    in_specs = (P("node", "local", None), P())
    out_specs = (P(("node", "local")), P(("node", "local")))
    return jax.shard_map(shards, mesh=mesh, in_specs=in_specs, out_specs=out_specs, check_vma=False)
```

```python
import functools
import jax
import jax.numpy as jnp
from jax import lax
from jax.experimental import pallas as pl
from jax.experimental.pallas import tpu as pltpu
from jax.sharding import PartitionSpec as P

ROT = 256
QGROUP = 128
HALVES = ROT // QGROUP
LANES = 128
VMEM_LIMIT = 50 * 1024 * 1024
SUM_VMEM_LIMIT = 24 * 1024 * 1024
AHEAD = 2


def sylvester():
    row = lax.broadcasted_iota(jnp.int32, (ROT, ROT), 0)
    column = lax.broadcasted_iota(jnp.int32, (ROT, ROT), 1)
    parity = lax.population_count(row & column) & 1
    return (1 - 2 * parity).astype(jnp.float32).astype(jnp.bfloat16)


def partner(index, step, count):
    if count & (count - 1) == 0:
        return index ^ step
    return (index + step) % count


def leading_power(x):
    q = x * jnp.float32(2.0**23 + 1.0)
    return q - q * jnp.float32(1.0 - 2.0**-24)


def recode(values):
    magnitude = jnp.abs(values)
    largest = jnp.max(magnitude, axis=-2, keepdims=True)
    least = leading_power(jnp.clip(largest, 2.0**-30, 2.0**30)) * jnp.float32(2.0**-13)
    shift = leading_power(jnp.maximum(magnitude, least)) * jnp.float32(2.0**20)
    nearest = (magnitude + shift) - shift
    rest = magnitude - nearest
    coded = jnp.where(rest == shift * jnp.float32(2.0**-24), magnitude + rest, nearest)
    return jnp.where(values < 0.0, -coded, coded)


class Layout:
    def __init__(self, length, members, groups):
        self.members = members
        self.groups = groups
        self.half = members // 2
        self.portion = length // (members * groups)
        self.rows = self.portion // LANES
        self.blocks = self.portion // ROT
        self.together = 1
        if self.blocks < LANES and LANES % self.blocks == 0 and groups % (LANES // self.blocks) == 0:
            self.together = LANES // self.blocks
        self.units = groups // self.together
        self.columns = self.together * self.blocks

    def shape(self):
        return (self.units, QGROUP, self.columns)

    def cuts(self, step, other):
        return HALVES if other and self.half > 1 and step == self.half // 2 else 1


def rotate_kernel(layout, other, values_ref, signs_ref, *refs):
    values, flips, turned, matrix, value_sems, sign_sems = refs[-6:]
    out_refs = list(refs[:-6])
    step_refs = [[out_refs.pop(0) for _ in range(layout.cuts(step, other))] for step in range(layout.half)]
    half, portion, rows = layout.half, layout.portion, layout.rows
    node = lax.axis_index("node")
    member = lax.axis_index("local")
    inner = lax.rem(member, half)
    first = half - (member - inner) if other else member - inner

    def fetches(unit, part):
        place = partner(node, unit * layout.together + part, layout.groups) * layout.members + first
        return (
            pltpu.make_async_copy(
                values_ref.at[:, pl.ds(pl.multiple_of(place * portion, portion), half * portion)],
                values.at[unit, part],
                value_sems.at[unit, part],
            ),
            pltpu.make_async_copy(
                signs_ref.at[pl.ds(pl.multiple_of(place * rows, rows), half * rows), :],
                flips.at[unit, part],
                sign_sems.at[unit, part],
            ),
        )

    def fetch(unit):
        for part in range(layout.together):
            for copy in fetches(unit, part):
                copy.start()

    for unit in range(min(AHEAD, layout.units)):
        fetch(unit)
    matrix[...] = sylvester()

    def body(unit, carry):
        for part in range(layout.together):
            for copy in fetches(unit, part):
                copy.wait()

        @pl.when(unit + AHEAD < layout.units)
        def _():
            fetch(unit + AHEAD)

        for step in range(half):
            owner = partner(inner, step, half)
            at = pl.ds(pl.multiple_of(owner * portion, portion), portion)
            at_rows = pl.ds(pl.multiple_of(owner * rows, rows), rows)
            for part in range(layout.together):
                wide = values[unit, part, :, at].astype(jnp.float32).reshape(rows, LANES)
                turned[step, part * rows : (part + 1) * rows] = jnp.where(
                    flips[unit, part, at_rows, :] == 0, wide, -wide
                )
            halves = [turned[step, pl.ds(part, layout.columns, stride=HALVES), :] for part in range(HALVES)]
            signed = jnp.concatenate(halves, axis=1).astype(jnp.bfloat16)
            rotated = lax.dot_general(
                matrix[...], signed, (((1,), (1,)), ((), ())), preferred_element_type=jnp.float32
            )
            for part in range(HALVES):
                rows_of = slice(part * QGROUP, (part + 1) * QGROUP)
                coded = recode(rotated[rows_of]).astype(jnp.bfloat16)
                if len(step_refs[step]) > 1:
                    step_refs[step][part][unit] = coded
                else:
                    step_refs[step][0][unit, rows_of] = coded
        return carry

    lax.fori_loop(0, layout.units, body, 0)
    if not other:
        out_refs[0][...] = flips[0, 0, pl.ds(pl.multiple_of(inner * rows, rows), rows), :]


def rotate(values, signs, layout, other):
    half, units, columns = layout.half, layout.units, layout.columns
    entries = half * layout.groups * layout.portion
    outs = []
    for step in range(half):
        cuts = layout.cuts(step, other)
        outs += [jax.ShapeDtypeStruct((units, ROT // cuts, columns), jnp.bfloat16)] * cuts
    if not other:
        outs.append(jax.ShapeDtypeStruct((layout.rows, LANES), jnp.int32))
    return pl.pallas_call(
        functools.partial(rotate_kernel, layout, other),
        in_specs=[pl.BlockSpec(memory_space=pltpu.HBM)] * 2,
        out_shape=outs,
        scratch_shapes=[
            pltpu.VMEM((units, layout.together, 1, half * layout.portion), jnp.bfloat16),
            pltpu.VMEM((units, layout.together, half * layout.rows, LANES), jnp.int32),
            pltpu.VMEM((half, layout.together * layout.rows, LANES), jnp.float32),
            pltpu.VMEM((ROT, ROT), jnp.bfloat16),
            pltpu.SemaphoreType.DMA((units, layout.together)),
            pltpu.SemaphoreType.DMA((units, layout.together)),
        ],
        compiler_params=pltpu.CompilerParams(vmem_limit_bytes=VMEM_LIMIT),
        cost_estimate=pl.CostEstimate(flops=2 * entries * ROT, bytes_accessed=10 * entries, transcendentals=0),
        name="rotate_code",
    )(values, signs)


def add_all(arrays):
    total = arrays[0].astype(jnp.float32)
    for array in arrays[1:]:
        total = total + array.astype(jnp.float32)
    return total


def far_sum_kernel(part, count, *refs):
    arrays = []
    for ref in refs[:count]:
        cut = ref.shape[1] == QGROUP
        arrays.append(ref[...] if cut else ref[:, part * QGROUP : (part + 1) * QGROUP])
    refs[-1][...] = add_all(arrays)


def far_sum(parts, layout, part, later):
    size = QGROUP * layout.units * layout.columns
    *later, total = pl.pallas_call(
        functools.partial(far_sum_kernel, part, len(parts)),
        in_specs=[pl.BlockSpec(memory_space=pltpu.VMEM)] * len(parts)
        + [pl.BlockSpec(memory_space=pl.ANY)] * len(later),
        out_specs=[pl.BlockSpec(memory_space=pl.ANY)] * len(later) + [pl.BlockSpec(memory_space=pltpu.VMEM)],
        out_shape=[jax.ShapeDtypeStruct(array.shape, array.dtype) for array in later]
        + [jax.ShapeDtypeStruct(layout.shape(), jnp.float32)],
        input_output_aliases={len(parts) + index: index for index in range(len(later))},
        compiler_params=pltpu.CompilerParams(vmem_limit_bytes=SUM_VMEM_LIMIT),
        cost_estimate=pl.CostEstimate(
            flops=2 * len(parts) * size, bytes_accessed=(2 * len(parts) + 4) * size, transcendentals=0
        ),
        name="far_sum",
    )(*parts, *later)
    return total, later


def group_sum_kernel(layout, *refs):
    across_refs, near_refs, out_refs = refs[:HALVES], refs[HALVES : HALVES + layout.half], refs[HALVES + layout.half :]
    for half, across_ref in enumerate(across_refs):
        near = [ref[:, half * QGROUP : (half + 1) * QGROUP] for ref in near_refs]
        first = recode(add_all(near + [across_ref[...]])).astype(jnp.bfloat16)
        for section, out_ref in enumerate(out_refs):
            at = section % layout.together * layout.blocks
            out_ref[half] = first[section // layout.together, :, at : at + layout.blocks]


def group_sum(near, across, layout):
    size = ROT * layout.units * layout.columns
    return pl.pallas_call(
        functools.partial(group_sum_kernel, layout),
        out_shape=[jax.ShapeDtypeStruct((HALVES, QGROUP, layout.blocks), jnp.bfloat16)] * layout.groups,
        compiler_params=pltpu.CompilerParams(vmem_limit_bytes=SUM_VMEM_LIMIT),
        cost_estimate=pl.CostEstimate(
            flops=30 * size, bytes_accessed=2 * (layout.half + 3) * size, transcendentals=0
        ),
        name="group_sum_code",
    )(*across, *near)


def bfloat16_terms(values):
    terms = []
    for _ in range(3):
        terms.append(values.astype(jnp.bfloat16))
        values = values - terms[-1].astype(jnp.float32)
    return terms


def finish_kernel(sign_ref, *refs):
    out_ref, max_ref = refs[-2:]
    second = [add_all([ref[half] for ref in refs[:-2]]) for half in range(HALVES)]
    blocks = second[0].shape[1]
    natural = jnp.concatenate([part.T for part in second], axis=1)
    block = lax.broadcasted_iota(jnp.int32, (blocks, HALVES * blocks), 0)
    lane = lax.broadcasted_iota(jnp.int32, (blocks, HALVES * blocks), 1)
    largest = jnp.zeros((1, HALVES * blocks), jnp.float32)
    for half in range(HALVES):
        peak = jnp.max(jnp.abs(natural[:, half * QGROUP : (half + 1) * QGROUP]), axis=1, keepdims=True)
        chosen = jnp.where(lane == HALVES * block + half, peak, 0.0)
        largest = jnp.maximum(largest, jnp.max(chosen, axis=0, keepdims=True))
    max_ref[...] = largest * jnp.float32(ROT**-0.5)
    matrix = sylvester()
    high, middle, low = [
        jnp.dot(term, matrix, preferred_element_type=jnp.float32) for term in bfloat16_terms(natural)
    ]
    turned = (high + (middle + low)) * jnp.float32(1.0 / ROT)
    for half in range(HALVES):
        at = pl.ds(half, blocks, stride=HALVES)
        part = turned[:, half * QGROUP : (half + 1) * QGROUP]
        out_ref[at, :] = jnp.where(sign_ref[at, :] == 0, part, -part)


def finish(parts, signs):
    rows = signs.shape[0]
    return pl.pallas_call(
        finish_kernel,
        out_shape=[
            jax.ShapeDtypeStruct((rows, LANES), jnp.float32),
            jax.ShapeDtypeStruct((1, rows), jnp.float32),
        ],
        compiler_params=pltpu.CompilerParams(vmem_limit_bytes=SUM_VMEM_LIMIT),
        name="sum_unrotate",
    )(signs, *parts)


def shards(partials, signs):
    length = partials.shape[-1]
    members = lax.axis_size("local")
    groups = lax.axis_size("node")
    layout = Layout(length, members, groups)
    half = layout.half

    def swap(part, step):
        pairs = []
        for source in range(members):
            first, index = source // half * half, source % half
            pairs.append((source, first + partner(index, step, half)))
        return lax.ppermute(part, "local", pairs)

    def share(parts):
        moved = [parts[0]]
        for step in range(1, groups):
            pairs = [(source, partner(source, step, groups)) for source in range(groups)]
            moved.append(lax.ppermute(parts[step], "node", pairs))
        return moved

    values, sign_rows = partials.reshape(1, length), signs.reshape(length // LANES, LANES)
    counterparts = [(member, (member + half) % members) for member in range(members)]
    steps = list(range(half - 1, 0, -1))
    outs = list(rotate(values, sign_rows, layout, True))
    far = [[outs.pop(0) for _ in range(layout.cuts(step, True))] for step in range(half)]
    last = []
    for step in steps:
        far[step][0] = swap(far[step][0], step)
        last += [step] if len(far[step]) > 1 else []
    for step in last:
        far[step][1] = swap(far[step][1], step)
    *near, own_signs = rotate(values, sign_rows, layout, False)
    across = []
    for part in range(HALVES):
        later = near[1:] if part == 0 else []
        total, later = far_sum([arrays[min(part, len(arrays) - 1)] for arrays in far], layout, part, later)
        across.append(lax.ppermute(total, "local", counterparts))
        if part == 0:
            near = near[:1] + later
    for step in steps:
        near[step] = swap(near[step], step)
    reduced, rotated_max = finish(share(group_sum(near, across, layout)), own_signs)
    return (reduced.reshape(-1), rotated_max.reshape(-1))


def solution(mesh):
    in_specs = (P("node", "local", None), P())
    out_specs = (P(("node", "local")), P(("node", "local")))
    return jax.shard_map(shards, mesh=mesh, in_specs=in_specs, out_specs=out_specs, check_vma=False)
```

```python
import functools
import jax
import jax.numpy as jnp
from jax import lax
from jax.experimental import pallas as pl
from jax.experimental.pallas import tpu as pltpu
from jax.sharding import PartitionSpec as P

ROT = 256
QGROUP = 128
HALVES = ROT // QGROUP
LANES = 128
VMEM_LIMIT = 50 * 1024 * 1024
SUM_VMEM_LIMIT = 24 * 1024 * 1024
AHEAD = 2


def sylvester():
    row = lax.broadcasted_iota(jnp.int32, (ROT, ROT), 0)
    column = lax.broadcasted_iota(jnp.int32, (ROT, ROT), 1)
    parity = lax.population_count(row & column) & 1
    return (1 - 2 * parity).astype(jnp.float32).astype(jnp.bfloat16)


def partner(index, step, count):
    if count & (count - 1) == 0:
        return index ^ step
    return (index + step) % count


def leading_power(x):
    q = x * jnp.float32(2.0**23 + 1.0)
    return q - q * jnp.float32(1.0 - 2.0**-24)


def recode(values):
    magnitude = jnp.abs(values)
    largest = jnp.max(magnitude, axis=-2, keepdims=True)
    least = leading_power(jnp.clip(largest, 2.0**-30, 2.0**30)) * jnp.float32(2.0**-13)
    shift = leading_power(jnp.maximum(magnitude, least)) * jnp.float32(2.0**20)
    nearest = (magnitude + shift) - shift
    rest = magnitude - nearest
    coded = jnp.where(rest == shift * jnp.float32(2.0**-24), magnitude + rest, nearest)
    return jnp.where(values < 0.0, -coded, coded)


class Layout:
    def __init__(self, length, members, groups):
        self.members = members
        self.groups = groups
        self.half = members // 2
        self.portion = length // (members * groups)
        self.rows = self.portion // LANES
        self.blocks = self.portion // ROT
        self.together = 1
        if self.blocks < LANES and LANES % self.blocks == 0 and groups % (LANES // self.blocks) == 0:
            self.together = LANES // self.blocks
        self.units = groups // self.together
        self.columns = self.together * self.blocks

    def span(self, steps):
        count = len(steps)
        aligned = steps[0] % count == 0 and steps == list(range(steps[0], steps[0] + count))
        return count if aligned and self.half & (self.half - 1) == 0 and count & (count - 1) == 0 else self.half


def rotate_kernel(layout, other, steps, after, values_ref, signs_ref, *refs):
    values, flips, turned, matrix, value_sems, sign_sems = refs[-6:]
    out_refs = refs[after:-6]
    half, portion, rows = layout.half, layout.portion, layout.rows
    node = lax.axis_index("node")
    member = lax.axis_index("local")
    inner = lax.rem(member, half)
    first = half - (member - inner) if other else member - inner
    span = layout.span(steps)
    lowest = partner(inner, steps[0], half) // span * span

    def fetches(unit, part):
        place = partner(node, unit * layout.together + part, layout.groups) * layout.members + first + lowest
        return (
            pltpu.make_async_copy(
                values_ref.at[:, pl.ds(pl.multiple_of(place * portion, portion), span * portion)],
                values.at[unit, part],
                value_sems.at[unit, part],
            ),
            pltpu.make_async_copy(
                signs_ref.at[pl.ds(pl.multiple_of(place * rows, rows), span * rows), :],
                flips.at[unit, part],
                sign_sems.at[unit, part],
            ),
        )

    def fetch(unit):
        for part in range(layout.together):
            for copy in fetches(unit, part):
                copy.start()

    for unit in range(min(AHEAD, layout.units)):
        fetch(unit)
    matrix[...] = sylvester()

    def body(unit, carry):
        for part in range(layout.together):
            for copy in fetches(unit, part):
                copy.wait()

        @pl.when(unit + AHEAD < layout.units)
        def _():
            fetch(unit + AHEAD)

        for index, step in enumerate(steps):
            owner = partner(inner, step, half) - lowest
            at = pl.ds(pl.multiple_of(owner * portion, portion), portion)
            at_rows = pl.ds(pl.multiple_of(owner * rows, rows), rows)
            for part in range(layout.together):
                wide = values[unit, part, :, at].astype(jnp.float32).reshape(rows, LANES)
                turned[index, part * rows : (part + 1) * rows] = jnp.where(
                    flips[unit, part, at_rows, :] == 0, wide, -wide
                )
            halves = [turned[index, pl.ds(part, layout.columns, stride=HALVES), :] for part in range(HALVES)]
            signed = jnp.concatenate(halves, axis=1).astype(jnp.bfloat16)
            rotated = lax.dot_general(
                matrix[...], signed, (((1,), (1,)), ((), ())), preferred_element_type=jnp.float32
            )
            for part in range(HALVES):
                rows_of = slice(part * QGROUP, (part + 1) * QGROUP)
                out_refs[index][unit, rows_of] = recode(rotated[rows_of]).astype(jnp.bfloat16)
        return carry

    lax.fori_loop(0, layout.units, body, 0)
    if not other:
        out_refs[-1][...] = flips[0, 0, pl.ds(pl.multiple_of((inner - lowest) * rows, rows), rows), :]


def rotate(values, signs, layout, other, steps, after=()):
    units = layout.units
    entries = len(steps) * layout.groups * layout.portion
    outs = [jax.ShapeDtypeStruct((units, ROT, layout.columns), jnp.bfloat16)] * len(steps)
    if not other:
        outs.append(jax.ShapeDtypeStruct((layout.rows, LANES), jnp.int32))
    return list(
        pl.pallas_call(
            functools.partial(rotate_kernel, layout, other, steps, len(after)),
            in_specs=[pl.BlockSpec(memory_space=pltpu.HBM)] * 2 + [pl.BlockSpec(memory_space=pl.ANY)] * len(after),
            out_shape=outs,
            scratch_shapes=[
                pltpu.VMEM((units, layout.together, 1, layout.span(steps) * layout.portion), jnp.bfloat16),
                pltpu.VMEM((units, layout.together, layout.span(steps) * layout.rows, LANES), jnp.int32),
                pltpu.VMEM((len(steps), layout.together * layout.rows, LANES), jnp.float32),
                pltpu.VMEM((ROT, ROT), jnp.bfloat16),
                pltpu.SemaphoreType.DMA((units, layout.together)),
                pltpu.SemaphoreType.DMA((units, layout.together)),
            ],
            compiler_params=pltpu.CompilerParams(vmem_limit_bytes=VMEM_LIMIT),
            cost_estimate=pl.CostEstimate(flops=2 * entries * ROT, bytes_accessed=10 * entries, transcendentals=0),
            name="rotate_code",
        )(values, signs, *after)
    )


def add_all(arrays):
    total = arrays[0].astype(jnp.float32)
    for array in arrays[1:]:
        total = total + array.astype(jnp.float32)
    return total


def far_sum_kernel(count, *refs):
    refs[-1][...] = add_all([ref[...] for ref in refs[:count]])


def far_sum(parts, later):
    size = parts[0].size
    *later, total = pl.pallas_call(
        functools.partial(far_sum_kernel, len(parts)),
        in_specs=[pl.BlockSpec(memory_space=pltpu.VMEM)] * len(parts)
        + [pl.BlockSpec(memory_space=pl.ANY)] * len(later),
        out_specs=[pl.BlockSpec(memory_space=pl.ANY)] * len(later) + [pl.BlockSpec(memory_space=pltpu.VMEM)],
        out_shape=[jax.ShapeDtypeStruct(array.shape, array.dtype) for array in later]
        + [jax.ShapeDtypeStruct(parts[0].shape, jnp.float32)],
        input_output_aliases={len(parts) + index: index for index in range(len(later))},
        compiler_params=pltpu.CompilerParams(vmem_limit_bytes=SUM_VMEM_LIMIT),
        cost_estimate=pl.CostEstimate(
            flops=2 * len(parts) * size, bytes_accessed=(2 * len(parts) + 4) * size, transcendentals=0
        ),
        name="far_sum",
    )(*parts, *later)
    return total, later


def group_sum_kernel(layout, across_ref, *refs):
    near_refs, out_refs = refs[: layout.half], refs[layout.half :]
    for half in range(HALVES):
        at_rows = slice(half * QGROUP, (half + 1) * QGROUP)
        first = recode(add_all([ref[:, at_rows] for ref in (*near_refs, across_ref)])).astype(jnp.bfloat16)
        for section, out_ref in enumerate(out_refs):
            at = section % layout.together * layout.blocks
            out_ref[half] = first[section // layout.together, :, at : at + layout.blocks]


def group_sum(near, across, layout):
    size = across.size
    return pl.pallas_call(
        functools.partial(group_sum_kernel, layout),
        out_shape=[jax.ShapeDtypeStruct((HALVES, QGROUP, layout.blocks), jnp.bfloat16)] * layout.groups,
        compiler_params=pltpu.CompilerParams(vmem_limit_bytes=SUM_VMEM_LIMIT),
        cost_estimate=pl.CostEstimate(
            flops=30 * size, bytes_accessed=2 * (layout.half + 3) * size, transcendentals=0
        ),
        name="group_sum_code",
    )(across, *near)


def bfloat16_terms(values):
    terms = []
    for _ in range(3):
        terms.append(values.astype(jnp.bfloat16))
        values = values - terms[-1].astype(jnp.float32)
    return terms


def finish_kernel(sign_ref, *refs):
    out_ref, max_ref = refs[-2:]
    second = [add_all([ref[half] for ref in refs[:-2]]) for half in range(HALVES)]
    blocks = second[0].shape[1]
    natural = jnp.concatenate([part.T for part in second], axis=1)
    block = lax.broadcasted_iota(jnp.int32, (blocks, HALVES * blocks), 0)
    lane = lax.broadcasted_iota(jnp.int32, (blocks, HALVES * blocks), 1)
    largest = jnp.zeros((1, HALVES * blocks), jnp.float32)
    for half in range(HALVES):
        peak = jnp.max(jnp.abs(natural[:, half * QGROUP : (half + 1) * QGROUP]), axis=1, keepdims=True)
        chosen = jnp.where(lane == HALVES * block + half, peak, 0.0)
        largest = jnp.maximum(largest, jnp.max(chosen, axis=0, keepdims=True))
    max_ref[...] = largest * jnp.float32(ROT**-0.5)
    matrix = sylvester()
    high, middle, low = [
        jnp.dot(term, matrix, preferred_element_type=jnp.float32) for term in bfloat16_terms(natural)
    ]
    turned = (high + (middle + low)) * jnp.float32(1.0 / ROT)
    for half in range(HALVES):
        at = pl.ds(half, blocks, stride=HALVES)
        part = turned[:, half * QGROUP : (half + 1) * QGROUP]
        out_ref[at, :] = jnp.where(sign_ref[at, :] == 0, part, -part)


def finish(parts, signs):
    rows = signs.shape[0]
    return pl.pallas_call(
        finish_kernel,
        out_shape=[
            jax.ShapeDtypeStruct((rows, LANES), jnp.float32),
            jax.ShapeDtypeStruct((1, rows), jnp.float32),
        ],
        compiler_params=pltpu.CompilerParams(vmem_limit_bytes=SUM_VMEM_LIMIT),
        name="sum_unrotate",
    )(signs, *parts)


def shards(partials, signs):
    length = partials.shape[-1]
    members = lax.axis_size("local")
    groups = lax.axis_size("node")
    layout = Layout(length, members, groups)
    half = layout.half

    def swap(part, step):
        pairs = []
        for source in range(members):
            first, index = source // half * half, source % half
            pairs.append((source, first + partner(index, step, half)))
        return lax.ppermute(part, "local", pairs)

    def share(parts):
        moved = [parts[0]]
        for step in range(1, groups):
            pairs = [(source, partner(source, step, groups)) for source in range(groups)]
            moved.append(lax.ppermute(parts[step], "node", pairs))
        return moved

    values, sign_rows = partials.reshape(1, length), signs.reshape(length // LANES, LANES)
    counterparts = [(member, (member + half) % members) for member in range(members)]
    slow = list(range(half // 2, half))
    fast = list(range(half // 2))
    far_slow = rotate(values, sign_rows, layout, True, slow)
    far_fast = rotate(values, sign_rows, layout, True, fast, far_slow[:1])
    far = [swap(part, step) for step, part in zip(slow, far_slow)]
    far += [swap(part, step) if step else part for step, part in zip(fast, far_fast)]
    *near, own_signs = rotate(values, sign_rows, layout, False, fast + slow, far_fast[:1])
    total, near[1:-1] = far_sum(far, near[1:-1])
    across = lax.ppermute(total, "local", counterparts)
    near = [swap(part, step) if step else part for step, part in zip(fast + slow, near)]
    reduced, rotated_max = finish(share(group_sum(near, across, layout)), own_signs)
    return (reduced.reshape(-1), rotated_max.reshape(-1))


def solution(mesh):
    in_specs = (P("node", "local", None), P())
    out_specs = (P(("node", "local")), P(("node", "local")))
    return jax.shard_map(shards, mesh=mesh, in_specs=in_specs, out_specs=out_specs, check_vma=False)
```

```python
import functools
import jax
import jax.numpy as jnp
from jax import lax
from jax.experimental import pallas as pl
from jax.experimental.pallas import tpu as pltpu
from jax.sharding import PartitionSpec as P

ROT = 256
QGROUP = 128
HALVES = ROT // QGROUP
LANES = 128
VMEM_LIMIT = 50 * 1024 * 1024
SUM_VMEM_LIMIT = 24 * 1024 * 1024
AHEAD = 2


def sylvester():
    row = lax.broadcasted_iota(jnp.int32, (ROT, ROT), 0)
    column = lax.broadcasted_iota(jnp.int32, (ROT, ROT), 1)
    parity = lax.population_count(row & column) & 1
    return (1 - 2 * parity).astype(jnp.float32).astype(jnp.bfloat16)


def partner(index, step, count):
    if count & (count - 1) == 0:
        return index ^ step
    return (index + step) % count


def leading_power(x):
    q = x * jnp.float32(2.0**23 + 1.0)
    return q - q * jnp.float32(1.0 - 2.0**-24)


def recode(values):
    magnitude = jnp.abs(values)
    largest = jnp.max(magnitude, axis=-2, keepdims=True)
    least = leading_power(jnp.clip(largest, 2.0**-30, 2.0**30)) * jnp.float32(2.0**-13)
    shift = leading_power(jnp.maximum(magnitude, least)) * jnp.float32(2.0**20)
    nearest = (magnitude + shift) - shift
    rest = magnitude - nearest
    coded = jnp.where(rest == shift * jnp.float32(2.0**-24), magnitude + rest, nearest)
    return jnp.where(values < 0.0, -coded, coded)


class Layout:
    def __init__(self, length, members, groups):
        self.members = members
        self.groups = groups
        self.half = members // 2
        self.portion = length // (members * groups)
        self.rows = self.portion // LANES
        self.blocks = self.portion // ROT
        self.together = 1
        if self.blocks < LANES and LANES % self.blocks == 0 and groups % (LANES // self.blocks) == 0:
            self.together = LANES // self.blocks
        self.units = groups // self.together
        self.columns = self.together * self.blocks

    def shape(self):
        return (self.units, QGROUP, self.columns)


def rotate_kernel(layout, other, later, values_ref, signs_ref, *refs):
    values, flips, turned, matrix, value_sems, sign_sems = refs[-6:]
    out_refs = refs[2 * later : -6]
    half, portion, rows = layout.half, layout.portion, layout.rows
    node = lax.axis_index("node")
    member = lax.axis_index("local")
    inner = lax.rem(member, half)
    first = half - (member - inner) if other else member - inner

    def fetches(unit, part):
        place = partner(node, unit * layout.together + part, layout.groups) * layout.members + first
        return (
            pltpu.make_async_copy(
                values_ref.at[:, pl.ds(pl.multiple_of(place * portion, portion), half * portion)],
                values.at[unit, part],
                value_sems.at[unit, part],
            ),
            pltpu.make_async_copy(
                signs_ref.at[pl.ds(pl.multiple_of(place * rows, rows), half * rows), :],
                flips.at[unit, part],
                sign_sems.at[unit, part],
            ),
        )

    def fetch(unit):
        for part in range(layout.together):
            for copy in fetches(unit, part):
                copy.start()

    for unit in range(min(AHEAD, layout.units)):
        fetch(unit)
    matrix[...] = sylvester()

    def body(unit, carry):
        for part in range(layout.together):
            for copy in fetches(unit, part):
                copy.wait()

        @pl.when(unit + AHEAD < layout.units)
        def _():
            fetch(unit + AHEAD)

        for step in range(half):
            owner = partner(inner, step, half)
            at = pl.ds(pl.multiple_of(owner * portion, portion), portion)
            at_rows = pl.ds(pl.multiple_of(owner * rows, rows), rows)
            for part in range(layout.together):
                wide = values[unit, part, :, at].astype(jnp.float32).reshape(rows, LANES)
                turned[step, part * rows : (part + 1) * rows] = jnp.where(
                    flips[unit, part, at_rows, :] == 0, wide, -wide
                )
            halves = [turned[step, pl.ds(part, layout.columns, stride=HALVES), :] for part in range(HALVES)]
            signed = jnp.concatenate(halves, axis=1).astype(jnp.bfloat16)
            rotated = lax.dot_general(
                matrix[...], signed, (((1,), (1,)), ((), ())), preferred_element_type=jnp.float32
            )
            for part in range(HALVES):
                rows_of = slice(part * QGROUP, (part + 1) * QGROUP)
                coded = recode(rotated[rows_of]).astype(jnp.bfloat16)
                if other:
                    out_refs[step * HALVES + part][unit] = coded
                else:
                    out_refs[step][unit, rows_of] = coded
        return carry

    lax.fori_loop(0, layout.units, body, 0)
    if not other:
        out_refs[-1][...] = flips[0, 0, pl.ds(pl.multiple_of(inner * rows, rows), rows), :]


def rotate(values, signs, layout, other, later=()):
    half, units, columns = layout.half, layout.units, layout.columns
    entries = half * layout.groups * layout.portion
    outs = [jax.ShapeDtypeStruct(array.shape, array.dtype) for array in later]
    if other:
        outs += [jax.ShapeDtypeStruct(layout.shape(), jnp.bfloat16)] * (HALVES * half)
    else:
        outs += [jax.ShapeDtypeStruct((units, ROT, columns), jnp.bfloat16)] * half
        outs.append(jax.ShapeDtypeStruct((layout.rows, LANES), jnp.int32))
    own = len(outs) - len(later)
    return list(
        pl.pallas_call(
            functools.partial(rotate_kernel, layout, other, len(later)),
            in_specs=[pl.BlockSpec(memory_space=pltpu.HBM)] * 2 + [pl.BlockSpec(memory_space=pl.ANY)] * len(later),
            out_specs=[pl.BlockSpec(memory_space=pl.ANY)] * len(later)
            + [pl.BlockSpec(memory_space=pltpu.VMEM)] * own,
            out_shape=outs,
            input_output_aliases={2 + index: index for index in range(len(later))},
            scratch_shapes=[
                pltpu.VMEM((units, layout.together, 1, half * layout.portion), jnp.bfloat16),
                pltpu.VMEM((units, layout.together, half * layout.rows, LANES), jnp.int32),
                pltpu.VMEM((half, layout.together * layout.rows, LANES), jnp.float32),
                pltpu.VMEM((ROT, ROT), jnp.bfloat16),
                pltpu.SemaphoreType.DMA((units, layout.together)),
                pltpu.SemaphoreType.DMA((units, layout.together)),
            ],
            compiler_params=pltpu.CompilerParams(vmem_limit_bytes=VMEM_LIMIT),
            cost_estimate=pl.CostEstimate(flops=2 * entries * ROT, bytes_accessed=10 * entries, transcendentals=0),
            name="rotate_code",
        )(values, signs, *later)
    )


def add_all(arrays):
    total = arrays[0].astype(jnp.float32)
    for array in arrays[1:]:
        total = total + array.astype(jnp.float32)
    return total


def far_sum_kernel(count, *refs):
    refs[-1][...] = add_all([ref[...] for ref in refs[:count]])


def far_sum(parts, later):
    size = parts[0].size
    *later, total = pl.pallas_call(
        functools.partial(far_sum_kernel, len(parts)),
        in_specs=[pl.BlockSpec(memory_space=pltpu.VMEM)] * len(parts)
        + [pl.BlockSpec(memory_space=pl.ANY)] * len(later),
        out_specs=[pl.BlockSpec(memory_space=pl.ANY)] * len(later) + [pl.BlockSpec(memory_space=pltpu.VMEM)],
        out_shape=[jax.ShapeDtypeStruct(array.shape, array.dtype) for array in later]
        + [jax.ShapeDtypeStruct(parts[0].shape, jnp.float32)],
        input_output_aliases={len(parts) + index: index for index in range(len(later))},
        compiler_params=pltpu.CompilerParams(vmem_limit_bytes=SUM_VMEM_LIMIT),
        cost_estimate=pl.CostEstimate(
            flops=2 * len(parts) * size, bytes_accessed=(2 * len(parts) + 4) * size, transcendentals=0
        ),
        name="far_sum",
    )(*parts, *later)
    return total, later


def group_sum_kernel(layout, *refs):
    across_refs, near_refs, out_refs = refs[:HALVES], refs[HALVES : HALVES + layout.half], refs[HALVES + layout.half :]
    for half, across_ref in enumerate(across_refs):
        near = [ref[:, half * QGROUP : (half + 1) * QGROUP] for ref in near_refs]
        first = recode(add_all(near + [across_ref[...]])).astype(jnp.bfloat16)
        for section, out_ref in enumerate(out_refs):
            at = section % layout.together * layout.blocks
            out_ref[half] = first[section // layout.together, :, at : at + layout.blocks]


def group_sum(near, across, layout):
    size = near[0].size
    return pl.pallas_call(
        functools.partial(group_sum_kernel, layout),
        out_shape=[jax.ShapeDtypeStruct((HALVES, QGROUP, layout.blocks), jnp.bfloat16)] * layout.groups,
        compiler_params=pltpu.CompilerParams(vmem_limit_bytes=SUM_VMEM_LIMIT),
        cost_estimate=pl.CostEstimate(
            flops=30 * size, bytes_accessed=2 * (layout.half + 3) * size, transcendentals=0
        ),
        name="group_sum_code",
    )(*across, *near)


def bfloat16_terms(values):
    terms = []
    for _ in range(3):
        terms.append(values.astype(jnp.bfloat16))
        values = values - terms[-1].astype(jnp.float32)
    return terms


def finish_kernel(sign_ref, *refs):
    out_ref, max_ref = refs[-2:]
    second = [add_all([ref[half] for ref in refs[:-2]]) for half in range(HALVES)]
    blocks = second[0].shape[1]
    natural = jnp.concatenate([part.T for part in second], axis=1)
    block = lax.broadcasted_iota(jnp.int32, (blocks, HALVES * blocks), 0)
    lane = lax.broadcasted_iota(jnp.int32, (blocks, HALVES * blocks), 1)
    largest = jnp.zeros((1, HALVES * blocks), jnp.float32)
    for half in range(HALVES):
        peak = jnp.max(jnp.abs(natural[:, half * QGROUP : (half + 1) * QGROUP]), axis=1, keepdims=True)
        chosen = jnp.where(lane == HALVES * block + half, peak, 0.0)
        largest = jnp.maximum(largest, jnp.max(chosen, axis=0, keepdims=True))
    max_ref[...] = largest * jnp.float32(ROT**-0.5)
    matrix = sylvester()
    high, middle, low = [
        jnp.dot(term, matrix, preferred_element_type=jnp.float32) for term in bfloat16_terms(natural)
    ]
    turned = (high + (middle + low)) * jnp.float32(1.0 / ROT)
    for half in range(HALVES):
        at = pl.ds(half, blocks, stride=HALVES)
        part = turned[:, half * QGROUP : (half + 1) * QGROUP]
        out_ref[at, :] = jnp.where(sign_ref[at, :] == 0, part, -part)


def finish(parts, signs):
    rows = signs.shape[0]
    return pl.pallas_call(
        finish_kernel,
        out_shape=[
            jax.ShapeDtypeStruct((rows, LANES), jnp.float32),
            jax.ShapeDtypeStruct((1, rows), jnp.float32),
        ],
        compiler_params=pltpu.CompilerParams(vmem_limit_bytes=SUM_VMEM_LIMIT),
        name="sum_unrotate",
    )(signs, *parts)


def shards(partials, signs):
    length = partials.shape[-1]
    members = lax.axis_size("local")
    groups = lax.axis_size("node")
    layout = Layout(length, members, groups)
    half = layout.half

    def swap(part, step):
        pairs = []
        for source in range(members):
            first, index = source // half * half, source % half
            pairs.append((source, first + partner(index, step, half)))
        return lax.ppermute(part, "local", pairs)

    def share(parts):
        moved = [parts[0]]
        for step in range(1, groups):
            pairs = [(source, partner(source, step, groups)) for source in range(groups)]
            moved.append(lax.ppermute(parts[step], "node", pairs))
        return moved

    values, sign_rows = partials.reshape(1, length), signs.reshape(length // LANES, LANES)
    counterparts = [(member, (member + half) % members) for member in range(members)]
    fast, slow = list(range(1, half // 2)), list(range(half // 2, half))
    outs = rotate(values, sign_rows, layout, True)
    far = [[outs[HALVES * step + part] for step in range(half)] for part in range(HALVES)]
    for step in slow + fast:
        far[0][step] = swap(far[0][step], step)
    for step in slow[:1]:
        far[1][step] = swap(far[1][step], step)
    outs = rotate(values, sign_rows, layout, False, [far[1][step] for step in slow[1:] + fast])
    for step in slow[1:] + fast:
        far[1][step] = outs.pop(0)
    *near, own_signs = outs
    for step in slow[1:]:
        far[1][step] = swap(far[1][step], step)
    first, later = far_sum(far[0], [far[1][step] for step in fast] + near[1:])
    across = [lax.ppermute(first, "local", counterparts)]
    for step in fast:
        far[1][step] = swap(later.pop(0), step)
    near[1:] = later
    for step in slow[1:]:
        near[step] = swap(near[step], step)
    second, later = far_sum(far[1], [near[step] for step in fast + slow[:1]])
    across.append(lax.ppermute(second, "local", counterparts))
    for step, part in zip(fast + slow[:1], later):
        near[step] = swap(part, step)
    reduced, rotated_max = finish(share(group_sum(near, across, layout)), own_signs)
    return (reduced.reshape(-1), rotated_max.reshape(-1))


def solution(mesh):
    in_specs = (P("node", "local", None), P())
    out_specs = (P(("node", "local")), P(("node", "local")))
    return jax.shard_map(shards, mesh=mesh, in_specs=in_specs, out_specs=out_specs, check_vma=False)
```

```python
import functools
import jax
import jax.numpy as jnp
from jax import lax
from jax.experimental import pallas as pl
from jax.experimental.pallas import tpu as pltpu
from jax.sharding import PartitionSpec as P

ROT = 256
QGROUP = 128
HALVES = ROT // QGROUP
LANES = 128
VMEM_LIMIT = 50 * 1024 * 1024
SUM_VMEM_LIMIT = 24 * 1024 * 1024
AHEAD = 2


def sylvester():
    row = lax.broadcasted_iota(jnp.int32, (ROT, ROT), 0)
    column = lax.broadcasted_iota(jnp.int32, (ROT, ROT), 1)
    parity = lax.population_count(row & column) & 1
    return (1 - 2 * parity).astype(jnp.float32).astype(jnp.bfloat16)


def partner(index, step, count):
    if count & (count - 1) == 0:
        return index ^ step
    return (index + step) % count


def leading_power(x):
    q = x * jnp.float32(2.0**23 + 1.0)
    return q - q * jnp.float32(1.0 - 2.0**-24)


def recode(values):
    magnitude = jnp.abs(values)
    largest = jnp.max(magnitude, axis=-2, keepdims=True)
    least = leading_power(jnp.clip(largest, 2.0**-30, 2.0**30)) * jnp.float32(2.0**-13)
    shift = leading_power(jnp.maximum(magnitude, least)) * jnp.float32(2.0**20)
    nearest = (magnitude + shift) - shift
    rest = magnitude - nearest
    coded = jnp.where(rest == shift * jnp.float32(2.0**-24), magnitude + rest, nearest)
    return jnp.where(values < 0.0, -coded, coded)


class Layout:
    def __init__(self, length, members, groups):
        self.members = members
        self.groups = groups
        self.half = members // 2
        self.portion = length // (members * groups)
        self.rows = self.portion // LANES
        self.blocks = self.portion // ROT
        self.together = 1
        if self.blocks < LANES and LANES % self.blocks == 0 and groups % (LANES // self.blocks) == 0:
            self.together = LANES // self.blocks
        self.units = groups // self.together
        self.columns = self.together * self.blocks

    def shape(self):
        return (self.units, QGROUP, self.columns)


def rotate_kernel(layout, other, later, values_ref, signs_ref, *refs):
    values, flips, turned, matrix, value_sems, sign_sems = refs[-6:]
    out_refs = refs[2 * later : -6]
    half, portion, rows = layout.half, layout.portion, layout.rows
    node = lax.axis_index("node")
    member = lax.axis_index("local")
    inner = lax.rem(member, half)
    first = half - (member - inner) if other else member - inner

    def fetches(unit, part):
        place = partner(node, unit * layout.together + part, layout.groups) * layout.members + first
        return (
            pltpu.make_async_copy(
                values_ref.at[:, pl.ds(pl.multiple_of(place * portion, portion), half * portion)],
                values.at[unit, part],
                value_sems.at[unit, part],
            ),
            pltpu.make_async_copy(
                signs_ref.at[pl.ds(pl.multiple_of(place * rows, rows), half * rows), :],
                flips.at[unit, part],
                sign_sems.at[unit, part],
            ),
        )

    def fetch(unit):
        for part in range(layout.together):
            for copy in fetches(unit, part):
                copy.start()

    for unit in range(min(AHEAD, layout.units)):
        fetch(unit)
    matrix[...] = sylvester()

    def body(unit, carry):
        for part in range(layout.together):
            for copy in fetches(unit, part):
                copy.wait()

        @pl.when(unit + AHEAD < layout.units)
        def _():
            fetch(unit + AHEAD)

        for step in range(half):
            owner = partner(inner, step, half)
            at = pl.ds(pl.multiple_of(owner * portion, portion), portion)
            at_rows = pl.ds(pl.multiple_of(owner * rows, rows), rows)
            for part in range(layout.together):
                wide = values[unit, part, :, at].astype(jnp.float32).reshape(rows, LANES)
                turned[step, part * rows : (part + 1) * rows] = jnp.where(
                    flips[unit, part, at_rows, :] == 0, wide, -wide
                )
            halves = [turned[step, pl.ds(part, layout.columns, stride=HALVES), :] for part in range(HALVES)]
            signed = jnp.concatenate(halves, axis=1).astype(jnp.bfloat16)
            rotated = lax.dot_general(
                matrix[...], signed, (((1,), (1,)), ((), ())), preferred_element_type=jnp.float32
            )
            for part in range(HALVES):
                rows_of = slice(part * QGROUP, (part + 1) * QGROUP)
                coded = recode(rotated[rows_of]).astype(jnp.bfloat16)
                if other:
                    out_refs[step * HALVES + part][unit] = coded
                else:
                    out_refs[step][unit, rows_of] = coded
        return carry

    lax.fori_loop(0, layout.units, body, 0)
    if not other:
        out_refs[-1][...] = flips[0, 0, pl.ds(pl.multiple_of(inner * rows, rows), rows), :]


def rotate(values, signs, layout, other, later=()):
    half, units, columns = layout.half, layout.units, layout.columns
    entries = half * layout.groups * layout.portion
    outs = [jax.ShapeDtypeStruct(array.shape, array.dtype) for array in later]
    if other:
        outs += [jax.ShapeDtypeStruct(layout.shape(), jnp.bfloat16)] * (HALVES * half)
    else:
        outs += [jax.ShapeDtypeStruct((units, ROT, columns), jnp.bfloat16)] * half
        outs.append(jax.ShapeDtypeStruct((layout.rows, LANES), jnp.int32))
    own = len(outs) - len(later)
    return list(
        pl.pallas_call(
            functools.partial(rotate_kernel, layout, other, len(later)),
            in_specs=[pl.BlockSpec(memory_space=pltpu.HBM)] * 2 + [pl.BlockSpec(memory_space=pl.ANY)] * len(later),
            out_specs=[pl.BlockSpec(memory_space=pl.ANY)] * len(later)
            + [pl.BlockSpec(memory_space=pltpu.VMEM)] * own,
            out_shape=outs,
            input_output_aliases={2 + index: index for index in range(len(later))},
            scratch_shapes=[
                pltpu.VMEM((units, layout.together, 1, half * layout.portion), jnp.bfloat16),
                pltpu.VMEM((units, layout.together, half * layout.rows, LANES), jnp.int32),
                pltpu.VMEM((half, layout.together * layout.rows, LANES), jnp.float32),
                pltpu.VMEM((ROT, ROT), jnp.bfloat16),
                pltpu.SemaphoreType.DMA((units, layout.together)),
                pltpu.SemaphoreType.DMA((units, layout.together)),
            ],
            compiler_params=pltpu.CompilerParams(vmem_limit_bytes=VMEM_LIMIT),
            cost_estimate=pl.CostEstimate(flops=2 * entries * ROT, bytes_accessed=10 * entries, transcendentals=0),
            name="rotate_code",
        )(values, signs, *later)
    )


def add_all(arrays):
    total = arrays[0].astype(jnp.float32)
    for array in arrays[1:]:
        total = total + array.astype(jnp.float32)
    return total


def far_sum_kernel(count, *refs):
    refs[-1][...] = add_all([ref[...] for ref in refs[:count]])


def far_sum(parts, later):
    size = parts[0].size
    *later, total = pl.pallas_call(
        functools.partial(far_sum_kernel, len(parts)),
        in_specs=[pl.BlockSpec(memory_space=pltpu.VMEM)] * len(parts)
        + [pl.BlockSpec(memory_space=pl.ANY)] * len(later),
        out_specs=[pl.BlockSpec(memory_space=pl.ANY)] * len(later) + [pl.BlockSpec(memory_space=pltpu.VMEM)],
        out_shape=[jax.ShapeDtypeStruct(array.shape, array.dtype) for array in later]
        + [jax.ShapeDtypeStruct(parts[0].shape, jnp.float32)],
        input_output_aliases={len(parts) + index: index for index in range(len(later))},
        compiler_params=pltpu.CompilerParams(vmem_limit_bytes=SUM_VMEM_LIMIT),
        cost_estimate=pl.CostEstimate(
            flops=2 * len(parts) * size, bytes_accessed=(2 * len(parts) + 4) * size, transcendentals=0
        ),
        name="far_sum",
    )(*parts, *later)
    return total, later


def group_sum_kernel(layout, *refs):
    across_refs, near_refs, out_refs = refs[:HALVES], refs[HALVES : HALVES + layout.half], refs[HALVES + layout.half :]
    for half, across_ref in enumerate(across_refs):
        near = [ref[:, half * QGROUP : (half + 1) * QGROUP] for ref in near_refs]
        first = recode(add_all(near + [across_ref[...]])).astype(jnp.bfloat16)
        for section, out_ref in enumerate(out_refs):
            at = section % layout.together * layout.blocks
            out_ref[half] = first[section // layout.together, :, at : at + layout.blocks]


def group_sum(near, across, layout):
    size = near[0].size
    return pl.pallas_call(
        functools.partial(group_sum_kernel, layout),
        out_shape=[jax.ShapeDtypeStruct((HALVES, QGROUP, layout.blocks), jnp.bfloat16)] * layout.groups,
        compiler_params=pltpu.CompilerParams(vmem_limit_bytes=SUM_VMEM_LIMIT),
        cost_estimate=pl.CostEstimate(
            flops=30 * size, bytes_accessed=2 * (layout.half + 3) * size, transcendentals=0
        ),
        name="group_sum_code",
    )(*across, *near)


def bfloat16_terms(values):
    terms = []
    for _ in range(3):
        terms.append(values.astype(jnp.bfloat16))
        values = values - terms[-1].astype(jnp.float32)
    return terms


def finish_kernel(sign_ref, *refs):
    out_ref, max_ref = refs[-2:]
    second = [add_all([ref[half] for ref in refs[:-2]]) for half in range(HALVES)]
    blocks = second[0].shape[1]
    natural = jnp.concatenate([part.T for part in second], axis=1)
    block = lax.broadcasted_iota(jnp.int32, (blocks, HALVES * blocks), 0)
    lane = lax.broadcasted_iota(jnp.int32, (blocks, HALVES * blocks), 1)
    largest = jnp.zeros((1, HALVES * blocks), jnp.float32)
    for half in range(HALVES):
        peak = jnp.max(jnp.abs(natural[:, half * QGROUP : (half + 1) * QGROUP]), axis=1, keepdims=True)
        chosen = jnp.where(lane == HALVES * block + half, peak, 0.0)
        largest = jnp.maximum(largest, jnp.max(chosen, axis=0, keepdims=True))
    max_ref[...] = largest * jnp.float32(ROT**-0.5)
    matrix = sylvester()
    high, middle, low = [
        jnp.dot(term, matrix, preferred_element_type=jnp.float32) for term in bfloat16_terms(natural)
    ]
    turned = (high + (middle + low)) * jnp.float32(1.0 / ROT)
    for half in range(HALVES):
        at = pl.ds(half, blocks, stride=HALVES)
        part = turned[:, half * QGROUP : (half + 1) * QGROUP]
        out_ref[at, :] = jnp.where(sign_ref[at, :] == 0, part, -part)


def finish(parts, signs):
    rows = signs.shape[0]
    return pl.pallas_call(
        finish_kernel,
        out_shape=[
            jax.ShapeDtypeStruct((rows, LANES), jnp.float32),
            jax.ShapeDtypeStruct((1, rows), jnp.float32),
        ],
        compiler_params=pltpu.CompilerParams(vmem_limit_bytes=SUM_VMEM_LIMIT),
        name="sum_unrotate",
    )(signs, *parts)


def shards(partials, signs):
    length = partials.shape[-1]
    members = lax.axis_size("local")
    groups = lax.axis_size("node")
    layout = Layout(length, members, groups)
    half = layout.half

    def swap(part, step):
        pairs = []
        for source in range(members):
            first, index = source // half * half, source % half
            pairs.append((source, first + partner(index, step, half)))
        return lax.ppermute(part, "local", pairs)

    def share(parts):
        moved = []
        for step in range(groups - 1, 0, -1):
            pairs = [(source, partner(source, step, groups)) for source in range(groups)]
            moved.append(lax.ppermute(parts[step], "node", pairs))
        return moved + [parts[0]]

    values, sign_rows = partials.reshape(1, length), signs.reshape(length // LANES, LANES)
    counterparts = [(member, (member + half) % members) for member in range(members)]
    slow, fast = list(range(max(half // 2, 1), half)), list(range(1, half // 2))
    order = slow + fast + [0]
    outs = rotate(values, sign_rows, layout, True)
    far = [[outs[HALVES * step + part] for step in range(half)] for part in range(HALVES)]
    for step in slow + fast:
        far[0][step] = swap(far[0][step], step)
    for step in slow[:1]:
        far[1][step] = swap(far[1][step], step)
    outs = rotate(values, sign_rows, layout, False, [far[1][step] for step in slow[1:] + fast])
    for step in slow[1:] + fast:
        far[1][step] = outs.pop(0)
    *near, own_signs = outs
    for step in slow[1:]:
        far[1][step] = swap(far[1][step], step)
    first, later = far_sum([far[0][step] for step in order], [far[1][step] for step in fast] + near[1:])
    across = [lax.ppermute(first, "local", counterparts)]
    for step in fast:
        far[1][step] = swap(later.pop(0), step)
    near[1:] = later
    for step in slow[:1]:
        near[step] = swap(near[step], step)
    rest = slow[1:] + fast
    second, later = far_sum([far[1][step] for step in order], [near[step] for step in rest])
    across.append(lax.ppermute(second, "local", counterparts))
    for step, part in zip(rest, later):
        near[step] = swap(part, step)
    reduced, rotated_max = finish(share(group_sum([near[step] for step in order], across, layout)), own_signs)
    return (reduced.reshape(-1), rotated_max.reshape(-1))


def solution(mesh):
    in_specs = (P("node", "local", None), P())
    out_specs = (P(("node", "local")), P(("node", "local")))
    return jax.shard_map(shards, mesh=mesh, in_specs=in_specs, out_specs=out_specs, check_vma=False)
```

```python
import functools
import jax
import jax.numpy as jnp
from jax import lax
from jax.experimental import pallas as pl
from jax.experimental.pallas import tpu as pltpu
from jax.sharding import PartitionSpec as P

ROT = 256
QGROUP = 128
HALVES = ROT // QGROUP
LANES = 128
VMEM_LIMIT = 50 * 1024 * 1024
SUM_VMEM_LIMIT = 24 * 1024 * 1024
AHEAD = 2
PIECES = 4


def sylvester():
    row = lax.broadcasted_iota(jnp.int32, (ROT, ROT), 0)
    column = lax.broadcasted_iota(jnp.int32, (ROT, ROT), 1)
    parity = lax.population_count(row & column) & 1
    return (1 - 2 * parity).astype(jnp.float32).astype(jnp.bfloat16)


def partner(index, step, count):
    if count & (count - 1) == 0:
        return index ^ step
    return (index + step) % count


def leading_power(x):
    q = x * jnp.float32(2.0**23 + 1.0)
    return q - q * jnp.float32(1.0 - 2.0**-24)


def recode(values):
    magnitude = jnp.abs(values)
    largest = jnp.max(magnitude, axis=-2, keepdims=True)
    least = leading_power(jnp.clip(largest, 2.0**-30, 2.0**30)) * jnp.float32(2.0**-13)
    shift = leading_power(jnp.maximum(magnitude, least)) * jnp.float32(2.0**20)
    nearest = (magnitude + shift) - shift
    rest = magnitude - nearest
    coded = jnp.where(rest == shift * jnp.float32(2.0**-24), magnitude + rest, nearest)
    return jnp.where(values < 0.0, -coded, coded)


class Layout:
    def __init__(self, length, members, groups):
        self.members = members
        self.groups = groups
        self.half = members // 2
        self.portion = length // (members * groups)
        self.rows = self.portion // LANES
        self.blocks = self.portion // ROT
        self.together = 1
        if self.blocks < LANES and LANES % self.blocks == 0 and groups % (LANES // self.blocks) == 0:
            self.together = LANES // self.blocks
        self.units = groups // self.together
        self.columns = self.together * self.blocks

    def shape(self):
        return (self.units, QGROUP, self.columns)

    def span(self, steps):
        return 1 if len(steps) == 1 else self.half

    def batch(self, steps):
        batch = max(1, PIECES // len(steps))
        return batch if self.units % batch == 0 else 1


def rotate_kernel(layout, other, steps, cut, signed_out, extra, values_ref, signs_ref, *refs):
    values, flips, turned, matrix, value_sems, sign_sems = refs[-6:]
    out_refs = list(refs[extra:-6])
    step_refs = [[out_refs.pop(0) for _ in range(HALVES if step in cut else 1)] for step in steps]
    half, portion, rows = layout.half, layout.portion, layout.rows
    node = lax.axis_index("node")
    member = lax.axis_index("local")
    inner = lax.rem(member, half)
    first = half - (member - inner) if other else member - inner
    span, batch = layout.span(steps), layout.batch(steps)
    lowest = partner(inner, steps[0], half) if span == 1 else 0

    def fetches(unit, part):
        place = partner(node, unit * layout.together + part, layout.groups) * layout.members + first + lowest
        return (
            pltpu.make_async_copy(
                values_ref.at[:, pl.ds(pl.multiple_of(place * portion, portion), span * portion)],
                values.at[unit, part],
                value_sems.at[unit, part],
            ),
            pltpu.make_async_copy(
                signs_ref.at[pl.ds(pl.multiple_of(place * rows, rows), span * rows), :],
                flips.at[unit, part],
                sign_sems.at[unit, part],
            ),
        )

    def fetch(unit):
        for part in range(layout.together):
            for copy in fetches(unit, part):
                copy.start()

    ahead = min(max(AHEAD, batch), layout.units)
    for unit in range(ahead):
        fetch(unit)
    matrix[...] = sylvester()

    def body(turn, carry):
        for index in range(batch):
            for part in range(layout.together):
                for copy in fetches(turn * batch + index, part):
                    copy.wait()

        if ahead < layout.units:
            for index in range(batch):

                @pl.when(turn * batch + index + ahead < layout.units)
                def _():
                    fetch(turn * batch + index + ahead)

        for index, (position, step) in [(i, p) for i in range(batch) for p in enumerate(steps)]:
            unit = turn * batch + index
            slot = turned.at[index * len(steps) + position]
            owner = 0 if span == 1 else partner(inner, step, half)
            at = pl.ds(pl.multiple_of(owner * portion, portion), portion)
            at_rows = pl.ds(pl.multiple_of(owner * rows, rows), rows)
            for part in range(layout.together):
                wide = values[unit, part, :, at].astype(jnp.float32).reshape(rows, LANES)
                slot[part * rows : (part + 1) * rows] = jnp.where(flips[unit, part, at_rows, :] == 0, wide, -wide)
            halves = [slot[pl.ds(part, layout.columns, stride=HALVES), :] for part in range(HALVES)]
            signed = jnp.concatenate(halves, axis=1).astype(jnp.bfloat16)
            rotated = lax.dot_general(
                matrix[...], signed, (((1,), (1,)), ((), ())), preferred_element_type=jnp.float32
            )
            for part in range(HALVES):
                rows_of = slice(part * QGROUP, (part + 1) * QGROUP)
                coded = recode(rotated[rows_of]).astype(jnp.bfloat16)
                if step in cut:
                    step_refs[position][part][unit] = coded
                else:
                    step_refs[position][0][unit, rows_of] = coded
        return carry

    lax.fori_loop(0, layout.units // batch, body, 0)
    if signed_out:
        out_refs[0][...] = flips[0, 0, pl.ds(pl.multiple_of(inner * rows, rows), rows), :]


def rotate(values, signs, layout, other, steps, cut=(), signed_out=False, after=(), later=()):
    half, units, columns = layout.half, layout.units, layout.columns
    span, batch = layout.span(steps), layout.batch(steps)
    entries = len(steps) * layout.groups * layout.portion
    passed = [jax.ShapeDtypeStruct(array.shape, array.dtype) for array in later]
    outs = []
    for step in steps:
        cuts = HALVES if step in cut else 1
        outs += [jax.ShapeDtypeStruct((units, ROT // cuts, columns), jnp.bfloat16)] * cuts
    if signed_out:
        outs.append(jax.ShapeDtypeStruct((layout.rows, LANES), jnp.int32))
    extra = len(after) + 2 * len(later)
    return list(
        pl.pallas_call(
            functools.partial(rotate_kernel, layout, other, steps, cut, signed_out, extra),
            in_specs=[pl.BlockSpec(memory_space=pltpu.HBM)] * 2
            + [pl.BlockSpec(memory_space=pl.ANY)] * (len(after) + len(later)),
            out_specs=[pl.BlockSpec(memory_space=pl.ANY)] * len(later)
            + [pl.BlockSpec(memory_space=pltpu.VMEM)] * len(outs),
            out_shape=passed + outs,
            input_output_aliases={2 + len(after) + index: index for index in range(len(later))},
            scratch_shapes=[
                pltpu.VMEM((units, layout.together, 1, span * layout.portion), jnp.bfloat16),
                pltpu.VMEM((units, layout.together, span * layout.rows, LANES), jnp.int32),
                pltpu.VMEM((batch * len(steps), layout.together * layout.rows, LANES), jnp.float32),
                pltpu.VMEM((ROT, ROT), jnp.bfloat16),
                pltpu.SemaphoreType.DMA((units, layout.together)),
                pltpu.SemaphoreType.DMA((units, layout.together)),
            ],
            compiler_params=pltpu.CompilerParams(vmem_limit_bytes=VMEM_LIMIT),
            cost_estimate=pl.CostEstimate(flops=2 * entries * ROT, bytes_accessed=10 * entries, transcendentals=0),
            name="rotate_code",
        )(values, signs, *after, *later)
    )


def add_all(arrays):
    total = arrays[0].astype(jnp.float32)
    for array in arrays[1:]:
        total = total + array.astype(jnp.float32)
    return total


def far_sum_kernel(part, count, *refs):
    arrays = []
    for ref in refs[:count]:
        cut = ref.shape[1] == QGROUP
        arrays.append(ref[...] if cut else ref[:, part * QGROUP : (part + 1) * QGROUP])
    refs[-1][...] = add_all(arrays)


def far_sum(parts, layout, part, later):
    size = QGROUP * layout.units * layout.columns
    *later, total = pl.pallas_call(
        functools.partial(far_sum_kernel, part, len(parts)),
        in_specs=[pl.BlockSpec(memory_space=pltpu.VMEM)] * len(parts)
        + [pl.BlockSpec(memory_space=pl.ANY)] * len(later),
        out_specs=[pl.BlockSpec(memory_space=pl.ANY)] * len(later) + [pl.BlockSpec(memory_space=pltpu.VMEM)],
        out_shape=[jax.ShapeDtypeStruct(array.shape, array.dtype) for array in later]
        + [jax.ShapeDtypeStruct(layout.shape(), jnp.float32)],
        input_output_aliases={len(parts) + index: index for index in range(len(later))},
        compiler_params=pltpu.CompilerParams(vmem_limit_bytes=SUM_VMEM_LIMIT),
        cost_estimate=pl.CostEstimate(
            flops=2 * len(parts) * size, bytes_accessed=(2 * len(parts) + 4) * size, transcendentals=0
        ),
        name="far_sum",
    )(*parts, *later)
    return total, later


def group_sum_kernel(layout, *refs):
    across_refs, near_refs, out_refs = refs[:HALVES], refs[HALVES : HALVES + layout.half], refs[HALVES + layout.half :]
    for half, across_ref in enumerate(across_refs):
        near = [ref[:, half * QGROUP : (half + 1) * QGROUP] for ref in near_refs]
        first = recode(add_all(near + [across_ref[...]])).astype(jnp.bfloat16)
        for section, out_ref in enumerate(out_refs):
            at = section % layout.together * layout.blocks
            out_ref[half] = first[section // layout.together, :, at : at + layout.blocks]


def group_sum(near, across, layout):
    size = near[0].size
    return pl.pallas_call(
        functools.partial(group_sum_kernel, layout),
        out_shape=[jax.ShapeDtypeStruct((HALVES, QGROUP, layout.blocks), jnp.bfloat16)] * layout.groups,
        compiler_params=pltpu.CompilerParams(vmem_limit_bytes=SUM_VMEM_LIMIT),
        cost_estimate=pl.CostEstimate(
            flops=30 * size, bytes_accessed=2 * (layout.half + 3) * size, transcendentals=0
        ),
        name="group_sum_code",
    )(*across, *near)


def bfloat16_terms(values):
    terms = []
    for _ in range(3):
        terms.append(values.astype(jnp.bfloat16))
        values = values - terms[-1].astype(jnp.float32)
    return terms


def finish_kernel(sign_ref, *refs):
    out_ref, max_ref = refs[-2:]
    second = [add_all([ref[half] for ref in refs[:-2]]) for half in range(HALVES)]
    blocks = second[0].shape[1]
    natural = jnp.concatenate([part.T for part in second], axis=1)
    block = lax.broadcasted_iota(jnp.int32, (blocks, HALVES * blocks), 0)
    lane = lax.broadcasted_iota(jnp.int32, (blocks, HALVES * blocks), 1)
    largest = jnp.zeros((1, HALVES * blocks), jnp.float32)
    for half in range(HALVES):
        peak = jnp.max(jnp.abs(natural[:, half * QGROUP : (half + 1) * QGROUP]), axis=1, keepdims=True)
        chosen = jnp.where(lane == HALVES * block + half, peak, 0.0)
        largest = jnp.maximum(largest, jnp.max(chosen, axis=0, keepdims=True))
    max_ref[...] = largest * jnp.float32(ROT**-0.5)
    matrix = sylvester()
    high, middle, low = [
        jnp.dot(term, matrix, preferred_element_type=jnp.float32) for term in bfloat16_terms(natural)
    ]
    turned = (high + (middle + low)) * jnp.float32(1.0 / ROT)
    for half in range(HALVES):
        at = pl.ds(half, blocks, stride=HALVES)
        part = turned[:, half * QGROUP : (half + 1) * QGROUP]
        out_ref[at, :] = jnp.where(sign_ref[at, :] == 0, part, -part)


def finish(parts, signs):
    rows = signs.shape[0]
    return pl.pallas_call(
        finish_kernel,
        out_shape=[
            jax.ShapeDtypeStruct((rows, LANES), jnp.float32),
            jax.ShapeDtypeStruct((1, rows), jnp.float32),
        ],
        compiler_params=pltpu.CompilerParams(vmem_limit_bytes=SUM_VMEM_LIMIT),
        name="sum_unrotate",
    )(signs, *parts)


def shards(partials, signs):
    length = partials.shape[-1]
    members = lax.axis_size("local")
    groups = lax.axis_size("node")
    layout = Layout(length, members, groups)
    half = layout.half

    def swap(part, step):
        pairs = []
        for source in range(members):
            first, index = source // half * half, source % half
            pairs.append((source, first + partner(index, step, half)))
        return lax.ppermute(part, "local", pairs)

    def share(parts):
        moved = []
        for step in range(groups - 1, 0, -1):
            pairs = [(source, partner(source, step, groups)) for source in range(groups)]
            moved.append(lax.ppermute(parts[step], "node", pairs))
        return moved + [parts[0]]

    values, sign_rows = partials.reshape(1, length), signs.reshape(length // LANES, LANES)
    counterparts = [(member, (member + half) % members) for member in range(members)]
    slow = half // 2
    others = [step for step in range(half - 1, 0, -1) if step != slow]
    order = [slow] + others + [0]
    (part,) = rotate(values, sign_rows, layout, True, [slow])
    far = {slow: [swap(part, slow)]}
    outs = rotate(values, sign_rows, layout, True, others + [0], others, after=[part])
    for step in others:
        far[step] = [outs.pop(0), outs.pop(0)]
    far[0] = outs
    for step in others:
        far[step][0] = swap(far[step][0], step)
    for step in others[:-1]:
        far[step][1] = swap(far[step][1], step)
    last = others[-1]
    far[last][1], part = rotate(values, sign_rows, layout, False, [slow], later=[far[last][1]])
    first, (part, far[last][1]) = far_sum([far[step][0] for step in order], layout, 0, [part, far[last][1]])
    across = [lax.ppermute(first, "local", counterparts)]
    near = {slow: swap(part, slow)}
    far[last][1] = swap(far[last][1], last)
    *outs, own_signs = rotate(values, sign_rows, layout, False, others + [0], signed_out=True, after=[first])
    second, outs[:-1] = far_sum([far[step][-1] for step in order], layout, 1, outs[:-1])
    across.append(lax.ppermute(second, "local", counterparts))
    for step, part in zip(others + [0], outs):
        near[step] = swap(part, step) if step else part
    reduced, rotated_max = finish(share(group_sum([near[step] for step in order], across, layout)), own_signs)
    return (reduced.reshape(-1), rotated_max.reshape(-1))


def solution(mesh):
    in_specs = (P("node", "local", None), P())
    out_specs = (P(("node", "local")), P(("node", "local")))
    return jax.shard_map(shards, mesh=mesh, in_specs=in_specs, out_specs=out_specs, check_vma=False)
```

```python
import functools
import jax
import jax.numpy as jnp
from jax import lax
from jax.experimental import pallas as pl
from jax.experimental.pallas import tpu as pltpu
from jax.sharding import PartitionSpec as P

ROT = 256
QGROUP = 128
HALVES = ROT // QGROUP
LANES = 128
VMEM_LIMIT = 50 * 1024 * 1024
SUM_VMEM_LIMIT = 24 * 1024 * 1024
AHEAD = 2
PIECES = 8


def sylvester():
    row = lax.broadcasted_iota(jnp.int32, (ROT, ROT), 0)
    column = lax.broadcasted_iota(jnp.int32, (ROT, ROT), 1)
    parity = lax.population_count(row & column) & 1
    return (1 - 2 * parity).astype(jnp.float32).astype(jnp.bfloat16)


def partner(index, step, count):
    if count & (count - 1) == 0:
        return index ^ step
    return (index + step) % count


def leading_power(x):
    q = x * jnp.float32(2.0**23 + 1.0)
    return q - q * jnp.float32(1.0 - 2.0**-24)


def recode(values):
    magnitude = jnp.abs(values)
    largest = jnp.max(magnitude, axis=-2, keepdims=True)
    least = leading_power(jnp.clip(largest, 2.0**-30, 2.0**30)) * jnp.float32(2.0**-13)
    shift = leading_power(jnp.maximum(magnitude, least)) * jnp.float32(2.0**20)
    nearest = (magnitude + shift) - shift
    rest = magnitude - nearest
    coded = jnp.where(rest == shift * jnp.float32(2.0**-24), magnitude + rest, nearest)
    return jnp.where(values < 0.0, -coded, coded)


class Layout:
    def __init__(self, length, members, groups):
        self.members = members
        self.groups = groups
        self.half = members // 2
        self.portion = length // (members * groups)
        self.rows = self.portion // LANES
        self.blocks = self.portion // ROT
        self.together = 1
        if self.blocks < LANES and LANES % self.blocks == 0 and groups % (LANES // self.blocks) == 0:
            self.together = LANES // self.blocks
        self.units = groups // self.together
        self.columns = self.together * self.blocks

    def shape(self):
        return (self.units, QGROUP, self.columns)

    def span(self, steps):
        return 1 if len(steps) == 1 else self.half

    def batch(self, steps):
        batch = max(1, PIECES // len(steps))
        return batch if self.units % batch == 0 else 1


def rotate_kernel(layout, other, steps, cut, signed_out, extra, values_ref, signs_ref, *refs):
    values, flips, turned, matrix, value_sems, sign_sems = refs[-6:]
    out_refs = list(refs[extra:-6])
    step_refs = [[out_refs.pop(0) for _ in range(HALVES if step in cut else 1)] for step in steps]
    half, portion, rows = layout.half, layout.portion, layout.rows
    node = lax.axis_index("node")
    member = lax.axis_index("local")
    inner = lax.rem(member, half)
    first = half - (member - inner) if other else member - inner
    span, batch = layout.span(steps), layout.batch(steps)
    lowest = partner(inner, steps[0], half) if span == 1 else 0

    def fetches(unit, part):
        place = partner(node, unit * layout.together + part, layout.groups) * layout.members + first + lowest
        return (
            pltpu.make_async_copy(
                values_ref.at[:, pl.ds(pl.multiple_of(place * portion, portion), span * portion)],
                values.at[unit, part],
                value_sems.at[unit, part],
            ),
            pltpu.make_async_copy(
                signs_ref.at[pl.ds(pl.multiple_of(place * rows, rows), span * rows), :],
                flips.at[unit, part],
                sign_sems.at[unit, part],
            ),
        )

    def fetch(unit):
        for part in range(layout.together):
            for copy in fetches(unit, part):
                copy.start()

    ahead = min(max(AHEAD, batch), layout.units)
    for unit in range(ahead):
        fetch(unit)
    matrix[...] = sylvester()

    def body(turn, carry):
        for index in range(batch):
            for part in range(layout.together):
                for copy in fetches(turn * batch + index, part):
                    copy.wait()

        if ahead < layout.units:
            for index in range(batch):

                @pl.when(turn * batch + index + ahead < layout.units)
                def _():
                    fetch(turn * batch + index + ahead)

        for index, (position, step) in [(i, p) for i in range(batch) for p in enumerate(steps)]:
            unit = turn * batch + index
            slot = turned.at[index * len(steps) + position]
            owner = 0 if span == 1 else partner(inner, step, half)
            at = pl.ds(pl.multiple_of(owner * portion, portion), portion)
            at_rows = pl.ds(pl.multiple_of(owner * rows, rows), rows)
            for part in range(layout.together):
                wide = values[unit, part, :, at].astype(jnp.float32).reshape(rows, LANES)
                slot[part * rows : (part + 1) * rows] = jnp.where(flips[unit, part, at_rows, :] == 0, wide, -wide)
            halves = [slot[pl.ds(part, layout.columns, stride=HALVES), :] for part in range(HALVES)]
            signed = jnp.concatenate(halves, axis=1).astype(jnp.bfloat16)
            rotated = lax.dot_general(
                matrix[...], signed, (((1,), (1,)), ((), ())), preferred_element_type=jnp.float32
            )
            for part in range(HALVES):
                rows_of = slice(part * QGROUP, (part + 1) * QGROUP)
                coded = recode(rotated[rows_of]).astype(jnp.bfloat16)
                if step in cut:
                    step_refs[position][part][unit] = coded
                else:
                    step_refs[position][0][unit, rows_of] = coded
        return carry

    lax.fori_loop(0, layout.units // batch, body, 0)
    if signed_out:
        out_refs[0][...] = flips[0, 0, pl.ds(pl.multiple_of(inner * rows, rows), rows), :]


def rotate(values, signs, layout, other, steps, cut=(), signed_out=False, after=(), later=()):
    half, units, columns = layout.half, layout.units, layout.columns
    span, batch = layout.span(steps), layout.batch(steps)
    entries = len(steps) * layout.groups * layout.portion
    passed = [jax.ShapeDtypeStruct(array.shape, array.dtype) for array in later]
    outs = []
    for step in steps:
        cuts = HALVES if step in cut else 1
        outs += [jax.ShapeDtypeStruct((units, ROT // cuts, columns), jnp.bfloat16)] * cuts
    if signed_out:
        outs.append(jax.ShapeDtypeStruct((layout.rows, LANES), jnp.int32))
    extra = len(after) + 2 * len(later)
    return list(
        pl.pallas_call(
            functools.partial(rotate_kernel, layout, other, steps, cut, signed_out, extra),
            in_specs=[pl.BlockSpec(memory_space=pltpu.HBM)] * 2
            + [pl.BlockSpec(memory_space=pl.ANY)] * (len(after) + len(later)),
            out_specs=[pl.BlockSpec(memory_space=pl.ANY)] * len(later)
            + [pl.BlockSpec(memory_space=pltpu.VMEM)] * len(outs),
            out_shape=passed + outs,
            input_output_aliases={2 + len(after) + index: index for index in range(len(later))},
            scratch_shapes=[
                pltpu.VMEM((units, layout.together, 1, span * layout.portion), jnp.bfloat16),
                pltpu.VMEM((units, layout.together, span * layout.rows, LANES), jnp.int32),
                pltpu.VMEM((batch * len(steps), layout.together * layout.rows, LANES), jnp.float32),
                pltpu.VMEM((ROT, ROT), jnp.bfloat16),
                pltpu.SemaphoreType.DMA((units, layout.together)),
                pltpu.SemaphoreType.DMA((units, layout.together)),
            ],
            compiler_params=pltpu.CompilerParams(vmem_limit_bytes=VMEM_LIMIT),
            cost_estimate=pl.CostEstimate(flops=2 * entries * ROT, bytes_accessed=10 * entries, transcendentals=0),
            name="rotate_code",
        )(values, signs, *after, *later)
    )


def add_all(arrays):
    total = arrays[0].astype(jnp.float32)
    for array in arrays[1:]:
        total = total + array.astype(jnp.float32)
    return total


def far_sum_kernel(part, count, *refs):
    arrays = []
    for ref in refs[:count]:
        cut = ref.shape[1] == QGROUP
        arrays.append(ref[...] if cut else ref[:, part * QGROUP : (part + 1) * QGROUP])
    refs[-1][...] = add_all(arrays)


def far_sum(parts, layout, part, later):
    size = QGROUP * layout.units * layout.columns
    *later, total = pl.pallas_call(
        functools.partial(far_sum_kernel, part, len(parts)),
        in_specs=[pl.BlockSpec(memory_space=pltpu.VMEM)] * len(parts)
        + [pl.BlockSpec(memory_space=pl.ANY)] * len(later),
        out_specs=[pl.BlockSpec(memory_space=pl.ANY)] * len(later) + [pl.BlockSpec(memory_space=pltpu.VMEM)],
        out_shape=[jax.ShapeDtypeStruct(array.shape, array.dtype) for array in later]
        + [jax.ShapeDtypeStruct(layout.shape(), jnp.float32)],
        input_output_aliases={len(parts) + index: index for index in range(len(later))},
        compiler_params=pltpu.CompilerParams(vmem_limit_bytes=SUM_VMEM_LIMIT),
        cost_estimate=pl.CostEstimate(
            flops=2 * len(parts) * size, bytes_accessed=(2 * len(parts) + 4) * size, transcendentals=0
        ),
        name="far_sum",
    )(*parts, *later)
    return total, later


def group_sum_kernel(layout, part, count, *refs):
    arrays = []
    for ref in refs[:count]:
        cut = ref.shape[1] == QGROUP
        arrays.append(ref[...] if cut else ref[:, part * QGROUP : (part + 1) * QGROUP])
    first = recode(add_all(arrays)).astype(jnp.bfloat16)
    for section, out_ref in enumerate(refs[count:]):
        at = section % layout.together * layout.blocks
        out_ref[...] = first[section // layout.together, :, at : at + layout.blocks]


def group_sum(parts, layout, part):
    size = QGROUP * layout.units * layout.columns
    return pl.pallas_call(
        functools.partial(group_sum_kernel, layout, part, len(parts)),
        out_shape=[jax.ShapeDtypeStruct((QGROUP, layout.blocks), jnp.bfloat16)] * layout.groups,
        compiler_params=pltpu.CompilerParams(vmem_limit_bytes=SUM_VMEM_LIMIT),
        cost_estimate=pl.CostEstimate(
            flops=30 * size, bytes_accessed=2 * (len(parts) + 2) * size, transcendentals=0
        ),
        name="group_sum_code",
    )(*parts)


def bfloat16_terms(values):
    terms = []
    for _ in range(3):
        terms.append(values.astype(jnp.bfloat16))
        values = values - terms[-1].astype(jnp.float32)
    return terms


def finish_kernel(sign_ref, *refs):
    out_ref, max_ref = refs[-2:]
    count = (len(refs) - 2) // HALVES
    second = [add_all([ref[...] for ref in refs[half * count : (half + 1) * count]]) for half in range(HALVES)]
    blocks = second[0].shape[1]
    natural = jnp.concatenate([part.T for part in second], axis=1)
    block = lax.broadcasted_iota(jnp.int32, (blocks, HALVES * blocks), 0)
    lane = lax.broadcasted_iota(jnp.int32, (blocks, HALVES * blocks), 1)
    largest = jnp.zeros((1, HALVES * blocks), jnp.float32)
    for half in range(HALVES):
        peak = jnp.max(jnp.abs(natural[:, half * QGROUP : (half + 1) * QGROUP]), axis=1, keepdims=True)
        chosen = jnp.where(lane == HALVES * block + half, peak, 0.0)
        largest = jnp.maximum(largest, jnp.max(chosen, axis=0, keepdims=True))
    max_ref[...] = largest * jnp.float32(ROT**-0.5)
    matrix = sylvester()
    high, middle, low = [
        jnp.dot(term, matrix, preferred_element_type=jnp.float32) for term in bfloat16_terms(natural)
    ]
    turned = (high + (middle + low)) * jnp.float32(1.0 / ROT)
    for half in range(HALVES):
        at = pl.ds(half, blocks, stride=HALVES)
        part = turned[:, half * QGROUP : (half + 1) * QGROUP]
        out_ref[at, :] = jnp.where(sign_ref[at, :] == 0, part, -part)


def finish(parts, signs):
    rows = signs.shape[0]
    return pl.pallas_call(
        finish_kernel,
        out_shape=[
            jax.ShapeDtypeStruct((rows, LANES), jnp.float32),
            jax.ShapeDtypeStruct((1, rows), jnp.float32),
        ],
        compiler_params=pltpu.CompilerParams(vmem_limit_bytes=SUM_VMEM_LIMIT),
        name="sum_unrotate",
    )(signs, *parts)


def shards(partials, signs):
    length = partials.shape[-1]
    members = lax.axis_size("local")
    groups = lax.axis_size("node")
    layout = Layout(length, members, groups)
    half = layout.half

    def swap(part, step):
        pairs = []
        for source in range(members):
            first, index = source // half * half, source % half
            pairs.append((source, first + partner(index, step, half)))
        return lax.ppermute(part, "local", pairs)

    def share(parts):
        moved = []
        for step in range(groups - 1, 0, -1):
            pairs = [(source, partner(source, step, groups)) for source in range(groups)]
            moved.append(lax.ppermute(parts[step], "node", pairs))
        return moved + [parts[0]]

    values, sign_rows = partials.reshape(1, length), signs.reshape(length // LANES, LANES)
    counterparts = [(member, (member + half) % members) for member in range(members)]
    slow = half // 2
    others = [slow] + [step for step in range(half - 1, 0, -1) if step != slow]
    last = others[-1]
    outs = rotate(values, sign_rows, layout, True, others + [0], others)
    far = {step: [outs.pop(0), outs.pop(0)] for step in others}
    far[0] = outs
    for step in others:
        far[step][0] = swap(far[step][0], step)
    for step in others[:-1]:
        far[step][1] = swap(far[step][1], step)
    part, *outs, own, own_signs = rotate(
        values, sign_rows, layout, False, others + [0], others, signed_out=True, later=[far[last][1]]
    )
    first, outs = far_sum([far[step][0] for step in others + [0]], layout, 0, [part] + outs)
    across = [lax.ppermute(first, "local", counterparts)]
    far[last][1] = swap(outs.pop(0), last)
    near = {step: [outs.pop(0), outs.pop(0)] for step in others}
    near[0] = [own]
    near[slow][0] = swap(near[slow][0], slow)
    later = [near[step][part] for part in range(HALVES) for step in others if part or step != slow]
    second, outs = far_sum([far[step][-1] for step in others + [0]], layout, 1, later)
    across.append(lax.ppermute(second, "local", counterparts))
    for part in range(HALVES):
        for step in others:
            if part or step != slow:
                near[step][part] = swap(outs.pop(0), step)
    coded = []
    for part in range(HALVES):
        arrays = [near[step][min(part, len(near[step]) - 1)] for step in others + [0]]
        coded += share(group_sum(arrays + [across[part]], layout, part))
    reduced, rotated_max = finish(coded, own_signs)
    return (reduced.reshape(-1), rotated_max.reshape(-1))


def solution(mesh):
    in_specs = (P("node", "local", None), P())
    out_specs = (P(("node", "local")), P(("node", "local")))
    return jax.shard_map(shards, mesh=mesh, in_specs=in_specs, out_specs=out_specs, check_vma=False)
```

```python
import functools
import jax
import jax.numpy as jnp
from jax import lax
from jax.experimental import pallas as pl
from jax.experimental.pallas import tpu as pltpu
from jax.sharding import PartitionSpec as P

ROT = 256
QGROUP = 128
HALVES = ROT // QGROUP
LANES = 128
VMEM_LIMIT = 50 * 1024 * 1024
SUM_VMEM_LIMIT = 24 * 1024 * 1024
AHEAD = 2


def sylvester():
    row = lax.broadcasted_iota(jnp.int32, (ROT, ROT), 0)
    column = lax.broadcasted_iota(jnp.int32, (ROT, ROT), 1)
    parity = lax.population_count(row & column) & 1
    return (1 - 2 * parity).astype(jnp.float32).astype(jnp.bfloat16)


def partner(index, step, count):
    if count & (count - 1) == 0:
        return index ^ step
    return (index + step) % count


def leading_power(x):
    q = x * jnp.float32(2.0**23 + 1.0)
    return q - q * jnp.float32(1.0 - 2.0**-24)


def recode(values):
    magnitude = jnp.abs(values)
    largest = jnp.max(magnitude, axis=-2, keepdims=True)
    least = leading_power(jnp.clip(largest, 2.0**-30, 2.0**30)) * jnp.float32(2.0**-13)
    shift = leading_power(jnp.maximum(magnitude, least)) * jnp.float32(2.0**20)
    nearest = (magnitude + shift) - shift
    rest = magnitude - nearest
    coded = jnp.where(rest == shift * jnp.float32(2.0**-24), magnitude + rest, nearest)
    return jnp.where(values < 0.0, -coded, coded)


class Layout:
    def __init__(self, length, members, groups):
        self.members = members
        self.groups = groups
        self.half = members // 2
        self.portion = length // (members * groups)
        self.rows = self.portion // LANES
        self.blocks = self.portion // ROT
        self.together = 1
        if self.blocks < LANES and LANES % self.blocks == 0 and groups % (LANES // self.blocks) == 0:
            self.together = LANES // self.blocks
        self.units = groups // self.together
        self.columns = self.together * self.blocks

    def shape(self):
        return (self.units, QGROUP, self.columns)


def rotate_kernel(layout, cut, values_ref, signs_ref, *refs):
    values, flips, turned, matrix, value_sems, sign_sems = refs[-6:]
    half, portion, rows = layout.half, layout.portion, layout.rows
    out_refs = list(refs[:-6])
    far_refs = [[out_refs.pop(0) for _ in range(HALVES if step in cut else 1)] for step in range(half)]
    near_refs = [[out_refs.pop(0)] for _ in range(half)]
    node = lax.axis_index("node")
    member = lax.axis_index("local")
    inner = lax.rem(member, half)
    firsts = (half - (member - inner), member - inner)

    def fetches(unit, side, part):
        place = partner(node, unit * layout.together + part, layout.groups) * layout.members + firsts[side]
        return (
            pltpu.make_async_copy(
                values_ref.at[:, pl.ds(pl.multiple_of(place * portion, portion), half * portion)],
                values.at[unit, side, part],
                value_sems.at[unit, side, part],
            ),
            pltpu.make_async_copy(
                signs_ref.at[pl.ds(pl.multiple_of(place * rows, rows), half * rows), :],
                flips.at[unit, side, part],
                sign_sems.at[unit, side, part],
            ),
        )

    def fetch(unit):
        for side in range(2):
            for part in range(layout.together):
                for copy in fetches(unit, side, part):
                    copy.start()

    for unit in range(min(AHEAD, layout.units)):
        fetch(unit)
    matrix[...] = sylvester()

    def body(unit, carry):
        @pl.when(unit + AHEAD < layout.units)
        def _():
            fetch(unit + AHEAD)

        for side, side_refs in enumerate((far_refs, near_refs)):
            for part in range(layout.together):
                for copy in fetches(unit, side, part):
                    copy.wait()
            for step in range(half):
                slot = turned.at[side * half + step]
                owner = partner(inner, step, half)
                at = pl.ds(pl.multiple_of(owner * portion, portion), portion)
                at_rows = pl.ds(pl.multiple_of(owner * rows, rows), rows)
                for part in range(layout.together):
                    wide = values[unit, side, part, :, at].astype(jnp.float32).reshape(rows, LANES)
                    signed = jnp.where(flips[unit, side, part, at_rows, :] == 0, wide, -wide)
                    slot[part * rows : (part + 1) * rows] = signed
                halves = [slot[pl.ds(part, layout.columns, stride=HALVES), :] for part in range(HALVES)]
                signed = jnp.concatenate(halves, axis=1).astype(jnp.bfloat16)
                rotated = lax.dot_general(
                    matrix[...], signed, (((1,), (1,)), ((), ())), preferred_element_type=jnp.float32
                )
                for part in range(HALVES):
                    rows_of = slice(part * QGROUP, (part + 1) * QGROUP)
                    coded = recode(rotated[rows_of]).astype(jnp.bfloat16)
                    if len(side_refs[step]) > 1:
                        side_refs[step][part][unit] = coded
                    else:
                        side_refs[step][0][unit, rows_of] = coded
        return carry

    lax.fori_loop(0, layout.units, body, 0)
    out_refs[0][...] = flips[0, 1, 0, pl.ds(pl.multiple_of(inner * rows, rows), rows), :]


def rotate(values, signs, layout, cut):
    half, units, columns = layout.half, layout.units, layout.columns
    outs = []
    for step in list(range(half)) + [None] * half:
        cuts = HALVES if step in cut else 1
        outs += [jax.ShapeDtypeStruct((units, ROT // cuts, columns), jnp.bfloat16)] * cuts
    outs.append(jax.ShapeDtypeStruct((layout.rows, LANES), jnp.int32))
    outs = pl.pallas_call(
        functools.partial(rotate_kernel, layout, cut),
        in_specs=[pl.BlockSpec(memory_space=pltpu.HBM)] * 2,
        out_shape=outs,
        scratch_shapes=[
            pltpu.VMEM((units, 2, layout.together, 1, half * layout.portion), jnp.bfloat16),
            pltpu.VMEM((units, 2, layout.together, half * layout.rows, LANES), jnp.int32),
            pltpu.VMEM((2 * half, layout.together * layout.rows, LANES), jnp.float32),
            pltpu.VMEM((ROT, ROT), jnp.bfloat16),
            pltpu.SemaphoreType.DMA((units, 2, layout.together)),
            pltpu.SemaphoreType.DMA((units, 2, layout.together)),
        ],
        compiler_params=pltpu.CompilerParams(vmem_limit_bytes=VMEM_LIMIT),
        cost_estimate=pl.CostEstimate(
            flops=2 * values.size * ROT, bytes_accessed=10 * values.size, transcendentals=0
        ),
        name="rotate_code",
    )(values, signs)
    outs = list(outs)
    far = [[outs.pop(0) for _ in range(HALVES if step in cut else 1)] for step in range(half)]
    return far, outs[:-1], outs[-1]


def add_all(arrays):
    total = arrays[0].astype(jnp.float32)
    for array in arrays[1:]:
        total = total + array.astype(jnp.float32)
    return total


def far_sum_kernel(part, count, *refs):
    arrays = []
    for ref in refs[:count]:
        cut = ref.shape[1] == QGROUP
        arrays.append(ref[...] if cut else ref[:, part * QGROUP : (part + 1) * QGROUP])
    refs[-1][...] = add_all(arrays)


def far_sum(parts, layout, part, later):
    size = QGROUP * layout.units * layout.columns
    *later, total = pl.pallas_call(
        functools.partial(far_sum_kernel, part, len(parts)),
        in_specs=[pl.BlockSpec(memory_space=pltpu.VMEM)] * len(parts)
        + [pl.BlockSpec(memory_space=pl.ANY)] * len(later),
        out_specs=[pl.BlockSpec(memory_space=pl.ANY)] * len(later) + [pl.BlockSpec(memory_space=pltpu.VMEM)],
        out_shape=[jax.ShapeDtypeStruct(array.shape, array.dtype) for array in later]
        + [jax.ShapeDtypeStruct(layout.shape(), jnp.float32)],
        input_output_aliases={len(parts) + index: index for index in range(len(later))},
        compiler_params=pltpu.CompilerParams(vmem_limit_bytes=SUM_VMEM_LIMIT),
        cost_estimate=pl.CostEstimate(
            flops=2 * len(parts) * size, bytes_accessed=(2 * len(parts) + 4) * size, transcendentals=0
        ),
        name="far_sum",
    )(*parts, *later)
    return total, later


def group_sum_kernel(layout, *refs):
    across_refs, near_refs, out_refs = refs[:HALVES], refs[HALVES : HALVES + layout.half], refs[HALVES + layout.half :]
    for half, across_ref in enumerate(across_refs):
        near = [ref[:, half * QGROUP : (half + 1) * QGROUP] for ref in near_refs]
        first = recode(add_all(near + [across_ref[...]])).astype(jnp.bfloat16)
        for section, out_ref in enumerate(out_refs):
            at = section % layout.together * layout.blocks
            out_ref[half] = first[section // layout.together, :, at : at + layout.blocks]


def group_sum(near, across, layout):
    size = near[0].size
    return pl.pallas_call(
        functools.partial(group_sum_kernel, layout),
        out_shape=[jax.ShapeDtypeStruct((HALVES, QGROUP, layout.blocks), jnp.bfloat16)] * layout.groups,
        compiler_params=pltpu.CompilerParams(vmem_limit_bytes=SUM_VMEM_LIMIT),
        cost_estimate=pl.CostEstimate(
            flops=30 * size, bytes_accessed=2 * (layout.half + 3) * size, transcendentals=0
        ),
        name="group_sum_code",
    )(*across, *near)


def bfloat16_terms(values):
    terms = []
    for _ in range(3):
        terms.append(values.astype(jnp.bfloat16))
        values = values - terms[-1].astype(jnp.float32)
    return terms


def finish_kernel(sign_ref, *refs):
    out_ref, max_ref = refs[-2:]
    second = [add_all([ref[half] for ref in refs[:-2]]) for half in range(HALVES)]
    blocks = second[0].shape[1]
    natural = jnp.concatenate([part.T for part in second], axis=1)
    block = lax.broadcasted_iota(jnp.int32, (blocks, HALVES * blocks), 0)
    lane = lax.broadcasted_iota(jnp.int32, (blocks, HALVES * blocks), 1)
    largest = jnp.zeros((1, HALVES * blocks), jnp.float32)
    for half in range(HALVES):
        peak = jnp.max(jnp.abs(natural[:, half * QGROUP : (half + 1) * QGROUP]), axis=1, keepdims=True)
        chosen = jnp.where(lane == HALVES * block + half, peak, 0.0)
        largest = jnp.maximum(largest, jnp.max(chosen, axis=0, keepdims=True))
    max_ref[...] = largest * jnp.float32(ROT**-0.5)
    matrix = sylvester()
    high, middle, low = [
        jnp.dot(term, matrix, preferred_element_type=jnp.float32) for term in bfloat16_terms(natural)
    ]
    turned = (high + (middle + low)) * jnp.float32(1.0 / ROT)
    for half in range(HALVES):
        at = pl.ds(half, blocks, stride=HALVES)
        part = turned[:, half * QGROUP : (half + 1) * QGROUP]
        out_ref[at, :] = jnp.where(sign_ref[at, :] == 0, part, -part)


def finish(parts, signs):
    rows = signs.shape[0]
    return pl.pallas_call(
        finish_kernel,
        out_shape=[
            jax.ShapeDtypeStruct((rows, LANES), jnp.float32),
            jax.ShapeDtypeStruct((1, rows), jnp.float32),
        ],
        compiler_params=pltpu.CompilerParams(vmem_limit_bytes=SUM_VMEM_LIMIT),
        name="sum_unrotate",
    )(signs, *parts)


def shards(partials, signs):
    length = partials.shape[-1]
    members = lax.axis_size("local")
    groups = lax.axis_size("node")
    layout = Layout(length, members, groups)
    half = layout.half

    def swap(part, step):
        pairs = []
        for source in range(members):
            first, index = source // half * half, source % half
            pairs.append((source, first + partner(index, step, half)))
        return lax.ppermute(part, "local", pairs)

    def share(parts):
        moved = []
        for step in range(groups - 1, 0, -1):
            pairs = [(source, partner(source, step, groups)) for source in range(groups)]
            moved.append(lax.ppermute(parts[step], "node", pairs))
        return moved + [parts[0]]

    counterparts = [(member, (member + half) % members) for member in range(members)]
    slow = half // 2
    others = [slow] + [step for step in range(half - 1, 0, -1) if step != slow]
    order = others + [0]
    last = others[-1]
    far, near, own_signs = rotate(
        partials.reshape(1, length), signs.reshape(length // LANES, LANES), layout, others
    )
    for step in others:
        far[step][0] = swap(far[step][0], step)
    for step in others[:-1]:
        far[step][1] = swap(far[step][1], step)
    later = [far[last][1]] + [near[step] for step in others]
    first, later = far_sum([far[step][0] for step in order], layout, 0, later)
    across = [lax.ppermute(first, "local", counterparts)]
    far[last][1] = swap(later.pop(0), last)
    near[slow] = swap(later.pop(0), slow)
    second, later = far_sum([far[step][-1] for step in order], layout, 1, later)
    across.append(lax.ppermute(second, "local", counterparts))
    for step, part in zip(others[1:], later):
        near[step] = swap(part, step)
    reduced, rotated_max = finish(share(group_sum([near[step] for step in order], across, layout)), own_signs)
    return (reduced.reshape(-1), rotated_max.reshape(-1))


def solution(mesh):
    in_specs = (P("node", "local", None), P())
    out_specs = (P(("node", "local")), P(("node", "local")))
    return jax.shard_map(shards, mesh=mesh, in_specs=in_specs, out_specs=out_specs, check_vma=False)
```

```python
import functools
import jax
import jax.numpy as jnp
from jax import lax
from jax.experimental import pallas as pl
from jax.experimental.pallas import tpu as pltpu
from jax.sharding import PartitionSpec as P

ROT = 256
QGROUP = 128
HALVES = ROT // QGROUP
LANES = 128
VMEM_LIMIT = 50 * 1024 * 1024
SUM_VMEM_LIMIT = 24 * 1024 * 1024
AHEAD = 4
PIECES = 8


def sylvester():
    row = lax.broadcasted_iota(jnp.int32, (ROT, ROT), 0)
    column = lax.broadcasted_iota(jnp.int32, (ROT, ROT), 1)
    parity = lax.population_count(row & column) & 1
    return (1 - 2 * parity).astype(jnp.float32).astype(jnp.bfloat16)


def partner(index, step, count):
    if count & (count - 1) == 0:
        return index ^ step
    return (index + step) % count


def leading_power(x, factor):
    q = x * jnp.float32((2.0**23 + 1.0) * factor)
    return q - q * jnp.float32(1.0 - 2.0**-24)


def recode(values):
    magnitude = jnp.abs(values)
    largest = jnp.max(magnitude, axis=-2, keepdims=True)
    least = jnp.clip(largest, 2.0**-30, 2.0**30) * jnp.float32(2.0**-13)
    shift = leading_power(jnp.maximum(magnitude, least), 2.0**20)
    nearest = (magnitude + shift) - shift
    rest = magnitude - nearest
    coded = jnp.where(rest == shift * jnp.float32(2.0**-24), magnitude + rest, nearest)
    return jnp.where(values < 0.0, -coded, coded)


class Layout:
    def __init__(self, length, members, groups):
        self.members = members
        self.groups = groups
        self.half = members // 2
        self.portion = length // (members * groups)
        self.rows = self.portion // LANES
        self.blocks = self.portion // ROT
        self.together = 1
        if self.blocks < LANES and LANES % self.blocks == 0 and groups % (LANES // self.blocks) == 0:
            self.together = LANES // self.blocks
        self.units = groups // self.together
        self.columns = self.together * self.blocks

    def shape(self):
        return (self.units, QGROUP, self.columns)

    def span(self, steps):
        return 1 if len(steps) == 1 else self.half

    def batch(self, steps):
        batch = max(1, PIECES // len(steps))
        return batch if self.units % batch == 0 else 1


def rotate_kernel(layout, other, steps, cut, signed_out, extra, values_ref, signs_ref, *refs):
    values, flips, turned, matrix, value_sems, sign_sems = refs[-6:]
    out_refs = list(refs[extra:-6])
    step_refs = [[out_refs.pop(0) for _ in range(HALVES if step in cut else 1)] for step in steps]
    half, portion, rows = layout.half, layout.portion, layout.rows
    node = lax.axis_index("node")
    member = lax.axis_index("local")
    inner = lax.rem(member, half)
    first = half - (member - inner) if other else member - inner
    span, batch = layout.span(steps), layout.batch(steps)
    lowest = partner(inner, steps[0], half) if span == 1 else 0

    def fetches(unit, part):
        place = partner(node, unit * layout.together + part, layout.groups) * layout.members + first + lowest
        return (
            pltpu.make_async_copy(
                values_ref.at[:, pl.ds(pl.multiple_of(place * portion, portion), span * portion)],
                values.at[unit, part],
                value_sems.at[unit, part],
            ),
            pltpu.make_async_copy(
                signs_ref.at[pl.ds(pl.multiple_of(place * rows, rows), span * rows), :],
                flips.at[unit, part],
                sign_sems.at[unit, part],
            ),
        )

    def fetch(unit):
        for part in range(layout.together):
            for copy in fetches(unit, part):
                copy.start()

    ahead = min(max(AHEAD, batch), layout.units)
    for unit in range(ahead):
        fetch(unit)
    matrix[...] = sylvester()

    def body(turn, carry):
        for index in range(batch):
            for part in range(layout.together):
                for copy in fetches(turn * batch + index, part):
                    copy.wait()

        if ahead < layout.units:
            for index in range(batch):

                @pl.when(turn * batch + index + ahead < layout.units)
                def _():
                    fetch(turn * batch + index + ahead)

        for index, (position, step) in [(i, p) for i in range(batch) for p in enumerate(steps)]:
            unit = turn * batch + index
            slot = turned.at[index * len(steps) + position]
            owner = 0 if span == 1 else partner(inner, step, half)
            at = pl.ds(pl.multiple_of(owner * portion, portion), portion)
            at_rows = pl.ds(pl.multiple_of(owner * rows, rows), rows)
            for part in range(layout.together):
                wide = values[unit, part, :, at].astype(jnp.float32).reshape(rows, LANES)
                slot[part * rows : (part + 1) * rows] = jnp.where(flips[unit, part, at_rows, :] == 0, wide, -wide)
            halves = [slot[pl.ds(part, layout.columns, stride=HALVES), :] for part in range(HALVES)]
            signed = jnp.concatenate(halves, axis=1).astype(jnp.bfloat16)
            rotated = lax.dot_general(
                matrix[...], signed, (((1,), (1,)), ((), ())), preferred_element_type=jnp.float32
            )
            for part in range(HALVES):
                rows_of = slice(part * QGROUP, (part + 1) * QGROUP)
                coded = recode(rotated[rows_of]).astype(jnp.bfloat16)
                if step in cut:
                    step_refs[position][part][unit] = coded
                else:
                    step_refs[position][0][unit, rows_of] = coded
        return carry

    lax.fori_loop(0, layout.units // batch, body, 0)
    if signed_out:
        out_refs[0][...] = flips[0, 0, pl.ds(pl.multiple_of(inner * rows, rows), rows), :]


def rotate(values, signs, layout, other, steps, cut=(), signed_out=False, after=(), later=()):
    half, units, columns = layout.half, layout.units, layout.columns
    span, batch = layout.span(steps), layout.batch(steps)
    entries = len(steps) * layout.groups * layout.portion
    passed = [jax.ShapeDtypeStruct(array.shape, array.dtype) for array in later]
    outs = []
    for step in steps:
        cuts = HALVES if step in cut else 1
        outs += [jax.ShapeDtypeStruct((units, ROT // cuts, columns), jnp.bfloat16)] * cuts
    if signed_out:
        outs.append(jax.ShapeDtypeStruct((layout.rows, LANES), jnp.int32))
    extra = len(after) + 2 * len(later)
    return list(
        pl.pallas_call(
            functools.partial(rotate_kernel, layout, other, steps, cut, signed_out, extra),
            in_specs=[pl.BlockSpec(memory_space=pltpu.HBM)] * 2
            + [pl.BlockSpec(memory_space=pl.ANY)] * (len(after) + len(later)),
            out_specs=[pl.BlockSpec(memory_space=pl.ANY)] * len(later)
            + [pl.BlockSpec(memory_space=pltpu.VMEM)] * len(outs),
            out_shape=passed + outs,
            input_output_aliases={2 + len(after) + index: index for index in range(len(later))},
            scratch_shapes=[
                pltpu.VMEM((units, layout.together, 1, span * layout.portion), jnp.bfloat16),
                pltpu.VMEM((units, layout.together, span * layout.rows, LANES), jnp.int32),
                pltpu.VMEM((batch * len(steps), layout.together * layout.rows, LANES), jnp.float32),
                pltpu.VMEM((ROT, ROT), jnp.bfloat16),
                pltpu.SemaphoreType.DMA((units, layout.together)),
                pltpu.SemaphoreType.DMA((units, layout.together)),
            ],
            compiler_params=pltpu.CompilerParams(vmem_limit_bytes=VMEM_LIMIT),
            cost_estimate=pl.CostEstimate(flops=2 * entries * ROT, bytes_accessed=10 * entries, transcendentals=0),
            name="rotate_code",
        )(values, signs, *after, *later)
    )


def add_all(arrays):
    total = arrays[0].astype(jnp.float32)
    for array in arrays[1:]:
        total = total + array.astype(jnp.float32)
    return total


def far_sum_kernel(part, count, *refs):
    arrays = []
    for ref in refs[:count]:
        cut = ref.shape[1] == QGROUP
        arrays.append(ref[...] if cut else ref[:, part * QGROUP : (part + 1) * QGROUP])
    refs[-1][...] = add_all(arrays)


def far_sum(parts, layout, part, later):
    size = QGROUP * layout.units * layout.columns
    *later, total = pl.pallas_call(
        functools.partial(far_sum_kernel, part, len(parts)),
        in_specs=[pl.BlockSpec(memory_space=pltpu.VMEM)] * len(parts)
        + [pl.BlockSpec(memory_space=pl.ANY)] * len(later),
        out_specs=[pl.BlockSpec(memory_space=pl.ANY)] * len(later) + [pl.BlockSpec(memory_space=pltpu.VMEM)],
        out_shape=[jax.ShapeDtypeStruct(array.shape, array.dtype) for array in later]
        + [jax.ShapeDtypeStruct(layout.shape(), jnp.float32)],
        input_output_aliases={len(parts) + index: index for index in range(len(later))},
        compiler_params=pltpu.CompilerParams(vmem_limit_bytes=SUM_VMEM_LIMIT),
        cost_estimate=pl.CostEstimate(
            flops=2 * len(parts) * size, bytes_accessed=(2 * len(parts) + 4) * size, transcendentals=0
        ),
        name="far_sum",
    )(*parts, *later)
    return total, later


def group_sum_kernel(layout, *refs):
    across_refs, near_refs, out_refs = refs[:HALVES], refs[HALVES : HALVES + layout.half], refs[HALVES + layout.half :]
    for half, across_ref in enumerate(across_refs):
        near = [ref[:, half * QGROUP : (half + 1) * QGROUP] for ref in near_refs]
        first = recode(add_all(near + [across_ref[...]])).astype(jnp.bfloat16)
        for section, out_ref in enumerate(out_refs):
            at = section % layout.together * layout.blocks
            out_ref[half] = first[section // layout.together, :, at : at + layout.blocks]


def group_sum(near, across, layout):
    size = near[0].size
    return pl.pallas_call(
        functools.partial(group_sum_kernel, layout),
        out_shape=[jax.ShapeDtypeStruct((HALVES, QGROUP, layout.blocks), jnp.bfloat16)] * layout.groups,
        compiler_params=pltpu.CompilerParams(vmem_limit_bytes=SUM_VMEM_LIMIT),
        cost_estimate=pl.CostEstimate(
            flops=30 * size, bytes_accessed=2 * (layout.half + 3) * size, transcendentals=0
        ),
        name="group_sum_code",
    )(*across, *near)


def bfloat16_terms(values):
    terms = []
    for _ in range(3):
        terms.append(values.astype(jnp.bfloat16))
        values = values - terms[-1].astype(jnp.float32)
    return terms


def finish_kernel(sign_ref, *refs):
    out_ref, max_ref = refs[-2:]
    second = [add_all([ref[half] for ref in refs[:-2]]) for half in range(HALVES)]
    blocks = second[0].shape[1]
    natural = jnp.concatenate([part.T for part in second], axis=1)
    block = lax.broadcasted_iota(jnp.int32, (blocks, HALVES * blocks), 0)
    lane = lax.broadcasted_iota(jnp.int32, (blocks, HALVES * blocks), 1)
    largest = jnp.zeros((1, HALVES * blocks), jnp.float32)
    for half in range(HALVES):
        peak = jnp.max(jnp.abs(natural[:, half * QGROUP : (half + 1) * QGROUP]), axis=1, keepdims=True)
        chosen = jnp.where(lane == HALVES * block + half, peak, 0.0)
        largest = jnp.maximum(largest, jnp.max(chosen, axis=0, keepdims=True))
    max_ref[...] = largest * jnp.float32(ROT**-0.5)
    matrix = sylvester()
    high, middle, low = [
        jnp.dot(term, matrix, preferred_element_type=jnp.float32) for term in bfloat16_terms(natural)
    ]
    turned = (high + (middle + low)) * jnp.float32(1.0 / ROT)
    for half in range(HALVES):
        at = pl.ds(half, blocks, stride=HALVES)
        part = turned[:, half * QGROUP : (half + 1) * QGROUP]
        out_ref[at, :] = jnp.where(sign_ref[at, :] == 0, part, -part)


def finish(parts, signs):
    rows = signs.shape[0]
    return pl.pallas_call(
        finish_kernel,
        out_shape=[
            jax.ShapeDtypeStruct((rows, LANES), jnp.float32),
            jax.ShapeDtypeStruct((1, rows), jnp.float32),
        ],
        compiler_params=pltpu.CompilerParams(vmem_limit_bytes=SUM_VMEM_LIMIT),
        name="sum_unrotate",
    )(signs, *parts)


def shards(partials, signs):
    length = partials.shape[-1]
    members = lax.axis_size("local")
    groups = lax.axis_size("node")
    layout = Layout(length, members, groups)
    half = layout.half

    def swap(part, step):
        pairs = []
        for source in range(members):
            first, index = source // half * half, source % half
            pairs.append((source, first + partner(index, step, half)))
        return lax.ppermute(part, "local", pairs)

    def share(parts):
        moved = []
        for step in range(groups - 1, 0, -1):
            pairs = [(source, partner(source, step, groups)) for source in range(groups)]
            moved.append(lax.ppermute(parts[step], "node", pairs))
        return moved + [parts[0]]

    values, sign_rows = partials.reshape(1, length), signs.reshape(length // LANES, LANES)
    counterparts = [(member, (member + half) % members) for member in range(members)]
    slow = half // 2
    others = [step for step in range(half - 1, 0, -1) if step != slow]
    order = [slow] + others + [0]
    last = order[-2]
    outs = rotate(values, sign_rows, layout, True, order, order[:-1])
    far = {step: [outs.pop(0), outs.pop(0)] for step in order[:-1]}
    far[0] = outs
    for step in order[:-1]:
        far[step][0] = swap(far[step][0], step)
    for step in order[:-2]:
        far[step][1] = swap(far[step][1], step)
    far[last][1], part = rotate(values, sign_rows, layout, False, [slow], later=[far[last][1]])
    first, (part, far[last][1]) = far_sum([far[step][0] for step in order], layout, 0, [part, far[last][1]])
    across = [lax.ppermute(first, "local", counterparts)]
    near = {slow: swap(part, slow)}
    far[last][1] = swap(far[last][1], last)
    *outs, own_signs = rotate(values, sign_rows, layout, False, others + [0], signed_out=True, after=[first])
    second, outs[:-1] = far_sum([far[step][-1] for step in order], layout, 1, outs[:-1])
    across.append(lax.ppermute(second, "local", counterparts))
    for step, part in zip(others + [0], outs):
        near[step] = swap(part, step) if step else part
    reduced, rotated_max = finish(share(group_sum([near[step] for step in order], across, layout)), own_signs)
    return (reduced.reshape(-1), rotated_max.reshape(-1))


def solution(mesh):
    in_specs = (P("node", "local", None), P())
    out_specs = (P(("node", "local")), P(("node", "local")))
    return jax.shard_map(shards, mesh=mesh, in_specs=in_specs, out_specs=out_specs, check_vma=False)
```

```python
import functools
import jax
import jax.numpy as jnp
from jax import lax
from jax.experimental import pallas as pl
from jax.experimental.pallas import tpu as pltpu
from jax.sharding import PartitionSpec as P

ROT = 256
QGROUP = 128
HALVES = ROT // QGROUP
LANES = 128
VMEM_LIMIT = 50 * 1024 * 1024
SUM_VMEM_LIMIT = 24 * 1024 * 1024
AHEAD = 4
PIECES = 8


def sylvester():
    row = lax.broadcasted_iota(jnp.int32, (ROT, ROT), 0)
    column = lax.broadcasted_iota(jnp.int32, (ROT, ROT), 1)
    parity = lax.population_count(row & column) & 1
    return (1 - 2 * parity).astype(jnp.float32).astype(jnp.bfloat16)


def partner(index, step, count):
    if count & (count - 1) == 0:
        return index ^ step
    return (index + step) % count


def leading_power(x, factor):
    q = x * jnp.float32((2.0**23 + 1.0) * factor)
    return q - q * jnp.float32(1.0 - 2.0**-24)


def recode(values):
    magnitude = jnp.abs(values)
    largest = jnp.max(magnitude, axis=-2, keepdims=True)
    least = jnp.clip(largest, 2.0**-30, 2.0**30) * jnp.float32(2.0**-13)
    shift = leading_power(jnp.maximum(magnitude, least), 2.0**20)
    nearest = (magnitude + shift) - shift
    rest = magnitude - nearest
    coded = jnp.where(rest == shift * jnp.float32(2.0**-24), magnitude + rest, nearest)
    return jnp.where(values < 0.0, -coded, coded)


class Layout:
    def __init__(self, length, members, groups):
        self.members = members
        self.groups = groups
        self.half = members // 2
        self.portion = length // (members * groups)
        self.rows = self.portion // LANES
        self.blocks = self.portion // ROT
        self.together = 1
        if self.blocks < LANES and LANES % self.blocks == 0 and groups % (LANES // self.blocks) == 0:
            self.together = LANES // self.blocks
        self.units = groups // self.together
        self.columns = self.together * self.blocks

    def shape(self):
        return (self.units, QGROUP, self.columns)

    def span(self, steps):
        return 1 if len(steps) == 1 else self.half

    def batch(self, steps):
        batch = min(self.units, max(1, PIECES // len(steps)))
        return batch if self.units % batch == 0 else 1


def rotate_kernel(layout, other, steps, cut, signed_out, extra, values_ref, signs_ref, *refs):
    values, flips, turned, matrix, value_sems, sign_sems = refs[-6:]
    out_refs = list(refs[extra:-6])
    step_refs = [[out_refs.pop(0) for _ in range(HALVES if step in cut else 1)] for step in steps]
    half, portion, rows = layout.half, layout.portion, layout.rows
    node = lax.axis_index("node")
    member = lax.axis_index("local")
    inner = lax.rem(member, half)
    first = half - (member - inner) if other else member - inner
    span, batch = layout.span(steps), layout.batch(steps)
    lowest = partner(inner, steps[0], half) if span == 1 else 0

    def fetches(unit, part):
        place = partner(node, unit * layout.together + part, layout.groups) * layout.members + first + lowest
        return (
            pltpu.make_async_copy(
                values_ref.at[:, pl.ds(pl.multiple_of(place * portion, portion), span * portion)],
                values.at[unit, part],
                value_sems.at[unit, part],
            ),
            pltpu.make_async_copy(
                signs_ref.at[pl.ds(pl.multiple_of(place * rows, rows), span * rows), :],
                flips.at[unit, part],
                sign_sems.at[unit, part],
            ),
        )

    def fetch(unit):
        for part in range(layout.together):
            for copy in fetches(unit, part):
                copy.start()

    ahead = min(max(AHEAD, batch), layout.units)
    for unit in range(ahead):
        fetch(unit)
    matrix[...] = sylvester()

    def body(turn, carry):
        for index in range(batch):
            for part in range(layout.together):
                for copy in fetches(turn * batch + index, part):
                    copy.wait()

        if ahead < layout.units:
            for index in range(batch):

                @pl.when(turn * batch + index + ahead < layout.units)
                def _():
                    fetch(turn * batch + index + ahead)

        for index, (position, step) in [(i, p) for i in range(batch) for p in enumerate(steps)]:
            unit = turn * batch + index
            slot = turned.at[index * len(steps) + position]
            owner = 0 if span == 1 else partner(inner, step, half)
            at = pl.ds(pl.multiple_of(owner * portion, portion), portion)
            at_rows = pl.ds(pl.multiple_of(owner * rows, rows), rows)
            for part in range(layout.together):
                wide = values[unit, part, :, at].astype(jnp.float32).reshape(rows, LANES)
                slot[part * rows : (part + 1) * rows] = jnp.where(flips[unit, part, at_rows, :] == 0, wide, -wide)
            halves = [slot[pl.ds(part, layout.columns, stride=HALVES), :] for part in range(HALVES)]
            signed = jnp.concatenate(halves, axis=1).astype(jnp.bfloat16)
            rotated = lax.dot_general(
                matrix[...], signed, (((1,), (1,)), ((), ())), preferred_element_type=jnp.float32
            )
            for part in range(HALVES):
                rows_of = slice(part * QGROUP, (part + 1) * QGROUP)
                coded = recode(rotated[rows_of]).astype(jnp.bfloat16)
                if step in cut:
                    step_refs[position][part][unit] = coded
                else:
                    step_refs[position][0][unit, rows_of] = coded
        return carry

    lax.fori_loop(0, layout.units // batch, body, 0)
    if signed_out:
        out_refs[0][...] = flips[0, 0, pl.ds(pl.multiple_of(inner * rows, rows), rows), :]


def rotate(values, signs, layout, other, steps, cut=(), signed_out=False, after=(), later=()):
    half, units, columns = layout.half, layout.units, layout.columns
    span, batch = layout.span(steps), layout.batch(steps)
    entries = len(steps) * layout.groups * layout.portion
    passed = [jax.ShapeDtypeStruct(array.shape, array.dtype) for array in later]
    outs = []
    for step in steps:
        cuts = HALVES if step in cut else 1
        outs += [jax.ShapeDtypeStruct((units, ROT // cuts, columns), jnp.bfloat16)] * cuts
    if signed_out:
        outs.append(jax.ShapeDtypeStruct((layout.rows, LANES), jnp.int32))
    extra = len(after) + 2 * len(later)
    return list(
        pl.pallas_call(
            functools.partial(rotate_kernel, layout, other, steps, cut, signed_out, extra),
            in_specs=[pl.BlockSpec(memory_space=pltpu.HBM)] * 2
            + [pl.BlockSpec(memory_space=pl.ANY)] * (len(after) + len(later)),
            out_specs=[pl.BlockSpec(memory_space=pl.ANY)] * len(later)
            + [pl.BlockSpec(memory_space=pltpu.VMEM)] * len(outs),
            out_shape=passed + outs,
            input_output_aliases={2 + len(after) + index: index for index in range(len(later))},
            scratch_shapes=[
                pltpu.VMEM((units, layout.together, 1, span * layout.portion), jnp.bfloat16),
                pltpu.VMEM((units, layout.together, span * layout.rows, LANES), jnp.int32),
                pltpu.VMEM((batch * len(steps), layout.together * layout.rows, LANES), jnp.float32),
                pltpu.VMEM((ROT, ROT), jnp.bfloat16),
                pltpu.SemaphoreType.DMA((units, layout.together)),
                pltpu.SemaphoreType.DMA((units, layout.together)),
            ],
            compiler_params=pltpu.CompilerParams(vmem_limit_bytes=VMEM_LIMIT),
            cost_estimate=pl.CostEstimate(flops=2 * entries * ROT, bytes_accessed=10 * entries, transcendentals=0),
            name="rotate_code",
        )(values, signs, *after, *later)
    )


def add_all(arrays):
    total = arrays[0].astype(jnp.float32)
    for array in arrays[1:]:
        total = total + array.astype(jnp.float32)
    return total


def far_sum_kernel(part, count, *refs):
    arrays = []
    for ref in refs[:count]:
        cut = ref.shape[1] == QGROUP
        arrays.append(ref[...] if cut else ref[:, part * QGROUP : (part + 1) * QGROUP])
    refs[-1][...] = add_all(arrays)


def far_sum(parts, layout, part, later):
    size = QGROUP * layout.units * layout.columns
    *later, total = pl.pallas_call(
        functools.partial(far_sum_kernel, part, len(parts)),
        in_specs=[pl.BlockSpec(memory_space=pltpu.VMEM)] * len(parts)
        + [pl.BlockSpec(memory_space=pl.ANY)] * len(later),
        out_specs=[pl.BlockSpec(memory_space=pl.ANY)] * len(later) + [pl.BlockSpec(memory_space=pltpu.VMEM)],
        out_shape=[jax.ShapeDtypeStruct(array.shape, array.dtype) for array in later]
        + [jax.ShapeDtypeStruct(layout.shape(), jnp.float32)],
        input_output_aliases={len(parts) + index: index for index in range(len(later))},
        compiler_params=pltpu.CompilerParams(vmem_limit_bytes=SUM_VMEM_LIMIT),
        cost_estimate=pl.CostEstimate(
            flops=2 * len(parts) * size, bytes_accessed=(2 * len(parts) + 4) * size, transcendentals=0
        ),
        name="far_sum",
    )(*parts, *later)
    return total, later


def group_sum_kernel(layout, *refs):
    across_refs, near_refs, out_refs = refs[:HALVES], refs[HALVES : HALVES + layout.half], refs[HALVES + layout.half :]
    for half, across_ref in enumerate(across_refs):
        near = [ref[:, half * QGROUP : (half + 1) * QGROUP] for ref in near_refs]
        first = recode(add_all(near + [across_ref[...]])).astype(jnp.bfloat16)
        for section, out_ref in enumerate(out_refs):
            at = section % layout.together * layout.blocks
            out_ref[half] = first[section // layout.together, :, at : at + layout.blocks]


def group_sum(near, across, layout):
    size = near[0].size
    return pl.pallas_call(
        functools.partial(group_sum_kernel, layout),
        out_shape=[jax.ShapeDtypeStruct((HALVES, QGROUP, layout.blocks), jnp.bfloat16)] * layout.groups,
        compiler_params=pltpu.CompilerParams(vmem_limit_bytes=SUM_VMEM_LIMIT),
        cost_estimate=pl.CostEstimate(
            flops=30 * size, bytes_accessed=2 * (layout.half + 3) * size, transcendentals=0
        ),
        name="group_sum_code",
    )(*across, *near)


def bfloat16_terms(values):
    terms = []
    for _ in range(3):
        terms.append(values.astype(jnp.bfloat16))
        values = values - terms[-1].astype(jnp.float32)
    return terms


def finish_kernel(sign_ref, *refs):
    out_ref, max_ref = refs[-2:]
    second = [add_all([ref[half] for ref in refs[:-2]]) for half in range(HALVES)]
    blocks = second[0].shape[1]
    natural = jnp.concatenate([part.T for part in second], axis=1)
    block = lax.broadcasted_iota(jnp.int32, (blocks, HALVES * blocks), 0)
    lane = lax.broadcasted_iota(jnp.int32, (blocks, HALVES * blocks), 1)
    largest = jnp.zeros((1, HALVES * blocks), jnp.float32)
    for half in range(HALVES):
        peak = jnp.max(jnp.abs(natural[:, half * QGROUP : (half + 1) * QGROUP]), axis=1, keepdims=True)
        chosen = jnp.where(lane == HALVES * block + half, peak, 0.0)
        largest = jnp.maximum(largest, jnp.max(chosen, axis=0, keepdims=True))
    max_ref[...] = largest * jnp.float32(ROT**-0.5)
    matrix = sylvester()
    high, middle, low = [
        jnp.dot(term, matrix, preferred_element_type=jnp.float32) for term in bfloat16_terms(natural)
    ]
    turned = (high + (middle + low)) * jnp.float32(1.0 / ROT)
    for half in range(HALVES):
        at = pl.ds(half, blocks, stride=HALVES)
        part = turned[:, half * QGROUP : (half + 1) * QGROUP]
        out_ref[at, :] = jnp.where(sign_ref[at, :] == 0, part, -part)


def finish(parts, signs):
    rows = signs.shape[0]
    return pl.pallas_call(
        finish_kernel,
        out_shape=[
            jax.ShapeDtypeStruct((rows, LANES), jnp.float32),
            jax.ShapeDtypeStruct((1, rows), jnp.float32),
        ],
        compiler_params=pltpu.CompilerParams(vmem_limit_bytes=SUM_VMEM_LIMIT),
        name="sum_unrotate",
    )(signs, *parts)


def shards(partials, signs):
    length = partials.shape[-1]
    members = lax.axis_size("local")
    groups = lax.axis_size("node")
    layout = Layout(length, members, groups)
    half = layout.half

    def swap(part, step):
        pairs = []
        for source in range(members):
            first, index = source // half * half, source % half
            pairs.append((source, first + partner(index, step, half)))
        return lax.ppermute(part, "local", pairs)

    def share(parts):
        moved = []
        for step in range(groups - 1, 0, -1):
            pairs = [(source, partner(source, step, groups)) for source in range(groups)]
            moved.append(lax.ppermute(parts[step], "node", pairs))
        return moved + [parts[0]]

    values, sign_rows = partials.reshape(1, length), signs.reshape(length // LANES, LANES)
    counterparts = [(member, (member + half) % members) for member in range(members)]
    slow = half // 2
    others = [step for step in range(half - 1, 0, -1) if step != slow]
    order = others[:1] + [slow] + others[1:] + [0]
    last = order[-2]
    outs = rotate(values, sign_rows, layout, True, order, order[:-1])
    far = {step: [outs.pop(0), outs.pop(0)] for step in order[:-1]}
    far[0] = outs
    for step in order[:-1]:
        far[step][0] = swap(far[step][0], step)
    for step in order[:-2]:
        far[step][1] = swap(far[step][1], step)
    far[last][1], part = rotate(values, sign_rows, layout, False, [slow], later=[far[last][1]])
    first, (part, far[last][1]) = far_sum([far[step][0] for step in order], layout, 0, [part, far[last][1]])
    across = [lax.ppermute(first, "local", counterparts)]
    near = {slow: swap(part, slow)}
    far[last][1] = swap(far[last][1], last)
    *outs, own_signs = rotate(values, sign_rows, layout, False, others + [0], signed_out=True, after=[part])
    second, outs[:-1] = far_sum([far[step][-1] for step in order], layout, 1, outs[:-1])
    across.append(lax.ppermute(second, "local", counterparts))
    for step, part in zip(others + [0], outs):
        near[step] = swap(part, step) if step else part
    reduced, rotated_max = finish(share(group_sum([near[step] for step in order], across, layout)), own_signs)
    return (reduced.reshape(-1), rotated_max.reshape(-1))


def solution(mesh):
    in_specs = (P("node", "local", None), P())
    out_specs = (P(("node", "local")), P(("node", "local")))
    return jax.shard_map(shards, mesh=mesh, in_specs=in_specs, out_specs=out_specs, check_vma=False)
```

```python
import functools
import jax
import jax.numpy as jnp
from jax import lax
from jax.experimental import pallas as pl
from jax.experimental.pallas import tpu as pltpu
from jax.sharding import PartitionSpec as P

ROT = 256
QGROUP = 128
HALVES = ROT // QGROUP
LANES = 128
VMEM_LIMIT = 50 * 1024 * 1024
SUM_VMEM_LIMIT = 24 * 1024 * 1024
AHEAD = 4
PIECES = 8


def sylvester():
    row = lax.broadcasted_iota(jnp.int32, (ROT, ROT), 0)
    column = lax.broadcasted_iota(jnp.int32, (ROT, ROT), 1)
    parity = lax.population_count(row & column) & 1
    return (1 - 2 * parity).astype(jnp.float32).astype(jnp.bfloat16)


def partner(index, step, count):
    if count & (count - 1) == 0:
        return index ^ step
    return (index + step) % count


def leading_power(x, factor):
    q = x * jnp.float32((2.0**23 + 1.0) * factor)
    return q - q * jnp.float32(1.0 - 2.0**-24)


def recode(values):
    magnitude = jnp.abs(values)
    largest = jnp.max(magnitude, axis=-2, keepdims=True)
    least = jnp.clip(largest, 2.0**-30, 2.0**30) * jnp.float32(2.0**-13)
    shift = leading_power(jnp.maximum(magnitude, least), 2.0**20)
    nearest = (magnitude + shift) - shift
    rest = magnitude - nearest
    coded = jnp.where(rest == shift * jnp.float32(2.0**-24), magnitude + rest, nearest)
    return jnp.where(values < 0.0, -coded, coded)


class Layout:
    def __init__(self, length, members, groups):
        self.members = members
        self.groups = groups
        self.half = members // 2
        self.portion = length // (members * groups)
        self.rows = self.portion // LANES
        self.blocks = self.portion // ROT
        self.together = 1
        if self.blocks < LANES and LANES % self.blocks == 0 and groups % (LANES // self.blocks) == 0:
            self.together = LANES // self.blocks
        self.units = groups // self.together
        self.columns = self.together * self.blocks

    def shape(self):
        return (self.units, QGROUP, self.columns)

    def span(self, steps):
        return 1 if len(steps) == 1 else self.half

    def batch(self, steps):
        batch = min(self.units, max(1, PIECES // len(steps)))
        return batch if self.units % batch == 0 else 1


def rotate_kernel(layout, other, steps, cut, signed_out, extra, values_ref, signs_ref, *refs):
    values, flips, turned, matrix, value_sems, sign_sems = refs[-6:]
    out_refs = list(refs[extra:-6])
    step_refs = [[out_refs.pop(0) for _ in range(HALVES if step in cut else 1)] for step in steps]
    half, portion, rows = layout.half, layout.portion, layout.rows
    node = lax.axis_index("node")
    member = lax.axis_index("local")
    inner = lax.rem(member, half)
    first = half - (member - inner) if other else member - inner
    span, batch = layout.span(steps), layout.batch(steps)
    lowest = partner(inner, steps[0], half) if span == 1 else 0

    def fetches(unit, part):
        place = partner(node, unit * layout.together + part, layout.groups) * layout.members + first + lowest
        return (
            pltpu.make_async_copy(
                values_ref.at[:, pl.ds(pl.multiple_of(place * portion, portion), span * portion)],
                values.at[unit, part],
                value_sems.at[unit, part],
            ),
            pltpu.make_async_copy(
                signs_ref.at[pl.ds(pl.multiple_of(place * rows, rows), span * rows), :],
                flips.at[unit, part],
                sign_sems.at[unit, part],
            ),
        )

    def fetch(unit):
        for part in range(layout.together):
            for copy in fetches(unit, part):
                copy.start()

    ahead = min(max(AHEAD, batch), layout.units)
    for unit in range(ahead):
        fetch(unit)
    matrix[...] = sylvester()

    def body(turn, carry):
        for index in range(batch):
            for part in range(layout.together):
                for copy in fetches(turn * batch + index, part):
                    copy.wait()

        if ahead < layout.units:
            for index in range(batch):

                @pl.when(turn * batch + index + ahead < layout.units)
                def _():
                    fetch(turn * batch + index + ahead)

        for index, (position, step) in [(i, p) for i in range(batch) for p in enumerate(steps)]:
            unit = turn * batch + index
            slot = turned.at[index * len(steps) + position]
            owner = 0 if span == 1 else partner(inner, step, half)
            at = pl.ds(pl.multiple_of(owner * portion, portion), portion)
            at_rows = pl.ds(pl.multiple_of(owner * rows, rows), rows)
            for part in range(layout.together):
                wide = values[unit, part, :, at].astype(jnp.float32).reshape(rows, LANES)
                slot[part * rows : (part + 1) * rows] = jnp.where(flips[unit, part, at_rows, :] == 0, wide, -wide)
            halves = [slot[pl.ds(part, layout.columns, stride=HALVES), :] for part in range(HALVES)]
            signed = jnp.concatenate(halves, axis=1).astype(jnp.bfloat16)
            rotated = lax.dot_general(
                matrix[...], signed, (((1,), (1,)), ((), ())), preferred_element_type=jnp.float32
            )
            for part in range(HALVES):
                rows_of = slice(part * QGROUP, (part + 1) * QGROUP)
                coded = recode(rotated[rows_of]).astype(jnp.bfloat16)
                if step in cut:
                    step_refs[position][part][unit] = coded
                else:
                    step_refs[position][0][unit, rows_of] = coded
        return carry

    lax.fori_loop(0, layout.units // batch, body, 0)
    if signed_out:
        out_refs[0][...] = flips[0, 0, pl.ds(pl.multiple_of(inner * rows, rows), rows), :]


def rotate(values, signs, layout, other, steps, cut=(), signed_out=False, after=(), later=()):
    half, units, columns = layout.half, layout.units, layout.columns
    span, batch = layout.span(steps), layout.batch(steps)
    entries = len(steps) * layout.groups * layout.portion
    passed = [jax.ShapeDtypeStruct(array.shape, array.dtype) for array in later]
    outs = []
    for step in steps:
        cuts = HALVES if step in cut else 1
        outs += [jax.ShapeDtypeStruct((units, ROT // cuts, columns), jnp.bfloat16)] * cuts
    if signed_out:
        outs.append(jax.ShapeDtypeStruct((layout.rows, LANES), jnp.int32))
    extra = len(after) + 2 * len(later)
    return list(
        pl.pallas_call(
            functools.partial(rotate_kernel, layout, other, steps, cut, signed_out, extra),
            in_specs=[pl.BlockSpec(memory_space=pltpu.HBM)] * 2
            + [pl.BlockSpec(memory_space=pl.ANY)] * (len(after) + len(later)),
            out_specs=[pl.BlockSpec(memory_space=pl.ANY)] * len(later)
            + [pl.BlockSpec(memory_space=pltpu.VMEM)] * len(outs),
            out_shape=passed + outs,
            input_output_aliases={2 + len(after) + index: index for index in range(len(later))},
            scratch_shapes=[
                pltpu.VMEM((units, layout.together, 1, span * layout.portion), jnp.bfloat16),
                pltpu.VMEM((units, layout.together, span * layout.rows, LANES), jnp.int32),
                pltpu.VMEM((batch * len(steps), layout.together * layout.rows, LANES), jnp.float32),
                pltpu.VMEM((ROT, ROT), jnp.bfloat16),
                pltpu.SemaphoreType.DMA((units, layout.together)),
                pltpu.SemaphoreType.DMA((units, layout.together)),
            ],
            compiler_params=pltpu.CompilerParams(vmem_limit_bytes=VMEM_LIMIT),
            cost_estimate=pl.CostEstimate(flops=2 * entries * ROT, bytes_accessed=10 * entries, transcendentals=0),
            name="rotate_code",
        )(values, signs, *after, *later)
    )


def add_all(arrays):
    total = arrays[0].astype(jnp.float32)
    for array in arrays[1:]:
        total = total + array.astype(jnp.float32)
    return total


def far_sum_kernel(part, count, *refs):
    arrays = []
    for ref in refs[:count]:
        cut = ref.shape[1] == QGROUP
        arrays.append(ref[...] if cut else ref[:, part * QGROUP : (part + 1) * QGROUP])
    refs[-1][...] = add_all(arrays)


def far_sum(parts, layout, part, later):
    size = QGROUP * layout.units * layout.columns
    *later, total = pl.pallas_call(
        functools.partial(far_sum_kernel, part, len(parts)),
        in_specs=[pl.BlockSpec(memory_space=pltpu.VMEM)] * len(parts)
        + [pl.BlockSpec(memory_space=pl.ANY)] * len(later),
        out_specs=[pl.BlockSpec(memory_space=pl.ANY)] * len(later) + [pl.BlockSpec(memory_space=pltpu.VMEM)],
        out_shape=[jax.ShapeDtypeStruct(array.shape, array.dtype) for array in later]
        + [jax.ShapeDtypeStruct(layout.shape(), jnp.float32)],
        input_output_aliases={len(parts) + index: index for index in range(len(later))},
        compiler_params=pltpu.CompilerParams(vmem_limit_bytes=SUM_VMEM_LIMIT),
        cost_estimate=pl.CostEstimate(
            flops=2 * len(parts) * size, bytes_accessed=(2 * len(parts) + 4) * size, transcendentals=0
        ),
        name="far_sum",
    )(*parts, *later)
    return total, later


def group_sum_kernel(layout, *refs):
    across_refs, near_refs, out_refs = refs[:HALVES], refs[HALVES : HALVES + layout.half], refs[HALVES + layout.half :]
    for half, across_ref in enumerate(across_refs):
        near = [ref[:, half * QGROUP : (half + 1) * QGROUP] for ref in near_refs]
        first = recode(add_all(near + [across_ref[...]])).astype(jnp.bfloat16)
        for section, out_ref in enumerate(out_refs):
            at = section % layout.together * layout.blocks
            out_ref[half] = first[section // layout.together, :, at : at + layout.blocks]


def group_sum(near, across, layout):
    size = near[0].size
    return pl.pallas_call(
        functools.partial(group_sum_kernel, layout),
        out_shape=[jax.ShapeDtypeStruct((HALVES, QGROUP, layout.blocks), jnp.bfloat16)] * layout.groups,
        compiler_params=pltpu.CompilerParams(vmem_limit_bytes=SUM_VMEM_LIMIT),
        cost_estimate=pl.CostEstimate(
            flops=30 * size, bytes_accessed=2 * (layout.half + 3) * size, transcendentals=0
        ),
        name="group_sum_code",
    )(*across, *near)


def bfloat16_terms(values):
    terms = []
    for _ in range(3):
        terms.append(values.astype(jnp.bfloat16))
        values = values - terms[-1].astype(jnp.float32)
    return terms


def finish_kernel(sign_ref, *refs):
    out_ref, max_ref = refs[-2:]
    second = [add_all([ref[half] for ref in refs[:-2]]) for half in range(HALVES)]
    blocks = second[0].shape[1]
    natural = jnp.concatenate([part.T for part in second], axis=1)
    block = lax.broadcasted_iota(jnp.int32, (blocks, HALVES * blocks), 0)
    lane = lax.broadcasted_iota(jnp.int32, (blocks, HALVES * blocks), 1)
    largest = jnp.zeros((1, HALVES * blocks), jnp.float32)
    for half in range(HALVES):
        peak = jnp.max(jnp.abs(natural[:, half * QGROUP : (half + 1) * QGROUP]), axis=1, keepdims=True)
        chosen = jnp.where(lane == HALVES * block + half, peak, 0.0)
        largest = jnp.maximum(largest, jnp.max(chosen, axis=0, keepdims=True))
    max_ref[...] = largest * jnp.float32(ROT**-0.5)
    matrix = sylvester()
    high, middle, low = [
        jnp.dot(term, matrix, preferred_element_type=jnp.float32) for term in bfloat16_terms(natural)
    ]
    turned = (high + (middle + low)) * jnp.float32(1.0 / ROT)
    for half in range(HALVES):
        at = pl.ds(half, blocks, stride=HALVES)
        part = turned[:, half * QGROUP : (half + 1) * QGROUP]
        out_ref[at, :] = jnp.where(sign_ref[at, :] == 0, part, -part)


def finish(parts, signs):
    rows = signs.shape[0]
    return pl.pallas_call(
        finish_kernel,
        out_shape=[
            jax.ShapeDtypeStruct((rows, LANES), jnp.float32),
            jax.ShapeDtypeStruct((1, rows), jnp.float32),
        ],
        compiler_params=pltpu.CompilerParams(vmem_limit_bytes=SUM_VMEM_LIMIT),
        name="sum_unrotate",
    )(signs, *parts)


def shards(partials, signs):
    length = partials.shape[-1]
    members = lax.axis_size("local")
    groups = lax.axis_size("node")
    layout = Layout(length, members, groups)
    half = layout.half

    def swap(part, step):
        pairs = []
        for source in range(members):
            first, index = source // half * half, source % half
            pairs.append((source, first + partner(index, step, half)))
        return lax.ppermute(part, "local", pairs)

    def share(parts):
        moved = []
        for step in range(groups - 1, 0, -1):
            pairs = [(source, partner(source, step, groups)) for source in range(groups)]
            moved.append(lax.ppermute(parts[step], "node", pairs))
        return moved + [parts[0]]

    values, sign_rows = partials.reshape(1, length), signs.reshape(length // LANES, LANES)
    counterparts = [(member, (member + half) % members) for member in range(members)]
    slow = half // 2
    others = [step for step in range(half - 1, 0, -1) if step != slow]
    order = others + [slow, 0]
    (part,) = rotate(values, sign_rows, layout, True, [slow])
    far = {slow: [swap(part, slow)]}
    outs = rotate(values, sign_rows, layout, True, others + [0], others, after=[part])
    for step in others:
        far[step] = [swap(outs.pop(0), step), outs.pop(0)]
    far[0] = outs
    *later, part = rotate(values, sign_rows, layout, False, [slow], later=[far[step][1] for step in others])
    near = {slow: swap(part, slow)}
    first, later = far_sum([far[step][0] for step in order], layout, 0, later)
    across = [lax.ppermute(first, "local", counterparts)]
    for step, part in zip(others, later):
        far[step][1] = swap(part, step)
    *outs, own_signs = rotate(values, sign_rows, layout, False, others + [0], signed_out=True, after=[first])
    for step in others[:1]:
        near[step] = swap(outs[0], step)
    second, (near[slow], *later) = far_sum(
        [far[step][-1] for step in order], layout, 1, [near[slow]] + outs[1:-1]
    )
    across.append(lax.ppermute(second, "local", counterparts))
    for step, part in zip(others[1:], later):
        near[step] = swap(part, step)
    near[0] = outs[-1]
    reduced, rotated_max = finish(share(group_sum([near[step] for step in order], across, layout)), own_signs)
    return (reduced.reshape(-1), rotated_max.reshape(-1))


def solution(mesh):
    in_specs = (P("node", "local", None), P())
    out_specs = (P(("node", "local")), P(("node", "local")))
    return jax.shard_map(shards, mesh=mesh, in_specs=in_specs, out_specs=out_specs, check_vma=False)
```

```python
import functools
import jax
import jax.numpy as jnp
from jax import lax
from jax.experimental import pallas as pl
from jax.experimental.pallas import tpu as pltpu
from jax.sharding import PartitionSpec as P

ROT = 256
QGROUP = 128
HALVES = ROT // QGROUP
LANES = 128
VMEM_LIMIT = 50 * 1024 * 1024
SUM_VMEM_LIMIT = 24 * 1024 * 1024
AHEAD = 4
PIECES = 8


def sylvester():
    row = lax.broadcasted_iota(jnp.int32, (ROT, ROT), 0)
    column = lax.broadcasted_iota(jnp.int32, (ROT, ROT), 1)
    parity = lax.population_count(row & column) & 1
    return (1 - 2 * parity).astype(jnp.float32).astype(jnp.bfloat16)


def partner(index, step, count):
    if count & (count - 1) == 0:
        return index ^ step
    return (index + step) % count


def leading_power(x, factor):
    q = x * jnp.float32((2.0**23 + 1.0) * factor)
    return q - q * jnp.float32(1.0 - 2.0**-24)


def recode(values):
    magnitude = jnp.abs(values)
    largest = jnp.max(magnitude, axis=-2, keepdims=True)
    least = jnp.clip(largest, 2.0**-30, 2.0**30) * jnp.float32(2.0**-13)
    shift = leading_power(jnp.maximum(magnitude, least), 2.0**20)
    nearest = (magnitude + shift) - shift
    rest = magnitude - nearest
    coded = jnp.where(rest == shift * jnp.float32(2.0**-24), magnitude + rest, nearest)
    return jnp.where(values < 0.0, -coded, coded)


class Layout:
    def __init__(self, length, members, groups):
        self.members = members
        self.groups = groups
        self.half = members // 2
        self.portion = length // (members * groups)
        self.rows = self.portion // LANES
        self.blocks = self.portion // ROT
        self.together = 1
        if self.blocks < LANES and LANES % self.blocks == 0 and groups % (LANES // self.blocks) == 0:
            self.together = LANES // self.blocks
        self.units = groups // self.together
        self.columns = self.together * self.blocks

    def shape(self):
        return (self.units, QGROUP, self.columns)

    def span(self, steps):
        return 1 if len(steps) == 1 else self.half

    def batch(self, steps):
        batch = min(self.units, max(1, PIECES // len(steps)))
        return batch if self.units % batch == 0 else 1


def rotate_kernel(layout, other, steps, cut, signed_out, extra, values_ref, signs_ref, *refs):
    values, flips, turned, matrix, value_sems, sign_sems = refs[-6:]
    out_refs = list(refs[extra:-6])
    step_refs = [[out_refs.pop(0) for _ in range(HALVES if step in cut else 1)] for step in steps]
    half, portion, rows = layout.half, layout.portion, layout.rows
    node = lax.axis_index("node")
    member = lax.axis_index("local")
    inner = lax.rem(member, half)
    first = half - (member - inner) if other else member - inner
    span, batch = layout.span(steps), layout.batch(steps)
    lowest = partner(inner, steps[0], half) if span == 1 else 0

    def fetches(unit, part):
        place = partner(node, unit * layout.together + part, layout.groups) * layout.members + first + lowest
        return (
            pltpu.make_async_copy(
                values_ref.at[:, pl.ds(pl.multiple_of(place * portion, portion), span * portion)],
                values.at[unit, part],
                value_sems.at[unit, part],
            ),
            pltpu.make_async_copy(
                signs_ref.at[pl.ds(pl.multiple_of(place * rows, rows), span * rows), :],
                flips.at[unit, part],
                sign_sems.at[unit, part],
            ),
        )

    def fetch(unit):
        for part in range(layout.together):
            for copy in fetches(unit, part):
                copy.start()

    ahead = min(max(AHEAD, batch), layout.units)
    for unit in range(ahead):
        fetch(unit)
    matrix[...] = sylvester()

    def body(turn, carry):
        for index in range(batch):
            for part in range(layout.together):
                for copy in fetches(turn * batch + index, part):
                    copy.wait()

        if ahead < layout.units:
            for index in range(batch):

                @pl.when(turn * batch + index + ahead < layout.units)
                def _():
                    fetch(turn * batch + index + ahead)

        for index, (position, step) in [(i, p) for i in range(batch) for p in enumerate(steps)]:
            unit = turn * batch + index
            slot = turned.at[index * len(steps) + position]
            owner = 0 if span == 1 else partner(inner, step, half)
            at = pl.ds(pl.multiple_of(owner * portion, portion), portion)
            at_rows = pl.ds(pl.multiple_of(owner * rows, rows), rows)
            for part in range(layout.together):
                wide = values[unit, part, :, at].astype(jnp.float32).reshape(rows, LANES)
                slot[part * rows : (part + 1) * rows] = jnp.where(flips[unit, part, at_rows, :] == 0, wide, -wide)
            halves = [slot[pl.ds(part, layout.columns, stride=HALVES), :] for part in range(HALVES)]
            signed = jnp.concatenate(halves, axis=1).astype(jnp.bfloat16)
            rotated = lax.dot_general(
                matrix[...], signed, (((1,), (1,)), ((), ())), preferred_element_type=jnp.float32
            )
            for part in range(HALVES):
                rows_of = slice(part * QGROUP, (part + 1) * QGROUP)
                coded = recode(rotated[rows_of]).astype(jnp.bfloat16)
                if step in cut:
                    step_refs[position][part][unit] = coded
                else:
                    step_refs[position][0][unit, rows_of] = coded
        return carry

    lax.fori_loop(0, layout.units // batch, body, 0)
    if signed_out:
        out_refs[0][...] = flips[0, 0, pl.ds(pl.multiple_of(inner * rows, rows), rows), :]


def rotate(values, signs, layout, other, steps, cut=(), signed_out=False, after=(), later=()):
    half, units, columns = layout.half, layout.units, layout.columns
    span, batch = layout.span(steps), layout.batch(steps)
    entries = len(steps) * layout.groups * layout.portion
    passed = [jax.ShapeDtypeStruct(array.shape, array.dtype) for array in later]
    outs = []
    for step in steps:
        cuts = HALVES if step in cut else 1
        outs += [jax.ShapeDtypeStruct((units, ROT // cuts, columns), jnp.bfloat16)] * cuts
    if signed_out:
        outs.append(jax.ShapeDtypeStruct((layout.rows, LANES), jnp.int32))
    extra = len(after) + 2 * len(later)
    return list(
        pl.pallas_call(
            functools.partial(rotate_kernel, layout, other, steps, cut, signed_out, extra),
            in_specs=[pl.BlockSpec(memory_space=pltpu.HBM)] * 2
            + [pl.BlockSpec(memory_space=pl.ANY)] * (len(after) + len(later)),
            out_specs=[pl.BlockSpec(memory_space=pl.ANY)] * len(later)
            + [pl.BlockSpec(memory_space=pltpu.VMEM)] * len(outs),
            out_shape=passed + outs,
            input_output_aliases={2 + len(after) + index: index for index in range(len(later))},
            scratch_shapes=[
                pltpu.VMEM((units, layout.together, 1, span * layout.portion), jnp.bfloat16),
                pltpu.VMEM((units, layout.together, span * layout.rows, LANES), jnp.int32),
                pltpu.VMEM((batch * len(steps), layout.together * layout.rows, LANES), jnp.float32),
                pltpu.VMEM((ROT, ROT), jnp.bfloat16),
                pltpu.SemaphoreType.DMA((units, layout.together)),
                pltpu.SemaphoreType.DMA((units, layout.together)),
            ],
            compiler_params=pltpu.CompilerParams(vmem_limit_bytes=VMEM_LIMIT),
            cost_estimate=pl.CostEstimate(flops=2 * entries * ROT, bytes_accessed=10 * entries, transcendentals=0),
            name="rotate_code",
        )(values, signs, *after, *later)
    )


def add_all(arrays):
    total = arrays[0].astype(jnp.float32)
    for array in arrays[1:]:
        total = total + array.astype(jnp.float32)
    return total


def far_sum_kernel(part, count, *refs):
    arrays = []
    for ref in refs[:count]:
        cut = ref.shape[1] == QGROUP
        arrays.append(ref[...] if cut else ref[:, part * QGROUP : (part + 1) * QGROUP])
    refs[-1][...] = add_all(arrays)


def far_sum(parts, layout, part, later, after=()):
    size = QGROUP * layout.units * layout.columns
    *later, total = pl.pallas_call(
        functools.partial(far_sum_kernel, part, len(parts)),
        in_specs=[pl.BlockSpec(memory_space=pltpu.VMEM)] * len(parts)
        + [pl.BlockSpec(memory_space=pl.ANY)] * (len(later) + len(after)),
        out_specs=[pl.BlockSpec(memory_space=pl.ANY)] * len(later) + [pl.BlockSpec(memory_space=pltpu.VMEM)],
        out_shape=[jax.ShapeDtypeStruct(array.shape, array.dtype) for array in later]
        + [jax.ShapeDtypeStruct(layout.shape(), jnp.float32)],
        input_output_aliases={len(parts) + index: index for index in range(len(later))},
        compiler_params=pltpu.CompilerParams(vmem_limit_bytes=SUM_VMEM_LIMIT),
        cost_estimate=pl.CostEstimate(
            flops=2 * len(parts) * size, bytes_accessed=(2 * len(parts) + 4) * size, transcendentals=0
        ),
        name="far_sum",
    )(*parts, *later, *after)
    return total, later


def group_sum_kernel(layout, *refs):
    across_refs, near_refs, out_refs = refs[:HALVES], refs[HALVES : HALVES + layout.half], refs[HALVES + layout.half :]
    for half, across_ref in enumerate(across_refs):
        near = [ref[:, half * QGROUP : (half + 1) * QGROUP] for ref in near_refs]
        first = recode(add_all(near + [across_ref[...]])).astype(jnp.bfloat16)
        for section, out_ref in enumerate(out_refs):
            at = section % layout.together * layout.blocks
            out_ref[half] = first[section // layout.together, :, at : at + layout.blocks]


def group_sum(near, across, layout):
    size = near[0].size
    return pl.pallas_call(
        functools.partial(group_sum_kernel, layout),
        out_shape=[jax.ShapeDtypeStruct((HALVES, QGROUP, layout.blocks), jnp.bfloat16)] * layout.groups,
        compiler_params=pltpu.CompilerParams(vmem_limit_bytes=SUM_VMEM_LIMIT),
        cost_estimate=pl.CostEstimate(
            flops=30 * size, bytes_accessed=2 * (layout.half + 3) * size, transcendentals=0
        ),
        name="group_sum_code",
    )(*across, *near)


def bfloat16_terms(values):
    terms = []
    for _ in range(3):
        terms.append(values.astype(jnp.bfloat16))
        values = values - terms[-1].astype(jnp.float32)
    return terms


def finish_kernel(sign_ref, *refs):
    out_ref, max_ref = refs[-2:]
    second = [add_all([ref[half] for ref in refs[:-2]]) for half in range(HALVES)]
    blocks = second[0].shape[1]
    natural = jnp.concatenate([part.T for part in second], axis=1)
    block = lax.broadcasted_iota(jnp.int32, (blocks, HALVES * blocks), 0)
    lane = lax.broadcasted_iota(jnp.int32, (blocks, HALVES * blocks), 1)
    largest = jnp.zeros((1, HALVES * blocks), jnp.float32)
    for half in range(HALVES):
        peak = jnp.max(jnp.abs(natural[:, half * QGROUP : (half + 1) * QGROUP]), axis=1, keepdims=True)
        chosen = jnp.where(lane == HALVES * block + half, peak, 0.0)
        largest = jnp.maximum(largest, jnp.max(chosen, axis=0, keepdims=True))
    max_ref[...] = largest * jnp.float32(ROT**-0.5)
    matrix = sylvester()
    high, middle, low = [
        jnp.dot(term, matrix, preferred_element_type=jnp.float32) for term in bfloat16_terms(natural)
    ]
    turned = (high + (middle + low)) * jnp.float32(1.0 / ROT)
    for half in range(HALVES):
        at = pl.ds(half, blocks, stride=HALVES)
        part = turned[:, half * QGROUP : (half + 1) * QGROUP]
        out_ref[at, :] = jnp.where(sign_ref[at, :] == 0, part, -part)


def finish(parts, signs):
    rows = signs.shape[0]
    return pl.pallas_call(
        finish_kernel,
        out_shape=[
            jax.ShapeDtypeStruct((rows, LANES), jnp.float32),
            jax.ShapeDtypeStruct((1, rows), jnp.float32),
        ],
        compiler_params=pltpu.CompilerParams(vmem_limit_bytes=SUM_VMEM_LIMIT),
        name="sum_unrotate",
    )(signs, *parts)


def shards(partials, signs):
    length = partials.shape[-1]
    members = lax.axis_size("local")
    groups = lax.axis_size("node")
    layout = Layout(length, members, groups)
    half = layout.half

    def swap(part, step):
        pairs = []
        for source in range(members):
            first, index = source // half * half, source % half
            pairs.append((source, first + partner(index, step, half)))
        return lax.ppermute(part, "local", pairs)

    def share(parts):
        moved = []
        for step in range(groups - 1, 0, -1):
            pairs = [(source, partner(source, step, groups)) for source in range(groups)]
            moved.append(lax.ppermute(parts[step], "node", pairs))
        return moved + [parts[0]]

    values, sign_rows = partials.reshape(1, length), signs.reshape(length // LANES, LANES)
    counterparts = [(member, (member + half) % members) for member in range(members)]
    slow = half // 2
    others = [step for step in range(half - 1, 0, -1) if step != slow]
    order = others[:1] + [slow] + others[1:] + [0]
    last = order[-2]
    outs = rotate(values, sign_rows, layout, True, order, order[:-1])
    far = {step: [outs.pop(0), outs.pop(0)] for step in order[:-1]}
    far[0] = outs
    for part in range(HALVES):
        for step in order[:-1]:
            far[step][part] = swap(far[step][part], step)
    (part,) = rotate(values, sign_rows, layout, False, [slow], after=far[0])
    first, (part,) = far_sum([far[step][0] for step in order], layout, 0, [part])
    across = [lax.ppermute(first, "local", counterparts)]
    near = {slow: swap(part, slow)}
    second, _ = far_sum([far[step][-1] for step in order], layout, 1, [], [first, part])
    across.append(lax.ppermute(second, "local", counterparts))
    *outs, own_signs = rotate(values, sign_rows, layout, False, others + [0], signed_out=True, after=[second])
    for step, part in zip(others + [0], outs):
        near[step] = swap(part, step) if step else part
    reduced, rotated_max = finish(share(group_sum([near[step] for step in order], across, layout)), own_signs)
    return (reduced.reshape(-1), rotated_max.reshape(-1))


def solution(mesh):
    in_specs = (P("node", "local", None), P())
    out_specs = (P(("node", "local")), P(("node", "local")))
    return jax.shard_map(shards, mesh=mesh, in_specs=in_specs, out_specs=out_specs, check_vma=False)
```

```python
import functools
import jax
import jax.numpy as jnp
from jax import lax
from jax.experimental import pallas as pl
from jax.experimental.pallas import tpu as pltpu
from jax.sharding import PartitionSpec as P

ROT = 256
QGROUP = 128
HALVES = ROT // QGROUP
LANES = 128
VMEM_LIMIT = 50 * 1024 * 1024
SUM_VMEM_LIMIT = 24 * 1024 * 1024
PIECES = 8


def sylvester():
    row = lax.broadcasted_iota(jnp.int32, (ROT, ROT), 0)
    column = lax.broadcasted_iota(jnp.int32, (ROT, ROT), 1)
    parity = lax.population_count(row & column) & 1
    return (1 - 2 * parity).astype(jnp.float32).astype(jnp.bfloat16)


def partner(index, step, count):
    if count & (count - 1) == 0:
        return index ^ step
    return (index + step) % count


def leading_power(x, factor):
    q = x * jnp.float32((2.0**23 + 1.0) * factor)
    return q - q * jnp.float32(1.0 - 2.0**-24)


def recode(values):
    magnitude = jnp.abs(values)
    largest = jnp.max(magnitude, axis=-2, keepdims=True)
    least = jnp.clip(largest, 2.0**-30, 2.0**30) * jnp.float32(2.0**-13)
    shift = leading_power(jnp.maximum(magnitude, least), 2.0**20)
    nearest = (magnitude + shift) - shift
    rest = magnitude - nearest
    coded = jnp.where(rest == shift * jnp.float32(2.0**-24), magnitude + rest, nearest)
    return jnp.where(values < 0.0, -coded, coded)


class Layout:
    def __init__(self, length, members, groups):
        self.members = members
        self.groups = groups
        self.half = members // 2
        self.portion = length // (members * groups)
        self.rows = self.portion // LANES
        self.blocks = self.portion // ROT
        self.together = 1
        if self.blocks < LANES and LANES % self.blocks == 0 and groups % (LANES // self.blocks) == 0:
            self.together = LANES // self.blocks
        self.units = groups // self.together
        self.columns = self.together * self.blocks

    def shape(self):
        return (self.units, QGROUP, self.columns)

    def runs(self, steps, inner):
        half = self.half
        if half & (half - 1) or len(steps) == half:
            return [(0, half)]
        low = 1
        while low < half and all(step in steps for step in range(2 * low)):
            low *= 2
        runs = [(inner // low * low, low)] if 0 in steps else []
        count = low if 0 in steps else 1
        while count < half:
            present = [step for step in range(count, 2 * count) if step in steps]
            if len(present) == count:
                runs.append(((inner ^ count) // count * count, count))
            else:
                runs += [(inner ^ step, 1) for step in present]
            count *= 2
        return runs

    def batch(self, steps):
        batch = min(self.units, max(1, PIECES // len(steps)))
        return batch if self.units % batch == 0 else 1


def rotate_kernel(layout, other, steps, parts, signed_out, extra, values_ref, signs_ref, *refs):
    values, flips, turned, matrix, value_sems, sign_sems = refs[-6:]
    out_refs = refs[extra:-6]
    half, portion, rows = layout.half, layout.portion, layout.rows
    node = lax.axis_index("node")
    member = lax.axis_index("local")
    inner = lax.rem(member, half)
    first = half - (member - inner) if other else member - inner
    runs, batch = layout.runs(steps, inner), layout.batch(steps)

    def fetches(unit):
        copies = []
        for part in range(layout.together):
            section = partner(node, unit * layout.together + part, layout.groups) * layout.members + first
            for index, (owner, count) in enumerate(runs):
                place = section + owner
                copies.append(
                    pltpu.make_async_copy(
                        values_ref.at[:, pl.ds(pl.multiple_of(place * portion, portion), count * portion)],
                        values.at[unit, part, :, pl.ds(pl.multiple_of(owner * portion, portion), count * portion)],
                        value_sems.at[unit, part, index],
                    )
                )
                copies.append(
                    pltpu.make_async_copy(
                        signs_ref.at[pl.ds(pl.multiple_of(place * rows, rows), count * rows), :],
                        flips.at[unit, part, pl.ds(pl.multiple_of(owner * rows, rows), count * rows), :],
                        sign_sems.at[unit, part, index],
                    )
                )
        return copies

    for unit in range(layout.units):
        for copy in fetches(unit):
            copy.start()
    matrix[...] = sylvester()

    def body(turn, carry):
        for index in range(batch):
            for copy in fetches(turn * batch + index):
                copy.wait()
        for index, (position, step) in [(i, p) for i in range(batch) for p in enumerate(steps)]:
            unit = turn * batch + index
            slot = turned.at[index * len(steps) + position]
            owner = partner(inner, step, half)
            at = pl.ds(pl.multiple_of(owner * portion, portion), portion)
            at_rows = pl.ds(pl.multiple_of(owner * rows, rows), rows)
            for part in range(layout.together):
                wide = values[unit, part, :, at].astype(jnp.float32).reshape(rows, LANES)
                slot[part * rows : (part + 1) * rows] = jnp.where(flips[unit, part, at_rows, :] == 0, wide, -wide)
            halves = [slot[pl.ds(part, layout.columns, stride=HALVES), :] for part in range(HALVES)]
            signed = jnp.concatenate(halves, axis=1).astype(jnp.bfloat16)
            wanted = parts[position]
            lowest = wanted[0] * QGROUP
            rotated = lax.dot_general(
                matrix[lowest : lowest + len(wanted) * QGROUP],
                signed,
                (((1,), (1,)), ((), ())),
                preferred_element_type=jnp.float32,
            )
            for part in range(len(wanted)):
                rows_of = slice(part * QGROUP, (part + 1) * QGROUP)
                out_refs[position][unit, rows_of] = recode(rotated[rows_of]).astype(jnp.bfloat16)
        return carry

    lax.fori_loop(0, layout.units // batch, body, 0)
    if signed_out:
        out_refs[-1][...] = flips[0, 0, pl.ds(pl.multiple_of(inner * rows, rows), rows), :]


def rotate(values, signs, layout, other, steps, parts, signed_out=False, after=()):
    half, units, columns = layout.half, layout.units, layout.columns
    batch = layout.batch(steps)
    runs = len(layout.runs(steps, 0))
    entries = len(steps) * layout.groups * layout.portion
    outs = [jax.ShapeDtypeStruct((units, len(wanted) * QGROUP, columns), jnp.bfloat16) for wanted in parts]
    if signed_out:
        outs.append(jax.ShapeDtypeStruct((layout.rows, LANES), jnp.int32))
    return list(
        pl.pallas_call(
            functools.partial(rotate_kernel, layout, other, steps, parts, signed_out, len(after)),
            in_specs=[pl.BlockSpec(memory_space=pltpu.HBM)] * 2 + [pl.BlockSpec(memory_space=pl.ANY)] * len(after),
            out_specs=[pl.BlockSpec(memory_space=pltpu.VMEM)] * len(outs),
            out_shape=outs,
            scratch_shapes=[
                pltpu.VMEM((units, layout.together, 1, half * layout.portion), jnp.bfloat16),
                pltpu.VMEM((units, layout.together, half * layout.rows, LANES), jnp.int32),
                pltpu.VMEM((batch * len(steps), layout.together * layout.rows, LANES), jnp.float32),
                pltpu.VMEM((ROT, ROT), jnp.bfloat16),
                pltpu.SemaphoreType.DMA((units, layout.together, runs)),
                pltpu.SemaphoreType.DMA((units, layout.together, runs)),
            ],
            compiler_params=pltpu.CompilerParams(vmem_limit_bytes=VMEM_LIMIT),
            cost_estimate=pl.CostEstimate(flops=2 * entries * ROT, bytes_accessed=10 * entries, transcendentals=0),
            name="rotate_code",
        )(values, signs, *after)
    )


def add_all(arrays):
    total = arrays[0].astype(jnp.float32)
    for array in arrays[1:]:
        total = total + array.astype(jnp.float32)
    return total


def far_sum_kernel(part, count, *refs):
    arrays = []
    for ref in refs[:count]:
        cut = ref.shape[1] == QGROUP
        arrays.append(ref[...] if cut else ref[:, part * QGROUP : (part + 1) * QGROUP])
    refs[-1][...] = add_all(arrays)


def far_sum(parts, layout, part, after=()):
    size = QGROUP * layout.units * layout.columns
    return pl.pallas_call(
        functools.partial(far_sum_kernel, part, len(parts)),
        in_specs=[pl.BlockSpec(memory_space=pltpu.VMEM)] * len(parts)
        + [pl.BlockSpec(memory_space=pl.ANY)] * len(after),
        out_specs=pl.BlockSpec(memory_space=pltpu.VMEM),
        out_shape=jax.ShapeDtypeStruct(layout.shape(), jnp.float32),
        compiler_params=pltpu.CompilerParams(vmem_limit_bytes=SUM_VMEM_LIMIT),
        cost_estimate=pl.CostEstimate(
            flops=2 * len(parts) * size, bytes_accessed=(2 * len(parts) + 4) * size, transcendentals=0
        ),
        name="far_sum",
    )(*parts, *after)


def group_sum_kernel(layout, *refs):
    across_refs, near_refs, out_refs = refs[:HALVES], refs[HALVES : HALVES + layout.half], refs[HALVES + layout.half :]
    for half, across_ref in enumerate(across_refs):
        near = [ref[:, half * QGROUP : (half + 1) * QGROUP] for ref in near_refs]
        first = recode(add_all(near + [across_ref[...]])).astype(jnp.bfloat16)
        for section, out_ref in enumerate(out_refs):
            at = section % layout.together * layout.blocks
            out_ref[half] = first[section // layout.together, :, at : at + layout.blocks]


def group_sum(near, across, layout):
    size = near[0].size
    return pl.pallas_call(
        functools.partial(group_sum_kernel, layout),
        out_shape=[jax.ShapeDtypeStruct((HALVES, QGROUP, layout.blocks), jnp.bfloat16)] * layout.groups,
        compiler_params=pltpu.CompilerParams(vmem_limit_bytes=SUM_VMEM_LIMIT),
        cost_estimate=pl.CostEstimate(
            flops=30 * size, bytes_accessed=2 * (layout.half + 3) * size, transcendentals=0
        ),
        name="group_sum_code",
    )(*across, *near)


def bfloat16_terms(values):
    terms = []
    for _ in range(3):
        terms.append(values.astype(jnp.bfloat16))
        values = values - terms[-1].astype(jnp.float32)
    return terms


def finish_kernel(sign_ref, *refs):
    out_ref, max_ref = refs[-2:]
    second = [add_all([ref[half] for ref in refs[:-2]]) for half in range(HALVES)]
    blocks = second[0].shape[1]
    natural = jnp.concatenate([part.T for part in second], axis=1)
    block = lax.broadcasted_iota(jnp.int32, (blocks, HALVES * blocks), 0)
    lane = lax.broadcasted_iota(jnp.int32, (blocks, HALVES * blocks), 1)
    largest = jnp.zeros((1, HALVES * blocks), jnp.float32)
    for half in range(HALVES):
        peak = jnp.max(jnp.abs(natural[:, half * QGROUP : (half + 1) * QGROUP]), axis=1, keepdims=True)
        chosen = jnp.where(lane == HALVES * block + half, peak, 0.0)
        largest = jnp.maximum(largest, jnp.max(chosen, axis=0, keepdims=True))
    max_ref[...] = largest * jnp.float32(ROT**-0.5)
    matrix = sylvester()
    high, middle, low = [
        jnp.dot(term, matrix, preferred_element_type=jnp.float32) for term in bfloat16_terms(natural)
    ]
    turned = (high + (middle + low)) * jnp.float32(1.0 / ROT)
    for half in range(HALVES):
        at = pl.ds(half, blocks, stride=HALVES)
        part = turned[:, half * QGROUP : (half + 1) * QGROUP]
        out_ref[at, :] = jnp.where(sign_ref[at, :] == 0, part, -part)


def finish(parts, signs):
    rows = signs.shape[0]
    return pl.pallas_call(
        finish_kernel,
        out_shape=[
            jax.ShapeDtypeStruct((rows, LANES), jnp.float32),
            jax.ShapeDtypeStruct((1, rows), jnp.float32),
        ],
        compiler_params=pltpu.CompilerParams(vmem_limit_bytes=SUM_VMEM_LIMIT),
        name="sum_unrotate",
    )(signs, *parts)


def shards(partials, signs):
    length = partials.shape[-1]
    members = lax.axis_size("local")
    groups = lax.axis_size("node")
    layout = Layout(length, members, groups)
    half = layout.half

    def swap(part, step):
        pairs = []
        for source in range(members):
            first, index = source // half * half, source % half
            pairs.append((source, first + partner(index, step, half)))
        return lax.ppermute(part, "local", pairs)

    def share(parts):
        moved = []
        for step in range(groups - 1, 0, -1):
            pairs = [(source, partner(source, step, groups)) for source in range(groups)]
            moved.append(lax.ppermute(parts[step], "node", pairs))
        return moved + [parts[0]]

    values, sign_rows = partials.reshape(1, length), signs.reshape(length // LANES, LANES)
    counterparts = [(member, (member + half) % members) for member in range(members)]
    slow = half // 2
    others = [step for step in range(half - 1, 0, -1) if step != slow]
    order = others[:1] + [slow] + others[1:]
    whole = tuple(range(HALVES))
    far0 = rotate(values, sign_rows, layout, True, order, [(0,)] * len(order))
    *far1, own = rotate(
        values, sign_rows, layout, True, order + [0], [(1,)] * len(order) + [whole], after=far0
    )
    far0 = [swap(part, step) for step, part in zip(order, far0)] + [own]
    early = far1
    (near_slow,) = rotate(values, sign_rows, layout, False, [slow], [whole], after=early)
    first = far_sum(far0, layout, 0, [near_slow])
    across = [lax.ppermute(first, "local", counterparts)]
    far1 = [swap(part, step) for step, part in zip(order, far1)] + [own]
    second = far_sum(far1, layout, 1, [first, near_slow])
    across.append(lax.ppermute(second, "local", counterparts))
    *outs, own_signs = rotate(
        values, sign_rows, layout, False, others + [0], [whole] * (len(others) + 1), signed_out=True, after=[second]
    )
    near = {step: swap(part, step) if step else part for step, part in zip(others + [0], outs)}
    near[slow] = swap(near_slow, slow)
    reduced, rotated_max = finish(share(group_sum([near[step] for step in order + [0]], across, layout)), own_signs)
    return (reduced.reshape(-1), rotated_max.reshape(-1))


def solution(mesh):
    in_specs = (P("node", "local", None), P())
    out_specs = (P(("node", "local")), P(("node", "local")))
    return jax.shard_map(shards, mesh=mesh, in_specs=in_specs, out_specs=out_specs, check_vma=False)
```

```python
import functools
import jax
import jax.numpy as jnp
from jax import lax
from jax.experimental import pallas as pl
from jax.experimental.pallas import tpu as pltpu
from jax.sharding import PartitionSpec as P

ROT = 256
QGROUP = 128
HALVES = ROT // QGROUP
LANES = 128
VMEM_LIMIT = 50 * 1024 * 1024
SUM_VMEM_LIMIT = 24 * 1024 * 1024
PIECES = 8


def sylvester():
    row = lax.broadcasted_iota(jnp.int32, (ROT, ROT), 0)
    column = lax.broadcasted_iota(jnp.int32, (ROT, ROT), 1)
    parity = lax.population_count(row & column) & 1
    return (1 - 2 * parity).astype(jnp.float32).astype(jnp.bfloat16)


def partner(index, step, count):
    if count & (count - 1) == 0:
        return index ^ step
    return (index + step) % count


def leading_power(x, factor):
    q = x * jnp.float32((2.0**23 + 1.0) * factor)
    return q - q * jnp.float32(1.0 - 2.0**-24)


def recode(values):
    magnitude = jnp.abs(values)
    largest = jnp.max(magnitude, axis=-2, keepdims=True)
    least = jnp.clip(largest, 2.0**-30, 2.0**30) * jnp.float32(2.0**-13)
    shift = leading_power(jnp.maximum(magnitude, least), 2.0**20)
    nearest = (magnitude + shift) - shift
    rest = magnitude - nearest
    coded = jnp.where(rest == shift * jnp.float32(2.0**-24), magnitude + rest, nearest)
    return jnp.where(values < 0.0, -coded, coded)


class Layout:
    def __init__(self, length, members, groups):
        self.members = members
        self.groups = groups
        self.half = members // 2
        self.portion = length // (members * groups)
        self.rows = self.portion // LANES
        self.blocks = self.portion // ROT
        self.together = 1
        if self.blocks < LANES and LANES % self.blocks == 0 and groups % (LANES // self.blocks) == 0:
            self.together = LANES // self.blocks
        self.units = groups // self.together
        self.columns = self.together * self.blocks

    def shape(self):
        return (self.units, QGROUP, self.columns)

    def runs(self, steps, inner):
        half = self.half
        if half & (half - 1) or len(steps) == half:
            return [(0, half)]
        low = 1
        while low < half and all(step in steps for step in range(2 * low)):
            low *= 2
        runs = [(inner // low * low, low)] if 0 in steps else []
        count = low if 0 in steps else 1
        while count < half:
            present = [step for step in range(count, 2 * count) if step in steps]
            if len(present) == count:
                runs.append(((inner ^ count) // count * count, count))
            else:
                runs += [(inner ^ step, 1) for step in present]
            count *= 2
        return runs

    def batch(self, steps):
        batch = min(self.units, max(1, PIECES // len(steps)))
        return batch if self.units % batch == 0 else 1


def rotate_kernel(layout, other, steps, parts, signed_out, extra, values_ref, signs_ref, *refs):
    values, flips, turned, matrix, value_sems, sign_sems = refs[-6:]
    out_refs = refs[extra:-6]
    half, portion, rows = layout.half, layout.portion, layout.rows
    node = lax.axis_index("node")
    member = lax.axis_index("local")
    inner = lax.rem(member, half)
    first = half - (member - inner) if other else member - inner
    runs, batch = layout.runs(steps, inner), layout.batch(steps)

    def fetches(unit):
        copies = []
        for part in range(layout.together):
            section = partner(node, unit * layout.together + part, layout.groups) * layout.members + first
            for index, (owner, count) in enumerate(runs):
                place = section + owner
                copies.append(
                    pltpu.make_async_copy(
                        values_ref.at[:, pl.ds(pl.multiple_of(place * portion, portion), count * portion)],
                        values.at[unit, part, :, pl.ds(pl.multiple_of(owner * portion, portion), count * portion)],
                        value_sems.at[unit, part, index],
                    )
                )
                copies.append(
                    pltpu.make_async_copy(
                        signs_ref.at[pl.ds(pl.multiple_of(place * rows, rows), count * rows), :],
                        flips.at[unit, part, pl.ds(pl.multiple_of(owner * rows, rows), count * rows), :],
                        sign_sems.at[unit, part, index],
                    )
                )
        return copies

    for unit in range(layout.units):
        for copy in fetches(unit):
            copy.start()
    matrix[...] = sylvester()

    def body(turn, carry):
        for index in range(batch):
            for copy in fetches(turn * batch + index):
                copy.wait()
        for index, (position, step) in [(i, p) for i in range(batch) for p in enumerate(steps)]:
            unit = turn * batch + index
            slot = turned.at[index * len(steps) + position]
            owner = partner(inner, step, half)
            at = pl.ds(pl.multiple_of(owner * portion, portion), portion)
            at_rows = pl.ds(pl.multiple_of(owner * rows, rows), rows)
            for part in range(layout.together):
                wide = values[unit, part, :, at].astype(jnp.float32).reshape(rows, LANES)
                slot[part * rows : (part + 1) * rows] = jnp.where(flips[unit, part, at_rows, :] == 0, wide, -wide)
            halves = [slot[pl.ds(part, layout.columns, stride=HALVES), :] for part in range(HALVES)]
            signed = jnp.concatenate(halves, axis=1).astype(jnp.bfloat16)
            wanted = parts[position]
            lowest = wanted[0] * QGROUP
            rotated = lax.dot_general(
                matrix[lowest : lowest + len(wanted) * QGROUP],
                signed,
                (((1,), (1,)), ((), ())),
                preferred_element_type=jnp.float32,
            )
            for part in range(len(wanted)):
                rows_of = slice(part * QGROUP, (part + 1) * QGROUP)
                out_refs[position][unit, rows_of] = recode(rotated[rows_of]).astype(jnp.bfloat16)
        return carry

    lax.fori_loop(0, layout.units // batch, body, 0)
    if signed_out:
        out_refs[-1][...] = flips[0, 0, pl.ds(pl.multiple_of(inner * rows, rows), rows), :]


def rotate(values, signs, layout, other, steps, parts, signed_out=False, after=()):
    half, units, columns = layout.half, layout.units, layout.columns
    batch = layout.batch(steps)
    runs = len(layout.runs(steps, 0))
    entries = len(steps) * layout.groups * layout.portion
    outs = [jax.ShapeDtypeStruct((units, len(wanted) * QGROUP, columns), jnp.bfloat16) for wanted in parts]
    if signed_out:
        outs.append(jax.ShapeDtypeStruct((layout.rows, LANES), jnp.int32))
    return list(
        pl.pallas_call(
            functools.partial(rotate_kernel, layout, other, steps, parts, signed_out, len(after)),
            in_specs=[pl.BlockSpec(memory_space=pltpu.HBM)] * 2 + [pl.BlockSpec(memory_space=pl.ANY)] * len(after),
            out_specs=[pl.BlockSpec(memory_space=pltpu.VMEM)] * len(outs),
            out_shape=outs,
            scratch_shapes=[
                pltpu.VMEM((units, layout.together, 1, half * layout.portion), jnp.bfloat16),
                pltpu.VMEM((units, layout.together, half * layout.rows, LANES), jnp.int32),
                pltpu.VMEM((batch * len(steps), layout.together * layout.rows, LANES), jnp.float32),
                pltpu.VMEM((ROT, ROT), jnp.bfloat16),
                pltpu.SemaphoreType.DMA((units, layout.together, runs)),
                pltpu.SemaphoreType.DMA((units, layout.together, runs)),
            ],
            compiler_params=pltpu.CompilerParams(vmem_limit_bytes=VMEM_LIMIT),
            cost_estimate=pl.CostEstimate(flops=2 * entries * ROT, bytes_accessed=10 * entries, transcendentals=0),
            name="rotate_code",
        )(values, signs, *after)
    )


def add_all(arrays):
    total = arrays[0].astype(jnp.float32)
    for array in arrays[1:]:
        total = total + array.astype(jnp.float32)
    return total


def far_sum_kernel(part, count, *refs):
    arrays = []
    for ref in refs[:count]:
        cut = ref.shape[1] == QGROUP
        arrays.append(ref[...] if cut else ref[:, part * QGROUP : (part + 1) * QGROUP])
    refs[-1][...] = add_all(arrays)


def far_sum(parts, layout, part, after=()):
    size = QGROUP * layout.units * layout.columns
    return pl.pallas_call(
        functools.partial(far_sum_kernel, part, len(parts)),
        in_specs=[pl.BlockSpec(memory_space=pltpu.VMEM)] * len(parts)
        + [pl.BlockSpec(memory_space=pl.ANY)] * len(after),
        out_specs=pl.BlockSpec(memory_space=pltpu.VMEM),
        out_shape=jax.ShapeDtypeStruct(layout.shape(), jnp.float32),
        compiler_params=pltpu.CompilerParams(vmem_limit_bytes=SUM_VMEM_LIMIT),
        cost_estimate=pl.CostEstimate(
            flops=2 * len(parts) * size, bytes_accessed=(2 * len(parts) + 4) * size, transcendentals=0
        ),
        name="far_sum",
    )(*parts, *after)


def group_sum_kernel(layout, *refs):
    across_refs, near_refs, out_refs = refs[:HALVES], refs[HALVES : HALVES + layout.half], refs[HALVES + layout.half :]
    for half, across_ref in enumerate(across_refs):
        near = [ref[:, half * QGROUP : (half + 1) * QGROUP] for ref in near_refs]
        first = recode(add_all(near + [across_ref[...]])).astype(jnp.bfloat16)
        for section, out_ref in enumerate(out_refs):
            at = section % layout.together * layout.blocks
            out_ref[half] = first[section // layout.together, :, at : at + layout.blocks]


def group_sum(near, across, layout):
    size = near[0].size
    return pl.pallas_call(
        functools.partial(group_sum_kernel, layout),
        out_shape=[jax.ShapeDtypeStruct((HALVES, QGROUP, layout.blocks), jnp.bfloat16)] * layout.groups,
        compiler_params=pltpu.CompilerParams(vmem_limit_bytes=SUM_VMEM_LIMIT),
        cost_estimate=pl.CostEstimate(
            flops=30 * size, bytes_accessed=2 * (layout.half + 3) * size, transcendentals=0
        ),
        name="group_sum_code",
    )(*across, *near)


def bfloat16_terms(values):
    terms = []
    for _ in range(3):
        terms.append(values.astype(jnp.bfloat16))
        values = values - terms[-1].astype(jnp.float32)
    return terms


def finish_kernel(sign_ref, *refs):
    out_ref, max_ref = refs[-2:]
    second = [add_all([ref[half] for ref in refs[:-2]]) for half in range(HALVES)]
    blocks = second[0].shape[1]
    natural = jnp.concatenate([part.T for part in second], axis=1)
    block = lax.broadcasted_iota(jnp.int32, (blocks, HALVES * blocks), 0)
    lane = lax.broadcasted_iota(jnp.int32, (blocks, HALVES * blocks), 1)
    largest = jnp.zeros((1, HALVES * blocks), jnp.float32)
    for half in range(HALVES):
        peak = jnp.max(jnp.abs(natural[:, half * QGROUP : (half + 1) * QGROUP]), axis=1, keepdims=True)
        chosen = jnp.where(lane == HALVES * block + half, peak, 0.0)
        largest = jnp.maximum(largest, jnp.max(chosen, axis=0, keepdims=True))
    max_ref[...] = largest * jnp.float32(ROT**-0.5)
    matrix = sylvester()
    high, middle, low = [
        jnp.dot(term, matrix, preferred_element_type=jnp.float32) for term in bfloat16_terms(natural)
    ]
    turned = (high + (middle + low)) * jnp.float32(1.0 / ROT)
    for half in range(HALVES):
        at = pl.ds(half, blocks, stride=HALVES)
        part = turned[:, half * QGROUP : (half + 1) * QGROUP]
        out_ref[at, :] = jnp.where(sign_ref[at, :] == 0, part, -part)


def finish(parts, signs):
    rows = signs.shape[0]
    return pl.pallas_call(
        finish_kernel,
        out_shape=[
            jax.ShapeDtypeStruct((rows, LANES), jnp.float32),
            jax.ShapeDtypeStruct((1, rows), jnp.float32),
        ],
        compiler_params=pltpu.CompilerParams(vmem_limit_bytes=SUM_VMEM_LIMIT),
        name="sum_unrotate",
    )(signs, *parts)


def shards(partials, signs):
    length = partials.shape[-1]
    members = lax.axis_size("local")
    groups = lax.axis_size("node")
    layout = Layout(length, members, groups)
    half = layout.half

    def swap(part, step):
        pairs = []
        for source in range(members):
            first, index = source // half * half, source % half
            pairs.append((source, first + partner(index, step, half)))
        return lax.ppermute(part, "local", pairs)

    def share(parts):
        moved = []
        for step in range(groups - 1, 0, -1):
            pairs = [(source, partner(source, step, groups)) for source in range(groups)]
            moved.append(lax.ppermute(parts[step], "node", pairs))
        return moved + [parts[0]]

    values, sign_rows = partials.reshape(1, length), signs.reshape(length // LANES, LANES)
    counterparts = [(member, (member + half) % members) for member in range(members)]
    slow = half // 2
    others = [step for step in range(half - 1, 0, -1) if step != slow]
    order = others[:1] + [slow] + others[1:]
    whole = tuple(range(HALVES))
    far0 = rotate(values, sign_rows, layout, True, order, [(0,)] * len(order))
    *far1, own = rotate(
        values, sign_rows, layout, True, order + [0], [(1,)] * len(order) + [whole], after=far0
    )
    far0 = [swap(part, step) for step, part in zip(order, far0)] + [own]
    early = far1
    first = far_sum(far0, layout, 0, [*early])
    across = [lax.ppermute(first, "local", counterparts)]
    (near_slow,) = rotate(values, sign_rows, layout, False, [slow], [whole], after=[first])
    far1 = [swap(part, step) for step, part in zip(order, far1)] + [own]
    second = far_sum(far1, layout, 1, [near_slow])
    across.append(lax.ppermute(second, "local", counterparts))
    *outs, own_signs = rotate(
        values, sign_rows, layout, False, others + [0], [whole] * (len(others) + 1), signed_out=True, after=[second]
    )
    near = {step: swap(part, step) if step else part for step, part in zip(others + [0], outs)}
    near[slow] = swap(near_slow, slow)
    reduced, rotated_max = finish(share(group_sum([near[step] for step in order + [0]], across, layout)), own_signs)
    return (reduced.reshape(-1), rotated_max.reshape(-1))


def solution(mesh):
    in_specs = (P("node", "local", None), P())
    out_specs = (P(("node", "local")), P(("node", "local")))
    return jax.shard_map(shards, mesh=mesh, in_specs=in_specs, out_specs=out_specs, check_vma=False)
```

```python
import functools
import jax
import jax.numpy as jnp
from jax import lax
from jax.experimental import pallas as pl
from jax.experimental.pallas import tpu as pltpu
from jax.sharding import PartitionSpec as P

ROT = 256
QGROUP = 128
HALVES = ROT // QGROUP
LANES = 128
VMEM_LIMIT = 50 * 1024 * 1024
SUM_VMEM_LIMIT = 24 * 1024 * 1024
PIECES = 8


def sylvester():
    row = lax.broadcasted_iota(jnp.int32, (ROT, ROT), 0)
    column = lax.broadcasted_iota(jnp.int32, (ROT, ROT), 1)
    parity = lax.population_count(row & column) & 1
    return (1 - 2 * parity).astype(jnp.float32).astype(jnp.bfloat16)


def partner(index, step, count):
    if count & (count - 1) == 0:
        return index ^ step
    return (index + step) % count


def leading_power(x, factor):
    q = x * jnp.float32((2.0**23 + 1.0) * factor)
    return q - q * jnp.float32(1.0 - 2.0**-24)


def recode(values):
    magnitude = jnp.abs(values)
    largest = jnp.max(magnitude, axis=-2, keepdims=True)
    least = jnp.clip(largest, 2.0**-30, 2.0**30) * jnp.float32(2.0**-13)
    shift = leading_power(jnp.maximum(magnitude, least), 2.0**20)
    nearest = (magnitude + shift) - shift
    rest = magnitude - nearest
    coded = jnp.where(rest == shift * jnp.float32(2.0**-24), magnitude + rest, nearest)
    return jnp.where(values < 0.0, -coded, coded)


class Layout:
    def __init__(self, length, members, groups):
        self.members = members
        self.groups = groups
        self.half = members // 2
        self.portion = length // (members * groups)
        self.rows = self.portion // LANES
        self.blocks = self.portion // ROT
        self.together = 1
        if self.blocks < LANES and LANES % self.blocks == 0 and groups % (LANES // self.blocks) == 0:
            self.together = LANES // self.blocks
        self.units = groups // self.together
        self.columns = self.together * self.blocks

    def shape(self):
        return (self.units, QGROUP, self.columns)

    def runs(self, steps, inner):
        half = self.half
        if half & (half - 1) or len(set(steps)) == half:
            return [(0, half)]
        low = 1
        while low < half and all(step in steps for step in range(2 * low)):
            low *= 2
        runs = [(inner // low * low, low)] if 0 in steps else []
        count = low if 0 in steps else 1
        while count < half:
            present = [step for step in range(count, 2 * count) if step in steps]
            if len(present) == count:
                runs.append(((inner ^ count) // count * count, count))
            else:
                runs += [(inner ^ step, 1) for step in present]
            count *= 2
        return runs

    def batch(self, steps):
        batch = min(self.units, max(1, PIECES // len(steps)))
        return batch if self.units % batch == 0 else 1


def rotate_kernel(layout, other, steps, parts, signed_out, extra, values_ref, signs_ref, *refs):
    values, flips, turned, matrix, value_sems, sign_sems = refs[-6:]
    out_refs = refs[extra:-6]
    half, portion, rows = layout.half, layout.portion, layout.rows
    node = lax.axis_index("node")
    member = lax.axis_index("local")
    inner = lax.rem(member, half)
    first = half - (member - inner) if other else member - inner
    runs, batch = layout.runs(steps, inner), layout.batch(steps)

    def fetches(unit):
        copies = []
        for part in range(layout.together):
            section = partner(node, unit * layout.together + part, layout.groups) * layout.members + first
            for index, (owner, count) in enumerate(runs):
                place = section + owner
                copies.append(
                    pltpu.make_async_copy(
                        values_ref.at[:, pl.ds(pl.multiple_of(place * portion, portion), count * portion)],
                        values.at[unit, part, :, pl.ds(pl.multiple_of(owner * portion, portion), count * portion)],
                        value_sems.at[unit, part, index],
                    )
                )
                copies.append(
                    pltpu.make_async_copy(
                        signs_ref.at[pl.ds(pl.multiple_of(place * rows, rows), count * rows), :],
                        flips.at[unit, part, pl.ds(pl.multiple_of(owner * rows, rows), count * rows), :],
                        sign_sems.at[unit, part, index],
                    )
                )
        return copies

    for unit in range(layout.units):
        for copy in fetches(unit):
            copy.start()
    matrix[...] = sylvester()

    def body(turn, carry):
        for index in range(batch):
            for copy in fetches(turn * batch + index):
                copy.wait()
        for index, (position, step) in [(i, p) for i in range(batch) for p in enumerate(steps)]:
            unit = turn * batch + index
            slot = turned.at[index * len(steps) + position]
            owner = partner(inner, step, half)
            at = pl.ds(pl.multiple_of(owner * portion, portion), portion)
            at_rows = pl.ds(pl.multiple_of(owner * rows, rows), rows)
            for part in range(layout.together):
                wide = values[unit, part, :, at].astype(jnp.float32).reshape(rows, LANES)
                slot[part * rows : (part + 1) * rows] = jnp.where(flips[unit, part, at_rows, :] == 0, wide, -wide)
            halves = [slot[pl.ds(part, layout.columns, stride=HALVES), :] for part in range(HALVES)]
            signed = jnp.concatenate(halves, axis=1).astype(jnp.bfloat16)
            wanted = parts[position]
            lowest = wanted[0] * QGROUP
            rotated = lax.dot_general(
                matrix[lowest : lowest + len(wanted) * QGROUP],
                signed,
                (((1,), (1,)), ((), ())),
                preferred_element_type=jnp.float32,
            )
            for part in range(len(wanted)):
                rows_of = slice(part * QGROUP, (part + 1) * QGROUP)
                out_refs[position][unit, rows_of] = recode(rotated[rows_of]).astype(jnp.bfloat16)
        return carry

    lax.fori_loop(0, layout.units // batch, body, 0)
    if signed_out:
        out_refs[-1][...] = flips[0, 0, pl.ds(pl.multiple_of(inner * rows, rows), rows), :]


def rotate(values, signs, layout, other, steps, parts, signed_out=False, after=()):
    half, units, columns = layout.half, layout.units, layout.columns
    batch = layout.batch(steps)
    runs = len(layout.runs(steps, 0))
    entries = len(steps) * layout.groups * layout.portion
    outs = [jax.ShapeDtypeStruct((units, len(wanted) * QGROUP, columns), jnp.bfloat16) for wanted in parts]
    if signed_out:
        outs.append(jax.ShapeDtypeStruct((layout.rows, LANES), jnp.int32))
    return list(
        pl.pallas_call(
            functools.partial(rotate_kernel, layout, other, steps, parts, signed_out, len(after)),
            in_specs=[pl.BlockSpec(memory_space=pltpu.HBM)] * 2 + [pl.BlockSpec(memory_space=pl.ANY)] * len(after),
            out_specs=[pl.BlockSpec(memory_space=pltpu.VMEM)] * len(outs),
            out_shape=outs,
            scratch_shapes=[
                pltpu.VMEM((units, layout.together, 1, half * layout.portion), jnp.bfloat16),
                pltpu.VMEM((units, layout.together, half * layout.rows, LANES), jnp.int32),
                pltpu.VMEM((batch * len(steps), layout.together * layout.rows, LANES), jnp.float32),
                pltpu.VMEM((ROT, ROT), jnp.bfloat16),
                pltpu.SemaphoreType.DMA((units, layout.together, runs)),
                pltpu.SemaphoreType.DMA((units, layout.together, runs)),
            ],
            compiler_params=pltpu.CompilerParams(vmem_limit_bytes=VMEM_LIMIT),
            cost_estimate=pl.CostEstimate(flops=2 * entries * ROT, bytes_accessed=10 * entries, transcendentals=0),
            name="rotate_code",
        )(values, signs, *after)
    )


def add_all(arrays):
    total = arrays[0].astype(jnp.float32)
    for array in arrays[1:]:
        total = total + array.astype(jnp.float32)
    return total


def far_sum_kernel(part, count, *refs):
    arrays = []
    for ref in refs[:count]:
        cut = ref.shape[1] == QGROUP
        arrays.append(ref[...] if cut else ref[:, part * QGROUP : (part + 1) * QGROUP])
    refs[-1][...] = add_all(arrays)


def far_sum(parts, layout, part, after=()):
    size = QGROUP * layout.units * layout.columns
    return pl.pallas_call(
        functools.partial(far_sum_kernel, part, len(parts)),
        in_specs=[pl.BlockSpec(memory_space=pltpu.VMEM)] * len(parts)
        + [pl.BlockSpec(memory_space=pl.ANY)] * len(after),
        out_specs=pl.BlockSpec(memory_space=pltpu.VMEM),
        out_shape=jax.ShapeDtypeStruct(layout.shape(), jnp.float32),
        compiler_params=pltpu.CompilerParams(vmem_limit_bytes=SUM_VMEM_LIMIT),
        cost_estimate=pl.CostEstimate(
            flops=2 * len(parts) * size, bytes_accessed=(2 * len(parts) + 4) * size, transcendentals=0
        ),
        name="far_sum",
    )(*parts, *after)


def group_sum_kernel(layout, *refs):
    across_refs, near_refs, out_refs = refs[:HALVES], refs[HALVES : HALVES + layout.half], refs[HALVES + layout.half :]
    for half, across_ref in enumerate(across_refs):
        near = [ref[:, half * QGROUP : (half + 1) * QGROUP] for ref in near_refs]
        first = recode(add_all(near + [across_ref[...]])).astype(jnp.bfloat16)
        for section, out_ref in enumerate(out_refs):
            at = section % layout.together * layout.blocks
            out_ref[half] = first[section // layout.together, :, at : at + layout.blocks]


def group_sum(near, across, layout):
    size = near[0].size
    return pl.pallas_call(
        functools.partial(group_sum_kernel, layout),
        out_shape=[jax.ShapeDtypeStruct((HALVES, QGROUP, layout.blocks), jnp.bfloat16)] * layout.groups,
        compiler_params=pltpu.CompilerParams(vmem_limit_bytes=SUM_VMEM_LIMIT),
        cost_estimate=pl.CostEstimate(
            flops=30 * size, bytes_accessed=2 * (layout.half + 3) * size, transcendentals=0
        ),
        name="group_sum_code",
    )(*across, *near)


def bfloat16_terms(values):
    terms = []
    for _ in range(3):
        terms.append(values.astype(jnp.bfloat16))
        values = values - terms[-1].astype(jnp.float32)
    return terms


def finish_kernel(sign_ref, *refs):
    out_ref, max_ref = refs[-2:]
    second = [add_all([ref[half] for ref in refs[:-2]]) for half in range(HALVES)]
    blocks = second[0].shape[1]
    natural = jnp.concatenate([part.T for part in second], axis=1)
    block = lax.broadcasted_iota(jnp.int32, (blocks, HALVES * blocks), 0)
    lane = lax.broadcasted_iota(jnp.int32, (blocks, HALVES * blocks), 1)
    largest = jnp.zeros((1, HALVES * blocks), jnp.float32)
    for half in range(HALVES):
        peak = jnp.max(jnp.abs(natural[:, half * QGROUP : (half + 1) * QGROUP]), axis=1, keepdims=True)
        chosen = jnp.where(lane == HALVES * block + half, peak, 0.0)
        largest = jnp.maximum(largest, jnp.max(chosen, axis=0, keepdims=True))
    max_ref[...] = largest * jnp.float32(ROT**-0.5)
    matrix = sylvester()
    high, middle, low = [
        jnp.dot(term, matrix, preferred_element_type=jnp.float32) for term in bfloat16_terms(natural)
    ]
    turned = (high + (middle + low)) * jnp.float32(1.0 / ROT)
    for half in range(HALVES):
        at = pl.ds(half, blocks, stride=HALVES)
        part = turned[:, half * QGROUP : (half + 1) * QGROUP]
        out_ref[at, :] = jnp.where(sign_ref[at, :] == 0, part, -part)


def finish(parts, signs):
    rows = signs.shape[0]
    return pl.pallas_call(
        finish_kernel,
        out_shape=[
            jax.ShapeDtypeStruct((rows, LANES), jnp.float32),
            jax.ShapeDtypeStruct((1, rows), jnp.float32),
        ],
        compiler_params=pltpu.CompilerParams(vmem_limit_bytes=SUM_VMEM_LIMIT),
        name="sum_unrotate",
    )(signs, *parts)


def shards(partials, signs):
    length = partials.shape[-1]
    members = lax.axis_size("local")
    groups = lax.axis_size("node")
    layout = Layout(length, members, groups)
    half = layout.half

    def swap(part, step):
        pairs = []
        for source in range(members):
            first, index = source // half * half, source % half
            pairs.append((source, first + partner(index, step, half)))
        return lax.ppermute(part, "local", pairs)

    def share(parts):
        moved = []
        for step in range(groups - 1, 0, -1):
            pairs = [(source, partner(source, step, groups)) for source in range(groups)]
            moved.append(lax.ppermute(parts[step], "node", pairs))
        return moved + [parts[0]]

    values, sign_rows = partials.reshape(1, length), signs.reshape(length // LANES, LANES)
    counterparts = [(member, (member + half) % members) for member in range(members)]
    slow = half // 2
    others = [step for step in range(half - 1, 0, -1) if step != slow]
    order = others[:1] + [slow] + others[1:]
    whole = tuple(range(HALVES))
    fast = order[-1]
    *far0, half1 = rotate(values, sign_rows, layout, True, order + [slow], [(0,)] * len(order) + [(1,)])
    *far1, own = rotate(
        values, sign_rows, layout, True, others + [0], [(1,)] * len(others) + [whole], after=[*far0, half1]
    )
    far0 = [swap(part, step) for step, part in zip(order, far0)] + [own]
    early = far1
    first = far_sum(far0, layout, 0, [*early])
    across = [lax.ppermute(first, "local", counterparts)]
    middle = [slow] + [fast] * (fast != slow)
    near = rotate(values, sign_rows, layout, False, middle, [whole] * len(middle), after=[first])
    far1 = [swap(part, step) for step, part in zip(others + [slow], far1 + [half1])] + [own]
    second = far_sum(far1, layout, 1, [*near])
    across.append(lax.ppermute(second, "local", counterparts))
    ends = [step for step in others if step not in middle] + [0]
    *outs, own_signs = rotate(
        values, sign_rows, layout, False, ends, [whole] * len(ends), signed_out=True, after=[second]
    )
    near = {step: swap(part, step) if step else part for step, part in zip(middle + ends, near + outs)}
    reduced, rotated_max = finish(share(group_sum([near[step] for step in order + [0]], across, layout)), own_signs)
    return (reduced.reshape(-1), rotated_max.reshape(-1))


def solution(mesh):
    in_specs = (P("node", "local", None), P())
    out_specs = (P(("node", "local")), P(("node", "local")))
    return jax.shard_map(shards, mesh=mesh, in_specs=in_specs, out_specs=out_specs, check_vma=False)
```

```python
import functools
import jax
import jax.numpy as jnp
from jax import lax
from jax.experimental import pallas as pl
from jax.experimental.pallas import tpu as pltpu
from jax.sharding import PartitionSpec as P

ROT = 256
QGROUP = 128
HALVES = ROT // QGROUP
LANES = 128
VMEM_LIMIT = 50 * 1024 * 1024
SUM_VMEM_LIMIT = 24 * 1024 * 1024
PIECES = 8


def sylvester():
    row = lax.broadcasted_iota(jnp.int32, (ROT, ROT), 0)
    column = lax.broadcasted_iota(jnp.int32, (ROT, ROT), 1)
    parity = lax.population_count(row & column) & 1
    return (1 - 2 * parity).astype(jnp.float32).astype(jnp.bfloat16)


def partner(index, step, count):
    if count & (count - 1) == 0:
        return index ^ step
    return (index + step) % count


def leading_power(x, factor):
    q = x * jnp.float32((2.0**23 + 1.0) * factor)
    return q - q * jnp.float32(1.0 - 2.0**-24)


def recode(values):
    magnitude = jnp.abs(values)
    largest = jnp.max(magnitude, axis=-2, keepdims=True)
    least = jnp.clip(largest, 2.0**-30, 2.0**30) * jnp.float32(2.0**-13)
    shift = leading_power(jnp.maximum(magnitude, least), 2.0**20)
    nearest = (magnitude + shift) - shift
    rest = magnitude - nearest
    coded = jnp.where(rest == shift * jnp.float32(2.0**-24), magnitude + rest, nearest)
    return jnp.where(values < 0.0, -coded, coded)


class Layout:
    def __init__(self, length, members, groups):
        self.members = members
        self.groups = groups
        self.half = members // 2
        self.portion = length // (members * groups)
        self.rows = self.portion // LANES
        self.blocks = self.portion // ROT
        self.together = 1
        if self.blocks < LANES and LANES % self.blocks == 0 and groups % (LANES // self.blocks) == 0:
            self.together = LANES // self.blocks
        self.units = groups // self.together
        self.columns = self.together * self.blocks

    def shape(self):
        return (self.units, QGROUP, self.columns)

    def runs(self, steps, inner):
        half = self.half
        if half & (half - 1) or len(set(steps)) == half:
            return [(0, half)]
        low = 1
        while low < half and all(step in steps for step in range(2 * low)):
            low *= 2
        runs = [(inner // low * low, low)] if 0 in steps else []
        count = low if 0 in steps else 1
        while count < half:
            present = [step for step in range(count, 2 * count) if step in steps]
            if len(present) == count:
                runs.append(((inner ^ count) // count * count, count))
            else:
                runs += [(inner ^ step, 1) for step in present]
            count *= 2
        return runs

    def batch(self, steps):
        batch = min(self.units, max(1, PIECES // len(steps)))
        return batch if self.units % batch == 0 else 1


def rotate_kernel(layout, other, steps, parts, signed_out, extra, values_ref, signs_ref, *refs):
    values, flips, turned, matrix, value_sems, sign_sems = refs[-6:]
    out_refs = refs[extra:-6]
    half, portion, rows = layout.half, layout.portion, layout.rows
    node = lax.axis_index("node")
    member = lax.axis_index("local")
    inner = lax.rem(member, half)
    first = half - (member - inner) if other else member - inner
    runs, batch = layout.runs(steps, inner), layout.batch(steps)

    def fetches(unit):
        copies = []
        for part in range(layout.together):
            section = partner(node, unit * layout.together + part, layout.groups) * layout.members + first
            for index, (owner, count) in enumerate(runs):
                place = section + owner
                copies.append(
                    pltpu.make_async_copy(
                        values_ref.at[:, pl.ds(pl.multiple_of(place * portion, portion), count * portion)],
                        values.at[unit, part, :, pl.ds(pl.multiple_of(owner * portion, portion), count * portion)],
                        value_sems.at[unit, part, index],
                    )
                )
                copies.append(
                    pltpu.make_async_copy(
                        signs_ref.at[pl.ds(pl.multiple_of(place * rows, rows), count * rows), :],
                        flips.at[unit, part, pl.ds(pl.multiple_of(owner * rows, rows), count * rows), :],
                        sign_sems.at[unit, part, index],
                    )
                )
        return copies

    for unit in range(layout.units):
        for copy in fetches(unit):
            copy.start()
    matrix[...] = sylvester()

    def body(turn, carry):
        for index in range(batch):
            for copy in fetches(turn * batch + index):
                copy.wait()
        for index, (position, step) in [(i, p) for i in range(batch) for p in enumerate(steps)]:
            unit = turn * batch + index
            slot = turned.at[index * len(steps) + position]
            owner = partner(inner, step, half)
            at = pl.ds(pl.multiple_of(owner * portion, portion), portion)
            at_rows = pl.ds(pl.multiple_of(owner * rows, rows), rows)
            for part in range(layout.together):
                wide = values[unit, part, :, at].astype(jnp.float32).reshape(rows, LANES)
                slot[part * rows : (part + 1) * rows] = jnp.where(flips[unit, part, at_rows, :] == 0, wide, -wide)
            halves = [slot[pl.ds(part, layout.columns, stride=HALVES), :] for part in range(HALVES)]
            signed = jnp.concatenate(halves, axis=1).astype(jnp.bfloat16)
            wanted = parts[position]
            lowest = wanted[0] * QGROUP
            rotated = lax.dot_general(
                matrix[lowest : lowest + len(wanted) * QGROUP],
                signed,
                (((1,), (1,)), ((), ())),
                preferred_element_type=jnp.float32,
            )
            for part in range(len(wanted)):
                rows_of = slice(part * QGROUP, (part + 1) * QGROUP)
                out_refs[position][unit, rows_of] = recode(rotated[rows_of]).astype(jnp.bfloat16)
        return carry

    lax.fori_loop(0, layout.units // batch, body, 0)
    if signed_out:
        out_refs[-1][...] = flips[0, 0, pl.ds(pl.multiple_of(inner * rows, rows), rows), :]


def rotate(values, signs, layout, other, steps, parts, signed_out=False, after=()):
    half, units, columns = layout.half, layout.units, layout.columns
    batch = layout.batch(steps)
    runs = len(layout.runs(steps, 0))
    entries = len(steps) * layout.groups * layout.portion
    outs = [jax.ShapeDtypeStruct((units, len(wanted) * QGROUP, columns), jnp.bfloat16) for wanted in parts]
    if signed_out:
        outs.append(jax.ShapeDtypeStruct((layout.rows, LANES), jnp.int32))
    return list(
        pl.pallas_call(
            functools.partial(rotate_kernel, layout, other, steps, parts, signed_out, len(after)),
            in_specs=[pl.BlockSpec(memory_space=pltpu.HBM)] * 2 + [pl.BlockSpec(memory_space=pl.ANY)] * len(after),
            out_specs=[pl.BlockSpec(memory_space=pltpu.VMEM)] * len(outs),
            out_shape=outs,
            scratch_shapes=[
                pltpu.VMEM((units, layout.together, 1, half * layout.portion), jnp.bfloat16),
                pltpu.VMEM((units, layout.together, half * layout.rows, LANES), jnp.int32),
                pltpu.VMEM((batch * len(steps), layout.together * layout.rows, LANES), jnp.float32),
                pltpu.VMEM((ROT, ROT), jnp.bfloat16),
                pltpu.SemaphoreType.DMA((units, layout.together, runs)),
                pltpu.SemaphoreType.DMA((units, layout.together, runs)),
            ],
            compiler_params=pltpu.CompilerParams(vmem_limit_bytes=VMEM_LIMIT),
            cost_estimate=pl.CostEstimate(flops=2 * entries * ROT, bytes_accessed=10 * entries, transcendentals=0),
            name="rotate_code",
        )(values, signs, *after)
    )


def add_all(arrays):
    total = arrays[0].astype(jnp.float32)
    for array in arrays[1:]:
        total = total + array.astype(jnp.float32)
    return total


def far_sum_kernel(part, count, *refs):
    arrays = []
    for ref in refs[:count]:
        cut = ref.shape[1] == QGROUP
        arrays.append(ref[...] if cut else ref[:, part * QGROUP : (part + 1) * QGROUP])
    refs[-1][...] = add_all(arrays)


def far_sum(parts, layout, part, after=()):
    size = QGROUP * layout.units * layout.columns
    return pl.pallas_call(
        functools.partial(far_sum_kernel, part, len(parts)),
        in_specs=[pl.BlockSpec(memory_space=pltpu.VMEM)] * len(parts)
        + [pl.BlockSpec(memory_space=pl.ANY)] * len(after),
        out_specs=pl.BlockSpec(memory_space=pltpu.VMEM),
        out_shape=jax.ShapeDtypeStruct(layout.shape(), jnp.float32),
        compiler_params=pltpu.CompilerParams(vmem_limit_bytes=SUM_VMEM_LIMIT),
        cost_estimate=pl.CostEstimate(
            flops=2 * len(parts) * size, bytes_accessed=(2 * len(parts) + 4) * size, transcendentals=0
        ),
        name="far_sum",
    )(*parts, *after)


def group_sum_kernel(layout, *refs):
    across_refs, near_refs, out_refs = refs[:HALVES], refs[HALVES : HALVES + layout.half], refs[HALVES + layout.half :]
    for half, across_ref in enumerate(across_refs):
        near = [ref[:, half * QGROUP : (half + 1) * QGROUP] for ref in near_refs]
        first = recode(add_all(near + [across_ref[...]])).astype(jnp.bfloat16)
        for section, out_ref in enumerate(out_refs):
            at = section % layout.together * layout.blocks
            out_ref[half] = first[section // layout.together, :, at : at + layout.blocks]


def group_sum(near, across, layout):
    size = near[0].size
    return pl.pallas_call(
        functools.partial(group_sum_kernel, layout),
        out_shape=[jax.ShapeDtypeStruct((HALVES, QGROUP, layout.blocks), jnp.bfloat16)] * layout.groups,
        compiler_params=pltpu.CompilerParams(vmem_limit_bytes=SUM_VMEM_LIMIT),
        cost_estimate=pl.CostEstimate(
            flops=30 * size, bytes_accessed=2 * (layout.half + 3) * size, transcendentals=0
        ),
        name="group_sum_code",
    )(*across, *near)


def bfloat16_terms(values):
    terms = []
    for _ in range(3):
        terms.append(values.astype(jnp.bfloat16))
        values = values - terms[-1].astype(jnp.float32)
    return terms


def finish_kernel(sign_ref, *refs):
    out_ref, max_ref = refs[-2:]
    second = [add_all([ref[half] for ref in refs[:-2]]) for half in range(HALVES)]
    blocks = second[0].shape[1]
    natural = jnp.concatenate([part.T for part in second], axis=1)
    block = lax.broadcasted_iota(jnp.int32, (blocks, HALVES * blocks), 0)
    lane = lax.broadcasted_iota(jnp.int32, (blocks, HALVES * blocks), 1)
    largest = jnp.zeros((1, HALVES * blocks), jnp.float32)
    for half in range(HALVES):
        peak = jnp.max(jnp.abs(natural[:, half * QGROUP : (half + 1) * QGROUP]), axis=1, keepdims=True)
        chosen = jnp.where(lane == HALVES * block + half, peak, 0.0)
        largest = jnp.maximum(largest, jnp.max(chosen, axis=0, keepdims=True))
    max_ref[...] = largest * jnp.float32(ROT**-0.5)
    matrix = sylvester()
    high, middle, low = [
        jnp.dot(term, matrix, preferred_element_type=jnp.float32) for term in bfloat16_terms(natural)
    ]
    turned = (high + (middle + low)) * jnp.float32(1.0 / ROT)
    for half in range(HALVES):
        at = pl.ds(half, blocks, stride=HALVES)
        part = turned[:, half * QGROUP : (half + 1) * QGROUP]
        out_ref[at, :] = jnp.where(sign_ref[at, :] == 0, part, -part)


def finish(parts, signs):
    rows = signs.shape[0]
    return pl.pallas_call(
        finish_kernel,
        out_shape=[
            jax.ShapeDtypeStruct((rows, LANES), jnp.float32),
            jax.ShapeDtypeStruct((1, rows), jnp.float32),
        ],
        compiler_params=pltpu.CompilerParams(vmem_limit_bytes=SUM_VMEM_LIMIT),
        name="sum_unrotate",
    )(signs, *parts)


def shards(partials, signs):
    length = partials.shape[-1]
    members = lax.axis_size("local")
    groups = lax.axis_size("node")
    layout = Layout(length, members, groups)
    half = layout.half

    def swap(part, step):
        pairs = []
        for source in range(members):
            first, index = source // half * half, source % half
            pairs.append((source, first + partner(index, step, half)))
        return lax.ppermute(part, "local", pairs)

    def share(parts):
        moved = []
        for step in range(groups - 1, 0, -1):
            pairs = [(source, partner(source, step, groups)) for source in range(groups)]
            moved.append(lax.ppermute(parts[step], "node", pairs))
        return moved + [parts[0]]

    values, sign_rows = partials.reshape(1, length), signs.reshape(length // LANES, LANES)
    counterparts = [(member, (member + half) % members) for member in range(members)]
    slow = half // 2
    others = [step for step in range(half - 1, 0, -1) if step != slow]
    order = others[:1] + [slow] + others[1:]
    whole = tuple(range(HALVES))
    *far0, half1 = rotate(values, sign_rows, layout, True, order + [slow], [(0,)] * len(order) + [(1,)])
    *far1, own = rotate(
        values, sign_rows, layout, True, others + [0], [(1,)] * len(others) + [whole], after=[*far0, half1]
    )
    far0 = [swap(part, step) for step, part in zip(order, far0)] + [own]
    early = far1
    first = far_sum(far0, layout, 0, [*early])
    across = [lax.ppermute(first, "local", counterparts)]
    middle = others[:1] + [slow]
    near = rotate(values, sign_rows, layout, False, middle, [whole] * len(middle), after=[first])
    far1 = [swap(part, step) for step, part in zip(others + [slow], far1 + [half1])] + [own]
    second = far_sum(far1, layout, 1, [*near])
    across.append(lax.ppermute(second, "local", counterparts))
    ends = [step for step in others if step not in middle] + [0]
    *outs, own_signs = rotate(
        values, sign_rows, layout, False, ends, [whole] * len(ends), signed_out=True, after=[second]
    )
    near = {step: swap(part, step) if step else part for step, part in zip(middle + ends, near + outs)}
    reduced, rotated_max = finish(share(group_sum([near[step] for step in order + [0]], across, layout)), own_signs)
    return (reduced.reshape(-1), rotated_max.reshape(-1))


def solution(mesh):
    in_specs = (P("node", "local", None), P())
    out_specs = (P(("node", "local")), P(("node", "local")))
    return jax.shard_map(shards, mesh=mesh, in_specs=in_specs, out_specs=out_specs, check_vma=False)
```

```python
import functools
import jax
import jax.numpy as jnp
from jax import lax
from jax.experimental import pallas as pl
from jax.experimental.pallas import tpu as pltpu
from jax.sharding import PartitionSpec as P

ROT = 256
QGROUP = 128
HALVES = ROT // QGROUP
LANES = 128
VMEM_LIMIT = 50 * 1024 * 1024
SUM_VMEM_LIMIT = 24 * 1024 * 1024
PIECES = 8


def sylvester():
    row = lax.broadcasted_iota(jnp.int32, (ROT, ROT), 0)
    column = lax.broadcasted_iota(jnp.int32, (ROT, ROT), 1)
    parity = lax.population_count(row & column) & 1
    return (1 - 2 * parity).astype(jnp.float32).astype(jnp.bfloat16)


def partner(index, step, count):
    if count & (count - 1) == 0:
        return index ^ step
    return (index + step) % count


def leading_power(x, factor):
    q = x * jnp.float32((2.0**23 + 1.0) * factor)
    return q - q * jnp.float32(1.0 - 2.0**-24)


def recode(values):
    magnitude = jnp.abs(values)
    largest = jnp.max(magnitude, axis=-2, keepdims=True)
    least = jnp.clip(largest, 2.0**-30, 2.0**30) * jnp.float32(2.0**-13)
    shift = leading_power(jnp.maximum(magnitude, least), 2.0**20)
    nearest = (magnitude + shift) - shift
    rest = magnitude - nearest
    coded = jnp.where(rest == shift * jnp.float32(2.0**-24), magnitude + rest, nearest)
    return jnp.where(values < 0.0, -coded, coded)


class Layout:
    def __init__(self, length, members, groups):
        self.members = members
        self.groups = groups
        self.half = members // 2
        self.portion = length // (members * groups)
        self.rows = self.portion // LANES
        self.blocks = self.portion // ROT
        self.together = 1
        if self.blocks < LANES and LANES % self.blocks == 0 and groups % (LANES // self.blocks) == 0:
            self.together = LANES // self.blocks
        self.units = groups // self.together
        self.columns = self.together * self.blocks

    def shape(self):
        return (self.units, QGROUP, self.columns)

    def runs(self, steps, inner):
        half = self.half
        if half & (half - 1) or len(set(steps)) == half:
            return [(0, half)]
        low = 1
        while low < half and all(step in steps for step in range(2 * low)):
            low *= 2
        runs = [(inner // low * low, low)] if 0 in steps else []
        count = low if 0 in steps else 1
        while count < half:
            present = [step for step in range(count, 2 * count) if step in steps]
            if len(present) == count:
                runs.append(((inner ^ count) // count * count, count))
            else:
                runs += [(inner ^ step, 1) for step in present]
            count *= 2
        return runs

    def batch(self, steps):
        batch = min(self.units, max(1, PIECES // len(steps)))
        return batch if self.units % batch == 0 else 1


def rotate_kernel(layout, other, steps, parts, signed_out, extra, values_ref, signs_ref, *refs):
    values, flips, turned, matrix, value_sems, sign_sems = refs[-6:]
    out_refs = refs[extra:-6]
    half, portion, rows = layout.half, layout.portion, layout.rows
    node = lax.axis_index("node")
    member = lax.axis_index("local")
    inner = lax.rem(member, half)
    first = half - (member - inner) if other else member - inner
    runs, batch = layout.runs(steps, inner), layout.batch(steps)

    def fetches(unit):
        copies = []
        for part in range(layout.together):
            section = partner(node, unit * layout.together + part, layout.groups) * layout.members + first
            for index, (owner, count) in enumerate(runs):
                place = section + owner
                copies.append(
                    pltpu.make_async_copy(
                        values_ref.at[:, pl.ds(pl.multiple_of(place * portion, portion), count * portion)],
                        values.at[unit, part, :, pl.ds(pl.multiple_of(owner * portion, portion), count * portion)],
                        value_sems.at[unit, part, index],
                    )
                )
                copies.append(
                    pltpu.make_async_copy(
                        signs_ref.at[pl.ds(pl.multiple_of(place * rows, rows), count * rows), :],
                        flips.at[unit, part, pl.ds(pl.multiple_of(owner * rows, rows), count * rows), :],
                        sign_sems.at[unit, part, index],
                    )
                )
        return copies

    for unit in range(layout.units):
        for copy in fetches(unit):
            copy.start()
    matrix[...] = sylvester()

    def body(turn, carry):
        for index in range(batch):
            for copy in fetches(turn * batch + index):
                copy.wait()
        for index, (position, step) in [(i, p) for i in range(batch) for p in enumerate(steps)]:
            unit = turn * batch + index
            slot = turned.at[index * len(steps) + position]
            owner = partner(inner, step, half)
            at = pl.ds(pl.multiple_of(owner * portion, portion), portion)
            at_rows = pl.ds(pl.multiple_of(owner * rows, rows), rows)
            for part in range(layout.together):
                wide = values[unit, part, :, at].astype(jnp.float32).reshape(rows, LANES)
                slot[part * rows : (part + 1) * rows] = jnp.where(flips[unit, part, at_rows, :] == 0, wide, -wide)
            halves = [slot[pl.ds(part, layout.columns, stride=HALVES), :] for part in range(HALVES)]
            signed = jnp.concatenate(halves, axis=1).astype(jnp.bfloat16)
            wanted = parts[position]
            lowest = wanted[0] * QGROUP
            rotated = lax.dot_general(
                matrix[lowest : lowest + len(wanted) * QGROUP],
                signed,
                (((1,), (1,)), ((), ())),
                preferred_element_type=jnp.float32,
            )
            for part in range(len(wanted)):
                rows_of = slice(part * QGROUP, (part + 1) * QGROUP)
                out_refs[position][unit, rows_of] = recode(rotated[rows_of]).astype(jnp.bfloat16)
        return carry

    lax.fori_loop(0, layout.units // batch, body, 0)
    if signed_out:
        out_refs[-2][...] = flips[0, 0, pl.ds(pl.multiple_of(inner * rows, rows), rows), :]
        out_refs[-1][...] = matrix[...]


def rotate(values, signs, layout, other, steps, parts, signed_out=False, after=()):
    half, units, columns = layout.half, layout.units, layout.columns
    batch = layout.batch(steps)
    runs = len(layout.runs(steps, 0))
    entries = len(steps) * layout.groups * layout.portion
    outs = [jax.ShapeDtypeStruct((units, len(wanted) * QGROUP, columns), jnp.bfloat16) for wanted in parts]
    if signed_out:
        outs.append(jax.ShapeDtypeStruct((layout.rows, LANES), jnp.int32))
        outs.append(jax.ShapeDtypeStruct((ROT, ROT), jnp.bfloat16))
    return list(
        pl.pallas_call(
            functools.partial(rotate_kernel, layout, other, steps, parts, signed_out, len(after)),
            in_specs=[pl.BlockSpec(memory_space=pltpu.HBM)] * 2 + [pl.BlockSpec(memory_space=pl.ANY)] * len(after),
            out_specs=[pl.BlockSpec(memory_space=pltpu.VMEM)] * len(outs),
            out_shape=outs,
            scratch_shapes=[
                pltpu.VMEM((units, layout.together, 1, half * layout.portion), jnp.bfloat16),
                pltpu.VMEM((units, layout.together, half * layout.rows, LANES), jnp.int32),
                pltpu.VMEM((batch * len(steps), layout.together * layout.rows, LANES), jnp.float32),
                pltpu.VMEM((ROT, ROT), jnp.bfloat16),
                pltpu.SemaphoreType.DMA((units, layout.together, runs)),
                pltpu.SemaphoreType.DMA((units, layout.together, runs)),
            ],
            compiler_params=pltpu.CompilerParams(vmem_limit_bytes=VMEM_LIMIT),
            cost_estimate=pl.CostEstimate(flops=2 * entries * ROT, bytes_accessed=10 * entries, transcendentals=0),
            name="rotate_code",
        )(values, signs, *after)
    )


def add_all(arrays):
    total = arrays[0].astype(jnp.float32)
    for array in arrays[1:]:
        total = total + array.astype(jnp.float32)
    return total


def far_sum_kernel(part, count, *refs):
    arrays = []
    for ref in refs[:count]:
        cut = ref.shape[1] == QGROUP
        arrays.append(ref[...] if cut else ref[:, part * QGROUP : (part + 1) * QGROUP])
    refs[-1][...] = add_all(arrays)


def far_sum(parts, layout, part, after=()):
    size = QGROUP * layout.units * layout.columns
    return pl.pallas_call(
        functools.partial(far_sum_kernel, part, len(parts)),
        in_specs=[pl.BlockSpec(memory_space=pltpu.VMEM)] * len(parts)
        + [pl.BlockSpec(memory_space=pl.ANY)] * len(after),
        out_specs=pl.BlockSpec(memory_space=pltpu.VMEM),
        out_shape=jax.ShapeDtypeStruct(layout.shape(), jnp.float32),
        compiler_params=pltpu.CompilerParams(vmem_limit_bytes=SUM_VMEM_LIMIT),
        cost_estimate=pl.CostEstimate(
            flops=2 * len(parts) * size, bytes_accessed=(2 * len(parts) + 4) * size, transcendentals=0
        ),
        name="far_sum",
    )(*parts, *after)


def group_sum_kernel(layout, *refs):
    across_refs, near_refs, out_refs = refs[:HALVES], refs[HALVES : HALVES + layout.half], refs[HALVES + layout.half :]
    for half, across_ref in enumerate(across_refs):
        near = [ref[:, half * QGROUP : (half + 1) * QGROUP] for ref in near_refs]
        first = recode(add_all(near + [across_ref[...]])).astype(jnp.bfloat16)
        for section, out_ref in enumerate(out_refs):
            at = section % layout.together * layout.blocks
            out_ref[half] = first[section // layout.together, :, at : at + layout.blocks]


def group_sum(near, across, layout):
    size = near[0].size
    return pl.pallas_call(
        functools.partial(group_sum_kernel, layout),
        out_shape=[jax.ShapeDtypeStruct((HALVES, QGROUP, layout.blocks), jnp.bfloat16)] * layout.groups,
        compiler_params=pltpu.CompilerParams(vmem_limit_bytes=SUM_VMEM_LIMIT),
        cost_estimate=pl.CostEstimate(
            flops=30 * size, bytes_accessed=2 * (layout.half + 3) * size, transcendentals=0
        ),
        name="group_sum_code",
    )(*across, *near)


def bfloat16_terms(values):
    terms = []
    for _ in range(3):
        terms.append(values.astype(jnp.bfloat16))
        values = values - terms[-1].astype(jnp.float32)
    return terms


def finish_kernel(matrix_ref, sign_ref, *refs):
    out_ref, max_ref = refs[-2:]
    second = [add_all([ref[half] for ref in refs[:-2]]) for half in range(HALVES)]
    blocks = second[0].shape[1]
    natural = jnp.concatenate([part.T for part in second], axis=1)
    block = lax.broadcasted_iota(jnp.int32, (blocks, HALVES * blocks), 0)
    lane = lax.broadcasted_iota(jnp.int32, (blocks, HALVES * blocks), 1)
    largest = jnp.zeros((1, HALVES * blocks), jnp.float32)
    for half in range(HALVES):
        peak = jnp.max(jnp.abs(natural[:, half * QGROUP : (half + 1) * QGROUP]), axis=1, keepdims=True)
        chosen = jnp.where(lane == HALVES * block + half, peak, 0.0)
        largest = jnp.maximum(largest, jnp.max(chosen, axis=0, keepdims=True))
    max_ref[...] = largest * jnp.float32(ROT**-0.5)
    matrix = matrix_ref[...]
    high, middle, low = [
        jnp.dot(term, matrix, preferred_element_type=jnp.float32) for term in bfloat16_terms(natural)
    ]
    turned = (high + (middle + low)) * jnp.float32(1.0 / ROT)
    for half in range(HALVES):
        at = pl.ds(half, blocks, stride=HALVES)
        part = turned[:, half * QGROUP : (half + 1) * QGROUP]
        out_ref[at, :] = jnp.where(sign_ref[at, :] == 0, part, -part)


def finish(parts, signs, matrix):
    rows = signs.shape[0]
    return pl.pallas_call(
        finish_kernel,
        out_shape=[
            jax.ShapeDtypeStruct((rows, LANES), jnp.float32),
            jax.ShapeDtypeStruct((1, rows), jnp.float32),
        ],
        compiler_params=pltpu.CompilerParams(vmem_limit_bytes=SUM_VMEM_LIMIT),
        name="sum_unrotate",
    )(matrix, signs, *parts)


def shards(partials, signs):
    length = partials.shape[-1]
    members = lax.axis_size("local")
    groups = lax.axis_size("node")
    layout = Layout(length, members, groups)
    half = layout.half

    def swap(part, step):
        pairs = []
        for source in range(members):
            first, index = source // half * half, source % half
            pairs.append((source, first + partner(index, step, half)))
        return lax.ppermute(part, "local", pairs)

    def share(parts):
        moved = []
        for step in range(groups - 1, 0, -1):
            pairs = [(source, partner(source, step, groups)) for source in range(groups)]
            moved.append(lax.ppermute(parts[step], "node", pairs))
        return moved + [parts[0]]

    values, sign_rows = partials.reshape(1, length), signs.reshape(length // LANES, LANES)
    counterparts = [(member, (member + half) % members) for member in range(members)]
    slow = half // 2
    others = [step for step in range(half - 1, 0, -1) if step != slow]
    order = others[:1] + [slow] + others[1:]
    whole = tuple(range(HALVES))
    *far0, half1 = rotate(values, sign_rows, layout, True, order + [slow], [(0,)] * len(order) + [(1,)])
    *far1, own = rotate(
        values, sign_rows, layout, True, others + [0], [(1,)] * len(others) + [whole], after=[*far0, half1]
    )
    far0 = [swap(part, step) for step, part in zip(order, far0)] + [own]
    early = far1
    first = far_sum(far0, layout, 0, [*early])
    across = [lax.ppermute(first, "local", counterparts)]
    middle = order
    near = rotate(values, sign_rows, layout, False, middle, [whole] * len(middle), after=[first])
    far1 = [swap(part, step) for step, part in zip(others + [slow], far1 + [half1])] + [own]
    second = far_sum(far1, layout, 1, near[2:])
    across.append(lax.ppermute(second, "local", counterparts))
    ends = [step for step in others if step not in middle] + [0]
    *outs, own_signs, matrix = rotate(
        values, sign_rows, layout, False, ends, [whole] * len(ends), signed_out=True, after=[second]
    )
    near = {step: swap(part, step) if step else part for step, part in zip(middle + ends, near + outs)}
    reduced, rotated_max = finish(share(group_sum([near[step] for step in order + [0]], across, layout)), own_signs, matrix)
    return (reduced.reshape(-1), rotated_max.reshape(-1))


def solution(mesh):
    in_specs = (P("node", "local", None), P())
    out_specs = (P(("node", "local")), P(("node", "local")))
    return jax.shard_map(shards, mesh=mesh, in_specs=in_specs, out_specs=out_specs, check_vma=False)
```

```python
import functools
import jax
import jax.numpy as jnp
from jax import lax
from jax.experimental import pallas as pl
from jax.experimental.pallas import tpu as pltpu
from jax.sharding import PartitionSpec as P

ROT = 256
QGROUP = 128
HALVES = ROT // QGROUP
LANES = 128
VMEM_LIMIT = 50 * 1024 * 1024
SUM_VMEM_LIMIT = 24 * 1024 * 1024
PIECES = 8


def sylvester():
    row = lax.broadcasted_iota(jnp.int32, (ROT, ROT), 0)
    column = lax.broadcasted_iota(jnp.int32, (ROT, ROT), 1)
    parity = lax.population_count(row & column) & 1
    return (1 - 2 * parity).astype(jnp.float32).astype(jnp.bfloat16)


def partner(index, step, count):
    if count & (count - 1) == 0:
        return index ^ step
    return (index + step) % count


def leading_power(x, factor):
    q = x * jnp.float32((2.0**23 + 1.0) * factor)
    return q - q * jnp.float32(1.0 - 2.0**-24)


def recode(values):
    magnitude = jnp.abs(values)
    largest = jnp.max(magnitude, axis=-2, keepdims=True)
    least = jnp.clip(largest, 2.0**-30, 2.0**30) * jnp.float32(2.0**-13)
    shift = leading_power(jnp.maximum(magnitude, least), 2.0**20)
    nearest = (magnitude + shift) - shift
    rest = magnitude - nearest
    coded = jnp.where(rest == shift * jnp.float32(2.0**-24), magnitude + rest, nearest)
    return jnp.where(values < 0.0, -coded, coded)


class Layout:
    def __init__(self, length, members, groups):
        self.members = members
        self.groups = groups
        self.half = members // 2
        self.portion = length // (members * groups)
        self.rows = self.portion // LANES
        self.blocks = self.portion // ROT
        self.together = 1
        if self.blocks < LANES and LANES % self.blocks == 0 and groups % (LANES // self.blocks) == 0:
            self.together = LANES // self.blocks
        self.units = groups // self.together
        self.columns = self.together * self.blocks

    def shape(self):
        return (self.units, QGROUP, self.columns)

    def runs(self, steps, inner):
        half = self.half
        if half & (half - 1) or len(set(steps)) == half:
            return [(0, half)]
        low = 1
        while low < half and all(step in steps for step in range(2 * low)):
            low *= 2
        runs = [(inner // low * low, low)] if 0 in steps else []
        count = low if 0 in steps else 1
        while count < half:
            present = [step for step in range(count, 2 * count) if step in steps]
            if len(present) == count:
                runs.append(((inner ^ count) // count * count, count))
            else:
                runs += [(inner ^ step, 1) for step in present]
            count *= 2
        return runs

    def batch(self, steps):
        batch = min(self.units, max(1, PIECES // len(steps)))
        return batch if self.units % batch == 0 else 1


def rotate_kernel(layout, other, steps, parts, signed_out, extra, values_ref, signs_ref, *refs):
    values, flips, turned, matrix, value_sems, sign_sems = refs[-6:]
    out_refs = refs[extra:-6]
    half, portion, rows = layout.half, layout.portion, layout.rows
    node = lax.axis_index("node")
    member = lax.axis_index("local")
    inner = lax.rem(member, half)
    first = half - (member - inner) if other else member - inner
    runs, batch = layout.runs(steps, inner), layout.batch(steps)

    def fetches(unit):
        copies = []
        for part in range(layout.together):
            section = partner(node, unit * layout.together + part, layout.groups) * layout.members + first
            for index, (owner, count) in enumerate(runs):
                place = section + owner
                copies.append(
                    pltpu.make_async_copy(
                        values_ref.at[:, pl.ds(pl.multiple_of(place * portion, portion), count * portion)],
                        values.at[unit, part, :, pl.ds(pl.multiple_of(owner * portion, portion), count * portion)],
                        value_sems.at[unit, part, index],
                    )
                )
                copies.append(
                    pltpu.make_async_copy(
                        signs_ref.at[pl.ds(pl.multiple_of(place * rows, rows), count * rows), :],
                        flips.at[unit, part, pl.ds(pl.multiple_of(owner * rows, rows), count * rows), :],
                        sign_sems.at[unit, part, index],
                    )
                )
        return copies

    for unit in range(layout.units):
        for copy in fetches(unit):
            copy.start()
    matrix[...] = sylvester()

    def body(turn, carry):
        for index in range(batch):
            for copy in fetches(turn * batch + index):
                copy.wait()
        for index, (position, step) in [(i, p) for i in range(batch) for p in enumerate(steps)]:
            unit = turn * batch + index
            slot = turned.at[index * len(steps) + position]
            owner = partner(inner, step, half)
            at = pl.ds(pl.multiple_of(owner * portion, portion), portion)
            at_rows = pl.ds(pl.multiple_of(owner * rows, rows), rows)
            for part in range(layout.together):
                wide = values[unit, part, :, at].astype(jnp.float32).reshape(rows, LANES)
                slot[part * rows : (part + 1) * rows] = jnp.where(flips[unit, part, at_rows, :] == 0, wide, -wide)
            halves = [slot[pl.ds(part, layout.columns, stride=HALVES), :] for part in range(HALVES)]
            signed = jnp.concatenate(halves, axis=1).astype(jnp.bfloat16)
            wanted = parts[position]
            lowest = wanted[0] * QGROUP
            rotated = lax.dot_general(
                matrix[lowest : lowest + len(wanted) * QGROUP],
                signed,
                (((1,), (1,)), ((), ())),
                preferred_element_type=jnp.float32,
            )
            for part in range(len(wanted)):
                rows_of = slice(part * QGROUP, (part + 1) * QGROUP)
                out_refs[position][unit, rows_of] = recode(rotated[rows_of]).astype(jnp.bfloat16)
        return carry

    lax.fori_loop(0, layout.units // batch, body, 0)
    if signed_out:
        out_refs[-1][...] = flips[0, 0, pl.ds(pl.multiple_of(inner * rows, rows), rows), :]


def rotate(values, signs, layout, other, steps, parts, signed_out=False, after=()):
    half, units, columns = layout.half, layout.units, layout.columns
    batch = layout.batch(steps)
    runs = len(layout.runs(steps, 0))
    entries = len(steps) * layout.groups * layout.portion
    outs = [jax.ShapeDtypeStruct((units, len(wanted) * QGROUP, columns), jnp.bfloat16) for wanted in parts]
    if signed_out:
        outs.append(jax.ShapeDtypeStruct((layout.rows, LANES), jnp.int32))
    return list(
        pl.pallas_call(
            functools.partial(rotate_kernel, layout, other, steps, parts, signed_out, len(after)),
            in_specs=[pl.BlockSpec(memory_space=pltpu.HBM)] * 2 + [pl.BlockSpec(memory_space=pl.ANY)] * len(after),
            out_specs=[pl.BlockSpec(memory_space=pltpu.VMEM)] * len(outs),
            out_shape=outs,
            scratch_shapes=[
                pltpu.VMEM((units, layout.together, 1, half * layout.portion), jnp.bfloat16),
                pltpu.VMEM((units, layout.together, half * layout.rows, LANES), jnp.int32),
                pltpu.VMEM((batch * len(steps), layout.together * layout.rows, LANES), jnp.float32),
                pltpu.VMEM((ROT, ROT), jnp.bfloat16),
                pltpu.SemaphoreType.DMA((units, layout.together, runs)),
                pltpu.SemaphoreType.DMA((units, layout.together, runs)),
            ],
            compiler_params=pltpu.CompilerParams(vmem_limit_bytes=VMEM_LIMIT),
            cost_estimate=pl.CostEstimate(flops=2 * entries * ROT, bytes_accessed=10 * entries, transcendentals=0),
            name="rotate_code",
        )(values, signs, *after)
    )


def add_all(arrays):
    total = arrays[0].astype(jnp.float32)
    for array in arrays[1:]:
        total = total + array.astype(jnp.float32)
    return total


def far_sum_kernel(part, count, *refs):
    arrays = []
    for ref in refs[:count]:
        cut = ref.shape[1] == QGROUP
        arrays.append(ref[...] if cut else ref[:, part * QGROUP : (part + 1) * QGROUP])
    refs[-1][...] = add_all(arrays)


def far_sum(parts, layout, part, after=()):
    size = QGROUP * layout.units * layout.columns
    return pl.pallas_call(
        functools.partial(far_sum_kernel, part, len(parts)),
        in_specs=[pl.BlockSpec(memory_space=pltpu.VMEM)] * len(parts)
        + [pl.BlockSpec(memory_space=pl.ANY)] * len(after),
        out_specs=pl.BlockSpec(memory_space=pltpu.VMEM),
        out_shape=jax.ShapeDtypeStruct(layout.shape(), jnp.float32),
        compiler_params=pltpu.CompilerParams(vmem_limit_bytes=SUM_VMEM_LIMIT),
        cost_estimate=pl.CostEstimate(
            flops=2 * len(parts) * size, bytes_accessed=(2 * len(parts) + 4) * size, transcendentals=0
        ),
        name="far_sum",
    )(*parts, *after)


def group_sum_kernel(layout, part, count, *refs):
    arrays = []
    for ref in refs[:count]:
        cut = ref.shape[1] == QGROUP
        arrays.append(ref[...] if cut else ref[:, part * QGROUP : (part + 1) * QGROUP])
    first = recode(add_all(arrays)).astype(jnp.bfloat16)
    for section, out_ref in enumerate(refs[count:]):
        at = section % layout.together * layout.blocks
        out_ref[...] = first[section // layout.together, :, at : at + layout.blocks]


def group_sum(parts, layout, part):
    size = QGROUP * layout.units * layout.columns
    return pl.pallas_call(
        functools.partial(group_sum_kernel, layout, part, len(parts)),
        out_shape=[jax.ShapeDtypeStruct((QGROUP, layout.blocks), jnp.bfloat16)] * layout.groups,
        compiler_params=pltpu.CompilerParams(vmem_limit_bytes=SUM_VMEM_LIMIT),
        cost_estimate=pl.CostEstimate(
            flops=30 * size, bytes_accessed=2 * (len(parts) + 2) * size, transcendentals=0
        ),
        name="group_sum_code",
    )(*parts)


def bfloat16_terms(values):
    terms = []
    for _ in range(3):
        terms.append(values.astype(jnp.bfloat16))
        values = values - terms[-1].astype(jnp.float32)
    return terms


def finish_kernel(sign_ref, *refs):
    out_ref, max_ref = refs[-2:]
    count = (len(refs) - 2) // HALVES
    second = [add_all([ref[...] for ref in refs[half * count : (half + 1) * count]]) for half in range(HALVES)]
    blocks = second[0].shape[1]
    natural = jnp.concatenate([part.T for part in second], axis=1)
    block = lax.broadcasted_iota(jnp.int32, (blocks, HALVES * blocks), 0)
    lane = lax.broadcasted_iota(jnp.int32, (blocks, HALVES * blocks), 1)
    largest = jnp.zeros((1, HALVES * blocks), jnp.float32)
    for half in range(HALVES):
        peak = jnp.max(jnp.abs(natural[:, half * QGROUP : (half + 1) * QGROUP]), axis=1, keepdims=True)
        chosen = jnp.where(lane == HALVES * block + half, peak, 0.0)
        largest = jnp.maximum(largest, jnp.max(chosen, axis=0, keepdims=True))
    max_ref[...] = largest * jnp.float32(ROT**-0.5)
    matrix = sylvester()
    high, middle, low = [
        jnp.dot(term, matrix, preferred_element_type=jnp.float32) for term in bfloat16_terms(natural)
    ]
    turned = (high + (middle + low)) * jnp.float32(1.0 / ROT)
    for half in range(HALVES):
        at = pl.ds(half, blocks, stride=HALVES)
        part = turned[:, half * QGROUP : (half + 1) * QGROUP]
        out_ref[at, :] = jnp.where(sign_ref[at, :] == 0, part, -part)


def finish(parts, signs):
    rows = signs.shape[0]
    return pl.pallas_call(
        finish_kernel,
        out_shape=[
            jax.ShapeDtypeStruct((rows, LANES), jnp.float32),
            jax.ShapeDtypeStruct((1, rows), jnp.float32),
        ],
        compiler_params=pltpu.CompilerParams(vmem_limit_bytes=SUM_VMEM_LIMIT),
        name="sum_unrotate",
    )(signs, *parts)


def shards(partials, signs):
    length = partials.shape[-1]
    members = lax.axis_size("local")
    groups = lax.axis_size("node")
    layout = Layout(length, members, groups)
    half = layout.half

    def swap(part, step):
        pairs = []
        for source in range(members):
            first, index = source // half * half, source % half
            pairs.append((source, first + partner(index, step, half)))
        return lax.ppermute(part, "local", pairs)

    def share(parts):
        moved = []
        for step in range(groups - 1, 0, -1):
            pairs = [(source, partner(source, step, groups)) for source in range(groups)]
            moved.append(lax.ppermute(parts[step], "node", pairs))
        return moved + [parts[0]]

    values, sign_rows = partials.reshape(1, length), signs.reshape(length // LANES, LANES)
    counterparts = [(member, (member + half) % members) for member in range(members)]
    slow = half // 2
    others = [step for step in range(half - 1, 0, -1) if step != slow]
    order = others[:1] + [slow] + others[1:]
    whole = tuple(range(HALVES))
    fast = order[-1]
    *far0, half1 = rotate(values, sign_rows, layout, True, order + [slow], [(0,)] * len(order) + [(1,)])
    *far1, own = rotate(
        values, sign_rows, layout, True, others + [0], [(1,)] * len(others) + [whole], after=[*far0, half1]
    )
    far0 = [swap(part, step) for step, part in zip(order, far0)] + [own]
    early = far1
    first = far_sum(far0, layout, 0, [*early])
    across = [lax.ppermute(first, "local", counterparts)]
    middle = [slow] + [fast] * (fast != slow)
    near = rotate(values, sign_rows, layout, False, middle, [whole] * len(middle), after=[first])
    far1 = [swap(part, step) for step, part in zip(others + [slow], far1 + [half1])] + [own]
    second = far_sum(far1, layout, 1, [*near])
    across.append(lax.ppermute(second, "local", counterparts))
    ends = [step for step in others if step not in middle]
    *outs, own, own_signs = rotate(
        values,
        sign_rows,
        layout,
        False,
        ends + ends + [0],
        [(0,)] * len(ends) + [(1,)] * len(ends) + [whole],
        signed_out=True,
        after=[first],
    )
    near = [swap(part, step) for step, part in zip(middle, near)] + [own]
    outs = [swap(part, step) for step, part in zip(ends + ends, outs)]
    coded = []
    for part in range(HALVES):
        cut = outs[part * len(ends) : (part + 1) * len(ends)]
        coded += share(group_sum(near + cut + [across[part]], layout, part))
    reduced, rotated_max = finish(coded, own_signs)
    return (reduced.reshape(-1), rotated_max.reshape(-1))


def solution(mesh):
    in_specs = (P("node", "local", None), P())
    out_specs = (P(("node", "local")), P(("node", "local")))
    return jax.shard_map(shards, mesh=mesh, in_specs=in_specs, out_specs=out_specs, check_vma=False)
```

```python
import functools
import jax
import jax.numpy as jnp
from jax import lax
from jax.experimental import pallas as pl
from jax.experimental.pallas import tpu as pltpu
from jax.sharding import PartitionSpec as P

ROT = 256
QGROUP = 128
HALVES = ROT // QGROUP
LANES = 128
VMEM_LIMIT = 50 * 1024 * 1024
SUM_VMEM_LIMIT = 24 * 1024 * 1024
PIECES = 8


def sylvester():
    row = lax.broadcasted_iota(jnp.int32, (ROT, ROT), 0)
    column = lax.broadcasted_iota(jnp.int32, (ROT, ROT), 1)
    parity = lax.population_count(row & column) & 1
    return (1 - 2 * parity).astype(jnp.float32).astype(jnp.bfloat16)


def partner(index, step, count):
    if count & (count - 1) == 0:
        return index ^ step
    return (index + step) % count


def leading_power(x, factor):
    q = x * jnp.float32((2.0**23 + 1.0) * factor)
    return q - q * jnp.float32(1.0 - 2.0**-24)


def recode(values):
    magnitude = jnp.abs(values)
    largest = jnp.max(magnitude, axis=-2, keepdims=True)
    least = jnp.clip(largest, 2.0**-30, 2.0**30) * jnp.float32(2.0**-13)
    shift = leading_power(jnp.maximum(magnitude, least), 2.0**20)
    nearest = (magnitude + shift) - shift
    rest = magnitude - nearest
    coded = jnp.where(rest == shift * jnp.float32(2.0**-24), magnitude + rest, nearest)
    return jnp.where(values < 0.0, -coded, coded)


class Layout:
    def __init__(self, length, members, groups):
        self.members = members
        self.groups = groups
        self.half = members // 2
        self.portion = length // (members * groups)
        self.rows = self.portion // LANES
        self.blocks = self.portion // ROT
        self.together = 1
        if self.blocks < LANES and LANES % self.blocks == 0 and groups % (LANES // self.blocks) == 0:
            self.together = LANES // self.blocks
        self.units = groups // self.together
        self.columns = self.together * self.blocks

    def shape(self):
        return (self.units, QGROUP, self.columns)

    def runs(self, steps, inner):
        half = self.half
        if half & (half - 1) or len(set(steps)) == half:
            return [(0, half)]
        low = 1
        while low < half and all(step in steps for step in range(2 * low)):
            low *= 2
        runs = [(inner // low * low, low)] if 0 in steps else []
        count = low if 0 in steps else 1
        while count < half:
            present = [step for step in range(count, 2 * count) if step in steps]
            if len(present) == count:
                runs.append(((inner ^ count) // count * count, count))
            else:
                runs += [(inner ^ step, 1) for step in present]
            count *= 2
        return runs

    def batch(self, steps):
        batch = min(self.units, max(1, PIECES // len(steps)))
        return batch if self.units % batch == 0 else 1


def rotate_kernel(layout, other, steps, parts, signed_out, extra, values_ref, signs_ref, *refs):
    values, flips, turned, matrix, value_sems, sign_sems = refs[-6:]
    out_refs = refs[extra:-6]
    half, portion, rows = layout.half, layout.portion, layout.rows
    node = lax.axis_index("node")
    member = lax.axis_index("local")
    inner = lax.rem(member, half)
    first = half - (member - inner) if other else member - inner
    runs, batch = layout.runs(steps, inner), layout.batch(steps)

    def fetches(unit):
        copies = []
        for part in range(layout.together):
            section = partner(node, unit * layout.together + part, layout.groups) * layout.members + first
            for index, (owner, count) in enumerate(runs):
                place = section + owner
                copies.append(
                    pltpu.make_async_copy(
                        values_ref.at[:, pl.ds(pl.multiple_of(place * portion, portion), count * portion)],
                        values.at[unit, part, :, pl.ds(pl.multiple_of(owner * portion, portion), count * portion)],
                        value_sems.at[unit, part, index],
                    )
                )
                copies.append(
                    pltpu.make_async_copy(
                        signs_ref.at[pl.ds(pl.multiple_of(place * rows, rows), count * rows), :],
                        flips.at[unit, part, pl.ds(pl.multiple_of(owner * rows, rows), count * rows), :],
                        sign_sems.at[unit, part, index],
                    )
                )
        return copies

    for unit in range(layout.units):
        for copy in fetches(unit):
            copy.start()
    matrix[...] = sylvester()

    def body(turn, carry):
        for index in range(batch):
            for copy in fetches(turn * batch + index):
                copy.wait()
        for index, (position, step) in [(i, p) for i in range(batch) for p in enumerate(steps)]:
            unit = turn * batch + index
            slot = turned.at[index * len(steps) + position]
            owner = partner(inner, step, half)
            at = pl.ds(pl.multiple_of(owner * portion, portion), portion)
            at_rows = pl.ds(pl.multiple_of(owner * rows, rows), rows)
            for part in range(layout.together):
                wide = values[unit, part, :, at].astype(jnp.float32).reshape(rows, LANES)
                slot[part * rows : (part + 1) * rows] = jnp.where(flips[unit, part, at_rows, :] == 0, wide, -wide)
            halves = [slot[pl.ds(part, layout.columns, stride=HALVES), :] for part in range(HALVES)]
            signed = jnp.concatenate(halves, axis=1).astype(jnp.bfloat16)
            wanted = parts[position]
            lowest = wanted[0] * QGROUP
            rotated = lax.dot_general(
                matrix[lowest : lowest + len(wanted) * QGROUP],
                signed,
                (((1,), (1,)), ((), ())),
                preferred_element_type=jnp.float32,
            )
            for part in range(len(wanted)):
                rows_of = slice(part * QGROUP, (part + 1) * QGROUP)
                out_refs[position][unit, rows_of] = recode(rotated[rows_of]).astype(jnp.bfloat16)
        return carry

    lax.fori_loop(0, layout.units // batch, body, 0)
    if signed_out:
        out_refs[-1][...] = flips[0, 0, pl.ds(pl.multiple_of(inner * rows, rows), rows), :]


def rotate(values, signs, layout, other, steps, parts, signed_out=False, after=()):
    half, units, columns = layout.half, layout.units, layout.columns
    batch = layout.batch(steps)
    runs = len(layout.runs(steps, 0))
    entries = len(steps) * layout.groups * layout.portion
    outs = [jax.ShapeDtypeStruct((units, len(wanted) * QGROUP, columns), jnp.bfloat16) for wanted in parts]
    if signed_out:
        outs.append(jax.ShapeDtypeStruct((layout.rows, LANES), jnp.int32))
    return list(
        pl.pallas_call(
            functools.partial(rotate_kernel, layout, other, steps, parts, signed_out, len(after)),
            in_specs=[pl.BlockSpec(memory_space=pltpu.HBM)] * 2 + [pl.BlockSpec(memory_space=pl.ANY)] * len(after),
            out_specs=[pl.BlockSpec(memory_space=pltpu.VMEM)] * len(outs),
            out_shape=outs,
            scratch_shapes=[
                pltpu.VMEM((units, layout.together, 1, half * layout.portion), jnp.bfloat16),
                pltpu.VMEM((units, layout.together, half * layout.rows, LANES), jnp.int32),
                pltpu.VMEM((batch * len(steps), layout.together * layout.rows, LANES), jnp.float32),
                pltpu.VMEM((ROT, ROT), jnp.bfloat16),
                pltpu.SemaphoreType.DMA((units, layout.together, runs)),
                pltpu.SemaphoreType.DMA((units, layout.together, runs)),
            ],
            compiler_params=pltpu.CompilerParams(vmem_limit_bytes=VMEM_LIMIT),
            cost_estimate=pl.CostEstimate(flops=2 * entries * ROT, bytes_accessed=10 * entries, transcendentals=0),
            name="rotate_code",
        )(values, signs, *after)
    )


def add_all(arrays):
    total = arrays[0].astype(jnp.float32)
    for array in arrays[1:]:
        total = total + array.astype(jnp.float32)
    return total


def hand_on_kernel(*refs):
    del refs


def hand_on(arrays, after):
    return list(
        pl.pallas_call(
            hand_on_kernel,
            in_specs=[pl.BlockSpec(memory_space=pl.ANY)] * (len(arrays) + 1),
            out_specs=[pl.BlockSpec(memory_space=pl.ANY)] * len(arrays),
            out_shape=[jax.ShapeDtypeStruct(array.shape, array.dtype) for array in arrays],
            input_output_aliases={index: index for index in range(len(arrays))},
            name="hand_on",
        )(*arrays, after)
    )


def far_sum_kernel(part, count, *refs):
    arrays = []
    for ref in refs[:count]:
        cut = ref.shape[1] == QGROUP
        arrays.append(ref[...] if cut else ref[:, part * QGROUP : (part + 1) * QGROUP])
    refs[-1][...] = add_all(arrays)


def far_sum(parts, layout, part, after=()):
    size = QGROUP * layout.units * layout.columns
    return pl.pallas_call(
        functools.partial(far_sum_kernel, part, len(parts)),
        in_specs=[pl.BlockSpec(memory_space=pltpu.VMEM)] * len(parts)
        + [pl.BlockSpec(memory_space=pl.ANY)] * len(after),
        out_specs=pl.BlockSpec(memory_space=pltpu.VMEM),
        out_shape=jax.ShapeDtypeStruct(layout.shape(), jnp.float32),
        compiler_params=pltpu.CompilerParams(vmem_limit_bytes=SUM_VMEM_LIMIT),
        cost_estimate=pl.CostEstimate(
            flops=2 * len(parts) * size, bytes_accessed=(2 * len(parts) + 4) * size, transcendentals=0
        ),
        name="far_sum",
    )(*parts, *after)


def group_sum_kernel(layout, part, count, *refs):
    arrays = []
    for ref in refs[:count]:
        cut = ref.shape[1] == QGROUP
        arrays.append(ref[...] if cut else ref[:, part * QGROUP : (part + 1) * QGROUP])
    first = recode(add_all(arrays)).astype(jnp.bfloat16)
    for section, out_ref in enumerate(refs[count:]):
        at = section % layout.together * layout.blocks
        out_ref[...] = first[section // layout.together, :, at : at + layout.blocks]


def group_sum(parts, layout, part):
    size = QGROUP * layout.units * layout.columns
    return pl.pallas_call(
        functools.partial(group_sum_kernel, layout, part, len(parts)),
        out_shape=[jax.ShapeDtypeStruct((QGROUP, layout.blocks), jnp.bfloat16)] * layout.groups,
        compiler_params=pltpu.CompilerParams(vmem_limit_bytes=SUM_VMEM_LIMIT),
        cost_estimate=pl.CostEstimate(
            flops=30 * size, bytes_accessed=2 * (len(parts) + 2) * size, transcendentals=0
        ),
        name="group_sum_code",
    )(*parts)


def bfloat16_terms(values):
    terms = []
    for _ in range(3):
        terms.append(values.astype(jnp.bfloat16))
        values = values - terms[-1].astype(jnp.float32)
    return terms


def finish_kernel(sign_ref, *refs):
    out_ref, max_ref = refs[-2:]
    count = (len(refs) - 2) // HALVES
    second = [add_all([ref[...] for ref in refs[half * count : (half + 1) * count]]) for half in range(HALVES)]
    blocks = second[0].shape[1]
    natural = jnp.concatenate([part.T for part in second], axis=1)
    block = lax.broadcasted_iota(jnp.int32, (blocks, HALVES * blocks), 0)
    lane = lax.broadcasted_iota(jnp.int32, (blocks, HALVES * blocks), 1)
    largest = jnp.zeros((1, HALVES * blocks), jnp.float32)
    for half in range(HALVES):
        peak = jnp.max(jnp.abs(natural[:, half * QGROUP : (half + 1) * QGROUP]), axis=1, keepdims=True)
        chosen = jnp.where(lane == HALVES * block + half, peak, 0.0)
        largest = jnp.maximum(largest, jnp.max(chosen, axis=0, keepdims=True))
    max_ref[...] = largest * jnp.float32(ROT**-0.5)
    matrix = sylvester()
    high, middle, low = [
        jnp.dot(term, matrix, preferred_element_type=jnp.float32) for term in bfloat16_terms(natural)
    ]
    turned = (high + (middle + low)) * jnp.float32(1.0 / ROT)
    for half in range(HALVES):
        at = pl.ds(half, blocks, stride=HALVES)
        part = turned[:, half * QGROUP : (half + 1) * QGROUP]
        out_ref[at, :] = jnp.where(sign_ref[at, :] == 0, part, -part)


def finish(parts, signs):
    rows = signs.shape[0]
    return pl.pallas_call(
        finish_kernel,
        out_shape=[
            jax.ShapeDtypeStruct((rows, LANES), jnp.float32),
            jax.ShapeDtypeStruct((1, rows), jnp.float32),
        ],
        compiler_params=pltpu.CompilerParams(vmem_limit_bytes=SUM_VMEM_LIMIT),
        name="sum_unrotate",
    )(signs, *parts)


def shards(partials, signs):
    length = partials.shape[-1]
    members = lax.axis_size("local")
    groups = lax.axis_size("node")
    layout = Layout(length, members, groups)
    half = layout.half

    def swap(part, step):
        pairs = []
        for source in range(members):
            first, index = source // half * half, source % half
            pairs.append((source, first + partner(index, step, half)))
        return lax.ppermute(part, "local", pairs)

    def share(parts):
        moved = []
        for step in range(groups - 1, 0, -1):
            pairs = [(source, partner(source, step, groups)) for source in range(groups)]
            moved.append(lax.ppermute(parts[step], "node", pairs))
        return moved + [parts[0]]

    values, sign_rows = partials.reshape(1, length), signs.reshape(length // LANES, LANES)
    counterparts = [(member, (member + half) % members) for member in range(members)]
    slow = half // 2
    others = [step for step in range(half - 1, 0, -1) if step != slow]
    order = others[:1] + [slow] + others[1:]
    whole = tuple(range(HALVES))
    fast = order[-1]
    *far0, half1 = rotate(values, sign_rows, layout, True, order + [slow], [(0,)] * len(order) + [(1,)])
    *far1, own = rotate(
        values, sign_rows, layout, True, others + [0], [(1,)] * len(others) + [whole], after=[*far0, half1]
    )
    far0 = [swap(part, step) for step, part in zip(order, far0)] + [own]
    early = far1
    first = far_sum(far0, layout, 0, [*early])
    across = [lax.ppermute(first, "local", counterparts)]
    middle = [slow] + [fast] * (fast != slow)
    near = rotate(values, sign_rows, layout, False, middle, [whole] * len(middle), after=[first])
    far1 = [swap(part, step) for step, part in zip(others + [slow], far1 + [half1])] + [own]
    second = far_sum(far1, layout, 1, [*near])
    across.append(lax.ppermute(second, "local", counterparts))
    ends = [step for step in others if step not in middle]
    *outs, own, own_signs = rotate(
        values,
        sign_rows,
        layout,
        False,
        ends + ends + [0],
        [(0,)] * len(ends) + [(1,)] * len(ends) + [whole],
        signed_out=True,
        after=[first],
    )
    near = [swap(part, step) for step, part in zip(middle, near)] + [own]
    if ends:
        outs[len(ends) :] = hand_on(outs[len(ends) :], across[0])
    outs = [swap(part, step) for step, part in zip(ends + ends, outs)]
    coded = []
    for part in range(HALVES):
        cut = outs[part * len(ends) : (part + 1) * len(ends)]
        coded += share(group_sum(near + cut + [across[part]], layout, part))
    reduced, rotated_max = finish(coded, own_signs)
    return (reduced.reshape(-1), rotated_max.reshape(-1))


def solution(mesh):
    in_specs = (P("node", "local", None), P())
    out_specs = (P(("node", "local")), P(("node", "local")))
    return jax.shard_map(shards, mesh=mesh, in_specs=in_specs, out_specs=out_specs, check_vma=False)
```

```python
import functools
import jax
import jax.numpy as jnp
from jax import lax
from jax.experimental import pallas as pl
from jax.experimental.pallas import tpu as pltpu
from jax.sharding import PartitionSpec as P

ROT = 256
QGROUP = 128
HALVES = ROT // QGROUP
LANES = 128
VMEM_LIMIT = 50 * 1024 * 1024
SUM_VMEM_LIMIT = 24 * 1024 * 1024
PIECES = 8


def sylvester():
    row = lax.broadcasted_iota(jnp.int32, (ROT, ROT), 0)
    column = lax.broadcasted_iota(jnp.int32, (ROT, ROT), 1)
    parity = lax.population_count(row & column) & 1
    return (1 - 2 * parity).astype(jnp.float32).astype(jnp.bfloat16)


def partner(index, step, count):
    if count & (count - 1) == 0:
        return index ^ step
    return (index + step) % count


def leading_power(x, factor):
    q = x * jnp.float32((2.0**23 + 1.0) * factor)
    return q - q * jnp.float32(1.0 - 2.0**-24)


def recode(values):
    magnitude = jnp.abs(values)
    largest = jnp.max(magnitude, axis=-2, keepdims=True)
    least = jnp.clip(largest, 2.0**-30, 2.0**30) * jnp.float32(2.0**-13)
    shift = leading_power(jnp.maximum(magnitude, least), 2.0**20)
    nearest = (magnitude + shift) - shift
    rest = magnitude - nearest
    coded = jnp.where(rest == shift * jnp.float32(2.0**-24), magnitude + rest, nearest)
    return jnp.where(values < 0.0, -coded, coded)


class Layout:
    def __init__(self, length, members, groups):
        self.members = members
        self.groups = groups
        self.half = members // 2
        self.portion = length // (members * groups)
        self.rows = self.portion // LANES
        self.blocks = self.portion // ROT
        self.together = 1
        if self.blocks < LANES and LANES % self.blocks == 0 and groups % (LANES // self.blocks) == 0:
            self.together = LANES // self.blocks
        self.units = groups // self.together
        self.columns = self.together * self.blocks

    def shape(self):
        return (self.units, QGROUP, self.columns)

    def runs(self, steps, inner):
        half = self.half
        if half & (half - 1) or len(set(steps)) == half:
            return [(0, half)]
        low = 1
        while low < half and all(step in steps for step in range(2 * low)):
            low *= 2
        runs = [(inner // low * low, low)] if 0 in steps else []
        count = low if 0 in steps else 1
        while count < half:
            present = [step for step in range(count, 2 * count) if step in steps]
            if len(present) == count:
                runs.append(((inner ^ count) // count * count, count))
            else:
                runs += [(inner ^ step, 1) for step in present]
            count *= 2
        return runs

    def batch(self, steps):
        batch = min(self.units, max(1, PIECES // len(steps)))
        return batch if self.units % batch == 0 else 1


def rotate_kernel(layout, other, steps, parts, signed_out, extra, values_ref, signs_ref, *refs):
    values, flips, turned, matrix, value_sems, sign_sems = refs[-6:]
    out_refs = refs[extra:-6]
    half, portion, rows = layout.half, layout.portion, layout.rows
    node = lax.axis_index("node")
    member = lax.axis_index("local")
    inner = lax.rem(member, half)
    first = half - (member - inner) if other else member - inner
    runs, batch = layout.runs(steps, inner), layout.batch(steps)

    def fetches(unit):
        copies = []
        for part in range(layout.together):
            section = partner(node, unit * layout.together + part, layout.groups) * layout.members + first
            for index, (owner, count) in enumerate(runs):
                place = section + owner
                copies.append(
                    pltpu.make_async_copy(
                        values_ref.at[:, pl.ds(pl.multiple_of(place * portion, portion), count * portion)],
                        values.at[unit, part, :, pl.ds(pl.multiple_of(owner * portion, portion), count * portion)],
                        value_sems.at[unit, part, index],
                    )
                )
                copies.append(
                    pltpu.make_async_copy(
                        signs_ref.at[pl.ds(pl.multiple_of(place * rows, rows), count * rows), :],
                        flips.at[unit, part, pl.ds(pl.multiple_of(owner * rows, rows), count * rows), :],
                        sign_sems.at[unit, part, index],
                    )
                )
        return copies

    for unit in range(layout.units):
        for copy in fetches(unit):
            copy.start()
    matrix[...] = sylvester()

    def body(turn, carry):
        for index in range(batch):
            for copy in fetches(turn * batch + index):
                copy.wait()
        for index, (position, step) in [(i, p) for i in range(batch) for p in enumerate(steps)]:
            unit = turn * batch + index
            slot = turned.at[index * len(steps) + position]
            owner = partner(inner, step, half)
            at = pl.ds(pl.multiple_of(owner * portion, portion), portion)
            at_rows = pl.ds(pl.multiple_of(owner * rows, rows), rows)
            for part in range(layout.together):
                wide = values[unit, part, :, at].astype(jnp.float32).reshape(rows, LANES)
                slot[part * rows : (part + 1) * rows] = jnp.where(flips[unit, part, at_rows, :] == 0, wide, -wide)
            halves = [slot[pl.ds(part, layout.columns, stride=HALVES), :] for part in range(HALVES)]
            signed = jnp.concatenate(halves, axis=1).astype(jnp.bfloat16)
            wanted = parts[position]
            lowest = wanted[0] * QGROUP
            rotated = lax.dot_general(
                matrix[lowest : lowest + len(wanted) * QGROUP],
                signed,
                (((1,), (1,)), ((), ())),
                preferred_element_type=jnp.float32,
            )
            for part in range(len(wanted)):
                rows_of = slice(part * QGROUP, (part + 1) * QGROUP)
                out_refs[position][unit, rows_of] = recode(rotated[rows_of]).astype(jnp.bfloat16)
        return carry

    lax.fori_loop(0, layout.units // batch, body, 0)
    if signed_out:
        out_refs[-1][...] = flips[0, 0, pl.ds(pl.multiple_of(inner * rows, rows), rows), :]


def rotate(values, signs, layout, other, steps, parts, signed_out=False, after=()):
    half, units, columns = layout.half, layout.units, layout.columns
    batch = layout.batch(steps)
    runs = len(layout.runs(steps, 0))
    entries = len(steps) * layout.groups * layout.portion
    outs = [jax.ShapeDtypeStruct((units, len(wanted) * QGROUP, columns), jnp.bfloat16) for wanted in parts]
    if signed_out:
        outs.append(jax.ShapeDtypeStruct((layout.rows, LANES), jnp.int32))
    return list(
        pl.pallas_call(
            functools.partial(rotate_kernel, layout, other, steps, parts, signed_out, len(after)),
            in_specs=[pl.BlockSpec(memory_space=pltpu.HBM)] * 2 + [pl.BlockSpec(memory_space=pl.ANY)] * len(after),
            out_specs=[pl.BlockSpec(memory_space=pltpu.VMEM)] * len(outs),
            out_shape=outs,
            scratch_shapes=[
                pltpu.VMEM((units, layout.together, 1, half * layout.portion), jnp.bfloat16),
                pltpu.VMEM((units, layout.together, half * layout.rows, LANES), jnp.int32),
                pltpu.VMEM((batch * len(steps), layout.together * layout.rows, LANES), jnp.float32),
                pltpu.VMEM((ROT, ROT), jnp.bfloat16),
                pltpu.SemaphoreType.DMA((units, layout.together, runs)),
                pltpu.SemaphoreType.DMA((units, layout.together, runs)),
            ],
            compiler_params=pltpu.CompilerParams(vmem_limit_bytes=VMEM_LIMIT),
            cost_estimate=pl.CostEstimate(flops=2 * entries * ROT, bytes_accessed=10 * entries, transcendentals=0),
            name="rotate_code",
        )(values, signs, *after)
    )


def add_all(arrays):
    total = arrays[0].astype(jnp.float32)
    for array in arrays[1:]:
        total = total + array.astype(jnp.float32)
    return total


def hand_on_kernel(*refs):
    del refs


def hand_on(arrays, after):
    return list(
        pl.pallas_call(
            hand_on_kernel,
            in_specs=[pl.BlockSpec(memory_space=pl.ANY)] * (len(arrays) + 1),
            out_specs=[pl.BlockSpec(memory_space=pl.ANY)] * len(arrays),
            out_shape=[jax.ShapeDtypeStruct(array.shape, array.dtype) for array in arrays],
            input_output_aliases={index: index for index in range(len(arrays))},
            compiler_params=pltpu.CompilerParams(vmem_limit_bytes=SUM_VMEM_LIMIT),
            name="hand_on",
        )(*arrays, after)
    )


def far_sum_kernel(part, count, *refs):
    arrays = []
    for ref in refs[:count]:
        cut = ref.shape[1] == QGROUP
        arrays.append(ref[...] if cut else ref[:, part * QGROUP : (part + 1) * QGROUP])
    refs[-1][...] = add_all(arrays)


def far_sum(parts, layout, part, after=()):
    size = QGROUP * layout.units * layout.columns
    return pl.pallas_call(
        functools.partial(far_sum_kernel, part, len(parts)),
        in_specs=[pl.BlockSpec(memory_space=pltpu.VMEM)] * len(parts)
        + [pl.BlockSpec(memory_space=pl.ANY)] * len(after),
        out_specs=pl.BlockSpec(memory_space=pltpu.VMEM),
        out_shape=jax.ShapeDtypeStruct(layout.shape(), jnp.float32),
        compiler_params=pltpu.CompilerParams(vmem_limit_bytes=SUM_VMEM_LIMIT),
        cost_estimate=pl.CostEstimate(
            flops=2 * len(parts) * size, bytes_accessed=(2 * len(parts) + 4) * size, transcendentals=0
        ),
        name="far_sum",
    )(*parts, *after)


def group_sum_kernel(layout, part, count, *refs):
    arrays = []
    for ref in refs[:count]:
        cut = ref.shape[1] == QGROUP
        arrays.append(ref[...] if cut else ref[:, part * QGROUP : (part + 1) * QGROUP])
    first = recode(add_all(arrays)).astype(jnp.bfloat16)
    for section, out_ref in enumerate(refs[count:]):
        at = section % layout.together * layout.blocks
        out_ref[...] = first[section // layout.together, :, at : at + layout.blocks]


def group_sum(parts, layout, part):
    size = QGROUP * layout.units * layout.columns
    return pl.pallas_call(
        functools.partial(group_sum_kernel, layout, part, len(parts)),
        out_shape=[jax.ShapeDtypeStruct((QGROUP, layout.blocks), jnp.bfloat16)] * layout.groups,
        compiler_params=pltpu.CompilerParams(vmem_limit_bytes=SUM_VMEM_LIMIT),
        cost_estimate=pl.CostEstimate(
            flops=30 * size, bytes_accessed=2 * (len(parts) + 2) * size, transcendentals=0
        ),
        name="group_sum_code",
    )(*parts)


def bfloat16_terms(values):
    terms = []
    for _ in range(3):
        terms.append(values.astype(jnp.bfloat16))
        values = values - terms[-1].astype(jnp.float32)
    return terms


def finish_kernel(sign_ref, *refs):
    out_ref, max_ref = refs[-2:]
    count = (len(refs) - 2) // HALVES
    second = [add_all([ref[...] for ref in refs[half * count : (half + 1) * count]]) for half in range(HALVES)]
    blocks = second[0].shape[1]
    natural = jnp.concatenate([part.T for part in second], axis=1)
    block = lax.broadcasted_iota(jnp.int32, (blocks, HALVES * blocks), 0)
    lane = lax.broadcasted_iota(jnp.int32, (blocks, HALVES * blocks), 1)
    largest = jnp.zeros((1, HALVES * blocks), jnp.float32)
    for half in range(HALVES):
        peak = jnp.max(jnp.abs(natural[:, half * QGROUP : (half + 1) * QGROUP]), axis=1, keepdims=True)
        chosen = jnp.where(lane == HALVES * block + half, peak, 0.0)
        largest = jnp.maximum(largest, jnp.max(chosen, axis=0, keepdims=True))
    max_ref[...] = largest * jnp.float32(ROT**-0.5)
    matrix = sylvester()
    high, middle, low = [
        jnp.dot(term, matrix, preferred_element_type=jnp.float32) for term in bfloat16_terms(natural)
    ]
    turned = (high + (middle + low)) * jnp.float32(1.0 / ROT)
    for half in range(HALVES):
        at = pl.ds(half, blocks, stride=HALVES)
        part = turned[:, half * QGROUP : (half + 1) * QGROUP]
        out_ref[at, :] = jnp.where(sign_ref[at, :] == 0, part, -part)


def finish(parts, signs):
    rows = signs.shape[0]
    return pl.pallas_call(
        finish_kernel,
        out_shape=[
            jax.ShapeDtypeStruct((rows, LANES), jnp.float32),
            jax.ShapeDtypeStruct((1, rows), jnp.float32),
        ],
        compiler_params=pltpu.CompilerParams(vmem_limit_bytes=SUM_VMEM_LIMIT),
        name="sum_unrotate",
    )(signs, *parts)


def shards(partials, signs):
    length = partials.shape[-1]
    members = lax.axis_size("local")
    groups = lax.axis_size("node")
    layout = Layout(length, members, groups)
    half = layout.half

    def swap(part, step):
        pairs = []
        for source in range(members):
            first, index = source // half * half, source % half
            pairs.append((source, first + partner(index, step, half)))
        return lax.ppermute(part, "local", pairs)

    def share(parts):
        moved = []
        for step in range(groups - 1, 0, -1):
            pairs = [(source, partner(source, step, groups)) for source in range(groups)]
            moved.append(lax.ppermute(parts[step], "node", pairs))
        return moved + [parts[0]]

    values, sign_rows = partials.reshape(1, length), signs.reshape(length // LANES, LANES)
    counterparts = [(member, (member + half) % members) for member in range(members)]
    slow = half // 2
    others = [step for step in range(half - 1, 0, -1) if step != slow]
    order = others[:1] + [slow] + others[1:]
    whole = tuple(range(HALVES))
    fast = order[-1]
    *far0, half1 = rotate(values, sign_rows, layout, True, order + [slow], [(0,)] * len(order) + [(1,)])
    *far1, own = rotate(
        values, sign_rows, layout, True, others + [0], [(1,)] * len(others) + [whole], after=[*far0, half1]
    )
    far0 = [swap(part, step) for step, part in zip(order, far0)] + [own]
    early = far1
    first = far_sum(far0, layout, 0, [*early])
    across = [lax.ppermute(first, "local", counterparts)]
    middle = [slow] + [fast] * (fast != slow)
    near = rotate(values, sign_rows, layout, False, middle, [whole] * len(middle), after=[first])
    far1 = [swap(part, step) for step, part in zip(others + [slow], far1 + [half1])] + [own]
    second = far_sum(far1, layout, 1, [*near])
    across.append(lax.ppermute(second, "local", counterparts))
    ends = [step for step in others if step not in middle]
    *outs, own, own_signs = rotate(
        values,
        sign_rows,
        layout,
        False,
        ends + ends + [0],
        [(0,)] * len(ends) + [(1,)] * len(ends) + [whole],
        signed_out=True,
        after=[first],
    )
    near = [swap(part, step) for step, part in zip(middle, near)] + [own]
    if ends:
        outs[len(ends) :] = hand_on(outs[len(ends) :], across[0])
    outs = [swap(part, step) for step, part in zip(ends + ends, outs)]
    coded = []
    for part in range(HALVES):
        cut = outs[part * len(ends) : (part + 1) * len(ends)]
        coded += share(group_sum(near + cut + [across[part]], layout, part))
    reduced, rotated_max = finish(coded, own_signs)
    return (reduced.reshape(-1), rotated_max.reshape(-1))


def solution(mesh):
    in_specs = (P("node", "local", None), P())
    out_specs = (P(("node", "local")), P(("node", "local")))
    return jax.shard_map(shards, mesh=mesh, in_specs=in_specs, out_specs=out_specs, check_vma=False)
```

```python
import functools
import jax
import jax.numpy as jnp
from jax import lax
from jax.experimental import pallas as pl
from jax.experimental.pallas import tpu as pltpu
from jax.sharding import PartitionSpec as P

ROT = 256
QGROUP = 128
HALVES = ROT // QGROUP
LANES = 128
VMEM_LIMIT = 50 * 1024 * 1024
SUM_VMEM_LIMIT = 24 * 1024 * 1024
PIECES = 8


def sylvester():
    row = lax.broadcasted_iota(jnp.int32, (ROT, ROT), 0)
    column = lax.broadcasted_iota(jnp.int32, (ROT, ROT), 1)
    parity = lax.population_count(row & column) & 1
    return (1 - 2 * parity).astype(jnp.float32).astype(jnp.bfloat16)


def partner(index, step, count):
    if count & (count - 1) == 0:
        return index ^ step
    return (index + step) % count


def leading_power(x, factor):
    q = x * jnp.float32((2.0**23 + 1.0) * factor)
    return q - q * jnp.float32(1.0 - 2.0**-24)


def recode(values):
    magnitude = jnp.abs(values)
    largest = jnp.max(magnitude, axis=-2, keepdims=True)
    least = jnp.clip(largest, 2.0**-30, 2.0**30) * jnp.float32(2.0**-13)
    shift = leading_power(jnp.maximum(magnitude, least), 2.0**20)
    nearest = (magnitude + shift) - shift
    rest = magnitude - nearest
    coded = jnp.where(rest == shift * jnp.float32(2.0**-24), magnitude + rest, nearest)
    return jnp.where(values < 0.0, -coded, coded)


class Layout:
    def __init__(self, length, members, groups):
        self.members = members
        self.groups = groups
        self.half = members // 2
        self.portion = length // (members * groups)
        self.rows = self.portion // LANES
        self.blocks = self.portion // ROT
        self.together = 1
        if self.blocks < LANES and LANES % self.blocks == 0 and groups % (LANES // self.blocks) == 0:
            self.together = LANES // self.blocks
        self.units = groups // self.together
        self.columns = self.together * self.blocks

    def shape(self):
        return (self.units, QGROUP, self.columns)

    def runs(self, steps, inner):
        half = self.half
        if half & (half - 1) or len(set(steps)) == half:
            return [(0, half)]
        low = 1
        while low < half and all(step in steps for step in range(2 * low)):
            low *= 2
        runs = [(inner // low * low, low)] if 0 in steps else []
        count = low if 0 in steps else 1
        while count < half:
            present = [step for step in range(count, 2 * count) if step in steps]
            if len(present) == count:
                runs.append(((inner ^ count) // count * count, count))
            else:
                runs += [(inner ^ step, 1) for step in present]
            count *= 2
        return runs

    def batch(self, steps):
        batch = min(self.units, max(1, PIECES // len(steps)))
        return batch if self.units % batch == 0 else 1


def rotate_kernel(layout, other, steps, parts, signed_out, extra, values_ref, signs_ref, *refs):
    values, flips, turned, matrix, value_sems, sign_sems = refs[-6:]
    out_refs = refs[extra:-6]
    half, portion, rows = layout.half, layout.portion, layout.rows
    node = lax.axis_index("node")
    member = lax.axis_index("local")
    inner = lax.rem(member, half)
    first = half - (member - inner) if other else member - inner
    runs, batch = layout.runs(steps, inner), layout.batch(steps)

    def fetches(unit):
        copies = []
        for part in range(layout.together):
            section = partner(node, unit * layout.together + part, layout.groups) * layout.members + first
            for index, (owner, count) in enumerate(runs):
                place = section + owner
                copies.append(
                    pltpu.make_async_copy(
                        values_ref.at[:, pl.ds(pl.multiple_of(place * portion, portion), count * portion)],
                        values.at[unit, part, :, pl.ds(pl.multiple_of(owner * portion, portion), count * portion)],
                        value_sems.at[unit, part, index],
                    )
                )
                copies.append(
                    pltpu.make_async_copy(
                        signs_ref.at[pl.ds(pl.multiple_of(place * rows, rows), count * rows), :],
                        flips.at[unit, part, pl.ds(pl.multiple_of(owner * rows, rows), count * rows), :],
                        sign_sems.at[unit, part, index],
                    )
                )
        return copies

    for unit in range(layout.units):
        for copy in fetches(unit):
            copy.start()
    matrix[...] = sylvester()

    def body(turn, carry):
        for index in range(batch):
            for copy in fetches(turn * batch + index):
                copy.wait()
        for index, (position, step) in [(i, p) for i in range(batch) for p in enumerate(steps)]:
            unit = turn * batch + index
            slot = turned.at[index * len(steps) + position]
            owner = partner(inner, step, half)
            at = pl.ds(pl.multiple_of(owner * portion, portion), portion)
            at_rows = pl.ds(pl.multiple_of(owner * rows, rows), rows)
            for part in range(layout.together):
                wide = values[unit, part, :, at].astype(jnp.float32).reshape(rows, LANES)
                slot[part * rows : (part + 1) * rows] = jnp.where(flips[unit, part, at_rows, :] == 0, wide, -wide)
            halves = [slot[pl.ds(part, layout.columns, stride=HALVES), :] for part in range(HALVES)]
            signed = jnp.concatenate(halves, axis=1).astype(jnp.bfloat16)
            wanted = parts[position]
            lowest = wanted[0] * QGROUP
            rotated = lax.dot_general(
                matrix[lowest : lowest + len(wanted) * QGROUP],
                signed,
                (((1,), (1,)), ((), ())),
                preferred_element_type=jnp.float32,
            )
            for part in range(len(wanted)):
                rows_of = slice(part * QGROUP, (part + 1) * QGROUP)
                out_refs[position][unit, rows_of] = recode(rotated[rows_of]).astype(jnp.bfloat16)
        return carry

    lax.fori_loop(0, layout.units // batch, body, 0)
    if signed_out:
        out_refs[-1][...] = flips[0, 0, pl.ds(pl.multiple_of(inner * rows, rows), rows), :]


def rotate(values, signs, layout, other, steps, parts, signed_out=False, after=()):
    half, units, columns = layout.half, layout.units, layout.columns
    batch = layout.batch(steps)
    runs = len(layout.runs(steps, 0))
    entries = len(steps) * layout.groups * layout.portion
    outs = [jax.ShapeDtypeStruct((units, len(wanted) * QGROUP, columns), jnp.bfloat16) for wanted in parts]
    if signed_out:
        outs.append(jax.ShapeDtypeStruct((layout.rows, LANES), jnp.int32))
    return list(
        pl.pallas_call(
            functools.partial(rotate_kernel, layout, other, steps, parts, signed_out, len(after)),
            in_specs=[pl.BlockSpec(memory_space=pltpu.HBM)] * 2 + [pl.BlockSpec(memory_space=pl.ANY)] * len(after),
            out_specs=[pl.BlockSpec(memory_space=pltpu.VMEM)] * len(outs),
            out_shape=outs,
            scratch_shapes=[
                pltpu.VMEM((units, layout.together, 1, half * layout.portion), jnp.bfloat16),
                pltpu.VMEM((units, layout.together, half * layout.rows, LANES), jnp.int32),
                pltpu.VMEM((batch * len(steps), layout.together * layout.rows, LANES), jnp.float32),
                pltpu.VMEM((ROT, ROT), jnp.bfloat16),
                pltpu.SemaphoreType.DMA((units, layout.together, runs)),
                pltpu.SemaphoreType.DMA((units, layout.together, runs)),
            ],
            compiler_params=pltpu.CompilerParams(vmem_limit_bytes=VMEM_LIMIT),
            cost_estimate=pl.CostEstimate(flops=2 * entries * ROT, bytes_accessed=10 * entries, transcendentals=0),
            name="rotate_code",
        )(values, signs, *after)
    )


def add_all(arrays):
    total = arrays[0].astype(jnp.float32)
    for array in arrays[1:]:
        total = total + array.astype(jnp.float32)
    return total


def hand_on_kernel(*refs):
    del refs


def hand_on(arrays, after):
    return list(
        pl.pallas_call(
            hand_on_kernel,
            in_specs=[pl.BlockSpec(memory_space=pl.ANY)] * (len(arrays) + 1),
            out_specs=[pl.BlockSpec(memory_space=pl.ANY)] * len(arrays),
            out_shape=[jax.ShapeDtypeStruct(array.shape, array.dtype) for array in arrays],
            input_output_aliases={index: index for index in range(len(arrays))},
            compiler_params=pltpu.CompilerParams(vmem_limit_bytes=SUM_VMEM_LIMIT),
            name="hand_on",
        )(*arrays, after)
    )


def far_sum_kernel(part, count, *refs):
    arrays = []
    for ref in refs[:count]:
        cut = ref.shape[1] == QGROUP
        arrays.append(ref[...] if cut else ref[:, part * QGROUP : (part + 1) * QGROUP])
    refs[-1][...] = add_all(arrays)


def far_sum(parts, layout, part, after=()):
    size = QGROUP * layout.units * layout.columns
    return pl.pallas_call(
        functools.partial(far_sum_kernel, part, len(parts)),
        in_specs=[pl.BlockSpec(memory_space=pltpu.VMEM)] * len(parts)
        + [pl.BlockSpec(memory_space=pl.ANY)] * len(after),
        out_specs=pl.BlockSpec(memory_space=pltpu.VMEM),
        out_shape=jax.ShapeDtypeStruct(layout.shape(), jnp.float32),
        compiler_params=pltpu.CompilerParams(vmem_limit_bytes=SUM_VMEM_LIMIT),
        cost_estimate=pl.CostEstimate(
            flops=2 * len(parts) * size, bytes_accessed=(2 * len(parts) + 4) * size, transcendentals=0
        ),
        name="far_sum",
    )(*parts, *after)


def group_sum_kernel(layout, part, count, *refs):
    arrays = []
    for ref in refs[:count]:
        cut = ref.shape[1] == QGROUP
        arrays.append(ref[...] if cut else ref[:, part * QGROUP : (part + 1) * QGROUP])
    first = recode(add_all(arrays)).astype(jnp.bfloat16)
    for section, out_ref in enumerate(refs[count:]):
        at = section % layout.together * layout.blocks
        out_ref[...] = first[section // layout.together, :, at : at + layout.blocks]


def group_sum(parts, layout, part):
    size = QGROUP * layout.units * layout.columns
    return pl.pallas_call(
        functools.partial(group_sum_kernel, layout, part, len(parts)),
        out_shape=[jax.ShapeDtypeStruct((QGROUP, layout.blocks), jnp.bfloat16)] * layout.groups,
        compiler_params=pltpu.CompilerParams(vmem_limit_bytes=SUM_VMEM_LIMIT),
        cost_estimate=pl.CostEstimate(
            flops=30 * size, bytes_accessed=2 * (len(parts) + 2) * size, transcendentals=0
        ),
        name="group_sum_code",
    )(*parts)


def bfloat16_terms(values):
    terms = []
    for _ in range(3):
        terms.append(values.astype(jnp.bfloat16))
        values = values - terms[-1].astype(jnp.float32)
    return terms


def finish_kernel(sign_ref, *refs):
    out_ref, max_ref = refs[-2:]
    count = (len(refs) - 2) // HALVES
    second = [add_all([ref[...] for ref in refs[half * count : (half + 1) * count]]) for half in range(HALVES)]
    blocks = second[0].shape[1]
    natural = jnp.concatenate([part.T for part in second], axis=1)
    block = lax.broadcasted_iota(jnp.int32, (blocks, HALVES * blocks), 0)
    lane = lax.broadcasted_iota(jnp.int32, (blocks, HALVES * blocks), 1)
    largest = jnp.zeros((1, HALVES * blocks), jnp.float32)
    for half in range(HALVES):
        peak = jnp.max(jnp.abs(natural[:, half * QGROUP : (half + 1) * QGROUP]), axis=1, keepdims=True)
        chosen = jnp.where(lane == HALVES * block + half, peak, 0.0)
        largest = jnp.maximum(largest, jnp.max(chosen, axis=0, keepdims=True))
    max_ref[...] = largest * jnp.float32(ROT**-0.5)
    matrix = sylvester()
    high, middle, low = [
        jnp.dot(term, matrix, preferred_element_type=jnp.float32) for term in bfloat16_terms(natural)
    ]
    turned = (high + (middle + low)) * jnp.float32(1.0 / ROT)
    for half in range(HALVES):
        at = pl.ds(half, blocks, stride=HALVES)
        part = turned[:, half * QGROUP : (half + 1) * QGROUP]
        out_ref[at, :] = jnp.where(sign_ref[at, :] == 0, part, -part)


def finish(parts, signs):
    rows = signs.shape[0]
    return pl.pallas_call(
        finish_kernel,
        out_shape=[
            jax.ShapeDtypeStruct((rows, LANES), jnp.float32),
            jax.ShapeDtypeStruct((1, rows), jnp.float32),
        ],
        compiler_params=pltpu.CompilerParams(vmem_limit_bytes=SUM_VMEM_LIMIT),
        name="sum_unrotate",
    )(signs, *parts)


def shards(partials, signs):
    length = partials.shape[-1]
    members = lax.axis_size("local")
    groups = lax.axis_size("node")
    layout = Layout(length, members, groups)
    half = layout.half

    def swap(part, step):
        pairs = []
        for source in range(members):
            first, index = source // half * half, source % half
            pairs.append((source, first + partner(index, step, half)))
        return lax.ppermute(part, "local", pairs)

    def share(parts):
        moved = []
        for step in range(groups - 1, 0, -1):
            pairs = [(source, partner(source, step, groups)) for source in range(groups)]
            moved.append(lax.ppermute(parts[step], "node", pairs))
        return moved + [parts[0]]

    values, sign_rows = partials.reshape(1, length), signs.reshape(length // LANES, LANES)
    counterparts = [(member, (member + half) % members) for member in range(members)]
    slow = half // 2
    others = [step for step in range(half - 1, 0, -1) if step != slow]
    order = others[:1] + [slow] + others[1:]
    whole = tuple(range(HALVES))
    fast = order[-1]
    *far0, half1 = rotate(values, sign_rows, layout, True, order + [slow], [(0,)] * len(order) + [(1,)])
    *far1, own = rotate(
        values, sign_rows, layout, True, others + [0], [(1,)] * len(others) + [whole], after=[*far0, half1]
    )
    far0 = [swap(part, step) for step, part in zip(order, far0)] + [own]
    early = far1
    first = far_sum(far0, layout, 0, [*early])
    across = [lax.ppermute(first, "local", counterparts)]
    middle = [slow] + [fast] * (fast != slow)
    ends = [step for step in others if step not in middle]
    near = rotate(
        values,
        sign_rows,
        layout,
        False,
        middle + ends,
        [whole] * len(middle) + [(0,)] * len(ends),
        after=[first],
    )
    outs, near = near[len(middle) :], near[: len(middle)]
    far1 = [swap(part, step) for step, part in zip(others + [slow], far1 + [half1])] + [own]
    second = far_sum(far1, layout, 1, [*near])
    across.append(lax.ppermute(second, "local", counterparts))
    *half1, own, own_signs = rotate(
        values,
        sign_rows,
        layout,
        False,
        ends + [0],
        [(1,)] * len(ends) + [whole],
        signed_out=True,
        after=[first],
    )
    near = [swap(part, step) for step, part in zip(middle, near)] + [own]
    outs += hand_on(half1, across[0]) if ends else []
    outs = [swap(part, step) for step, part in zip(ends + ends, outs)]
    coded = []
    for part in range(HALVES):
        cut = outs[part * len(ends) : (part + 1) * len(ends)]
        coded += share(group_sum(near + cut + [across[part]], layout, part))
    reduced, rotated_max = finish(coded, own_signs)
    return (reduced.reshape(-1), rotated_max.reshape(-1))


def solution(mesh):
    in_specs = (P("node", "local", None), P())
    out_specs = (P(("node", "local")), P(("node", "local")))
    return jax.shard_map(shards, mesh=mesh, in_specs=in_specs, out_specs=out_specs, check_vma=False)
```
